32 devices in a mesh: rows: 8 (over y, x, core), feat: 4 (over z).
Axes of the slice: x: 2, y: 2, z: 4, core: 2. Of those that a mesh axis runs over, the one named last changes fastest.
Arguments:
- tokens: bfloat16 [8192, 1024], P(('rows', 'feat')), may hold values from -6 to 6
- cotangent: bfloat16 [8192, 1024], P(('rows', 'feat')), may hold values from -6 to 6
- image_length: int32 [32], replicated, may hold values from 0 to 7168, as said below
- image_start: int32 [32], replicated, may hold values from 0 to 8192, as said below
- norm_gain: float32 [2, 2, 1024], replicated, may hold values from 0.5 to 1.5
- norm_bias: float32 [2, 2, 1024], replicated, may hold values from -1 to 1
- weight_in: bfloat16 [2, 1024, 3, 1024], P(None, None, None, 'feat'), may hold values from -0.1875 to 0.1875
- weight_mix: bfloat16 [2, 1024, 1024], P(None, None, 'feat'), may hold values from -1.5 to 1.5
- weight_up: bfloat16 [2, 1024, 4096], P(None, None, 'feat'), may hold values from -0.1875 to 0.1875
- weight_down: bfloat16 [2, 1024, 4096], P(None, None, 'feat'), may hold values from -0.09375 to 0.09375
Outputs:
- output: bfloat16 [8192, 1024], P(('rows', 'feat'))
- grad_input: float32 [8192, 1024], P(('rows', 'feat'))
- grad_gain: float32 [2, 2, 1024], replicated
- grad_bias: float32 [2, 2, 1024], replicated
- grad_bias_top: float32 [1024], replicated
- grad_in: float32 [2, 1024, 3, 1024], P(None, 'rows', None, 'feat')
- grad_mix: float32 [2, 1024, 1024], P(None, 'rows', 'feat')
- grad_up: float32 [2, 1024, 4096], P(None, 'rows', 'feat')
- grad_down: float32 [2, 1024, 4096], P(None, 'rows', 'feat')
- log_max: float32 [], replicated
- log_mean: float32 [], replicated
The draws below stay inside these ranges and needn't reach their ends.
Inputs may be any that keep to these rules, and one draw needn't show every extreme that they name: `image_length`: images lie end to end from pixel 0 in order: each image_start is the previous start plus the previous length. One image has 7168 pixels; every other live image has 256 pixels, at least one before the long image and at least one after it. Entries after the last image have length 0. `image_start`: entries after the last image start at 8192.
All inputs are finite; a program needn't handle non-finite values.
Results may differ from the reference program's by a relative error of at most 0.017.
Values may be sent and summed in bfloat16 or wider, within the bound.
A program may use at most 192 MiB of HBM per device.

```python
import jax
import jax.numpy as jnp
from jax import lax

D = 1024
HEADS = 16
HD = 64
FF = 4096
LAYERS = 2
BLK = 512
IMG_SMALL = 256
TOK_DEV = 1024
TOKENS = 8192
NIMG = 32


def image_layout(key):
    units = TOK_DEV // IMG_SMALL
    before = jax.random.randint(jax.random.fold_in(key, 101), (), 1, units).astype(jnp.int32)
    after = (units - before).astype(jnp.int32)
    index = jnp.arange(NIMG, dtype=jnp.int32)
    tail_start = TOKENS - after * IMG_SMALL + (index - before - 1) * IMG_SMALL
    starts = jnp.where(index < before, index * IMG_SMALL, jnp.where(index == before, before * IMG_SMALL, jnp.where(index <= units, tail_start, TOKENS))).astype(jnp.int32)
    lengths = jnp.where(index == before, TOKENS - TOK_DEV, jnp.where(index <= units, IMG_SMALL, 0)).astype(jnp.int32)
    return (lengths, starts)


def draw_image_length(key, part):
    return image_layout(key)[0]


def draw_image_start(key, part):
    return image_layout(key)[1]


def levels(own_key, shape, shards, smallest, largest):
    level = 1.0
    for position, parts in shards:
        steps = jax.random.uniform(jax.random.fold_in(jax.random.fold_in(own_key, 6), position), (parts,), jnp.float32, smallest / len(shards), largest / len(shards))
        level = level * jnp.repeat(jnp.exp(steps), shape[position] // parts).reshape((-1,) + (1,) * (len(shape) - 1 - position))
    return level


def scatter_about(key, extent, scale, reach, cuts=(), held_as=jnp.bfloat16):
    loudness = levels(key, extent, cuts, -0.22, 0.18) if cuts else 1.0
    values = jax.random.normal(key, extent, jnp.float32) * scale * loudness
    return jnp.minimum(jnp.maximum(values, -reach), reach).astype(held_as)


def setup_inputs(seed: int = 0) -> dict:
    seeds = jax.random.split(jax.random.key(seed), 11)
    return {
        "tokens": scatter_about(seeds[0], (TOKENS, D), 1.0, 6.0, ((0, 32),)),
        "cotangent": scatter_about(seeds[1], (TOKENS, D), 1.0, 6.0, ((0, 32),)),
        "image_length": draw_image_length(jax.random.fold_in(seeds[10], 71), 0),
        "image_start": draw_image_start(jax.random.fold_in(seeds[10], 71), 0),
        "norm_gain": jnp.clip(1.0 + 0.1 * jax.random.normal(seeds[4], (LAYERS, 2, D), jnp.float32), 0.5, 1.5),
        "norm_bias": scatter_about(seeds[5], (LAYERS, 2, D), 0.2, 1.0, (), jnp.float32),
        "weight_in": scatter_about(seeds[6], (LAYERS, D, 3, D), D ** -0.5, 0.1875, ((3, 4),)),
        "weight_mix": scatter_about(seeds[7], (LAYERS, D, D), (max(D // 64, 1)) ** -0.5, 1.5, ((2, 4),)),
        "weight_up": scatter_about(seeds[8], (LAYERS, D, FF), D ** -0.5, 0.1875, ((2, 4),)),
        "weight_down": scatter_about(seeds[9], (LAYERS, D, FF), FF ** -0.5, 0.09375, ((2, 4),)),
    }


EPS_NORM = 1e-05
EPS_DEN = 1e-06
HIGHEST = lax.Precision.HIGHEST

@jax.custom_vjp
def low(v):
    return lax.optimization_barrier(v.astype(jnp.bfloat16)).astype(jnp.float32)

@jax.custom_vjp
def low_back(v):
    return v

def low_keep(v):
    return (low(v), None)

def low_pass(kept, grad):
    return (grad,)

def back_keep(v):
    return (v, None)

def back_low(kept, grad):
    return (low(grad),)
low.defvjp(low_keep, low_pass)
low_back.defvjp(back_keep, back_low)

def layer_norm(values, gain, bias):
    center = lax.optimization_barrier(jnp.mean(values, axis=-1, keepdims=True))
    shifted = values - center
    spread = lax.optimization_barrier(jnp.mean(shifted * shifted, axis=-1, keepdims=True))
    return shifted * lax.rsqrt(spread + EPS_NORM) * gain + bias

def feature(values):
    return jax.nn.elu(values) + 1.0

def image_table(image_length, image_start):
    live = (image_length > 0).astype(jnp.int32)
    marks = jnp.zeros((TOKENS + 1,), jnp.int32).at[image_start.astype(jnp.int32)].add(live)[:TOKENS]
    segment = (jnp.cumsum(marks) - 1).astype(jnp.int32)
    return (segment, marks > 0)

def attend_block(carry, block):
    state, total = carry
    query_block, key_block, value_block, segment, opening = block
    order = jnp.arange(BLK)
    same = ((segment[:, None] == segment[None, :]) & (order[None, :] <= order[:, None])).astype(jnp.float32)
    carried = ((segment == segment[0]) & jnp.logical_not(opening[0])).astype(jnp.float32)
    last = (segment == segment[BLK - 1]).astype(jnp.float32)
    scores = low_back(jnp.einsum('ihc,jhc->hij', query_block, key_block, precision=HIGHEST) * same[None])
    weights = low(scores)
    numerator = jnp.einsum('hij,jhe->ihe', weights, value_block, precision=HIGHEST)
    numerator = numerator + carried[:, None, None] * jnp.einsum('ihc,hce->ihe', query_block, state, precision=HIGHEST)
    numerator = low_back(numerator)
    denominator = lax.optimization_barrier(jnp.sum(scores, axis=2)).T + carried[:, None] * jnp.einsum('ihc,hc->ih', query_block, total, precision=HIGHEST) + EPS_DEN
    keep = carried[BLK - 1]
    masked = key_block * last[:, None, None]
    state_next = keep * state + jnp.einsum('jhc,jhe->hce', masked, value_block, precision=HIGHEST)
    total_next = keep * total + lax.optimization_barrier(jnp.sum(masked, axis=0))
    return ((state_next, total_next), (numerator / denominator[:, :, None], denominator))

def attend(query_feat, key_feat, values, segment, opening):
    count = TOKENS // BLK

    def split(array):
        return array.reshape((count, BLK) + array.shape[1:])
    begin = (jnp.zeros((HEADS, HD, HD), jnp.float32), jnp.zeros((HEADS, HD), jnp.float32))
    pieces = (split(query_feat), split(key_feat), split(values), split(segment), split(opening))
    _, (ratio, denominator) = lax.scan(jax.checkpoint(attend_block), begin, pieces)
    return (ratio.reshape(TOKENS, D), denominator.reshape(TOKENS, HEADS))

def layer(stream, gain, bias, weight_in, weight_mix, weight_up, weight_down, segment, opening):
    normed = low(layer_norm(stream, gain[0], bias[0]))
    projected = jnp.einsum('td,dke->tke', normed, weight_in, precision=HIGHEST)
    query_feat = low(feature(low_back(projected[:, 0]))).reshape(TOKENS, HEADS, HD)
    key_feat = low(feature(low_back(projected[:, 1]))).reshape(TOKENS, HEADS, HD)
    values = low(low_back(projected[:, 2])).reshape(TOKENS, HEADS, HD)
    ratio, denominator = attend(query_feat, key_feat, values, segment, opening)
    mixed = low(low_back(ratio))
    middle = stream + low_back(jnp.einsum('te,de->td', mixed, weight_mix, precision=HIGHEST))
    normed_mid = low(layer_norm(middle, gain[1], bias[1]))
    upward = low_back(jnp.dot(normed_mid, weight_up, precision=HIGHEST))
    active = low(jax.nn.gelu(upward, approximate=False))
    return (middle + low_back(jnp.einsum('tf,df->td', active, weight_down, precision=HIGHEST)), denominator)

def forward(stream, gain, bias, weight_in, weight_mix, weight_up, weight_down, segment, opening):
    denominators = []
    for level in range(LAYERS):
        stream, denominator = layer(stream, gain[level], bias[level], weight_in[level], weight_mix[level], weight_up[level], weight_down[level], segment, opening)
        denominators.append(denominator)
    return (stream, jnp.stack(denominators))

def reference(tokens, cotangent, image_length, image_start, norm_gain, norm_bias, weight_in, weight_mix, weight_up, weight_down):
    segment, opening = image_table(image_length, image_start)

    def run(stream, gain, bias, first, second, third, fourth):
        return forward(stream, gain, bias, first, second, third, fourth, segment, opening)
    floats = [array.astype(jnp.float32) for array in (tokens, norm_gain, norm_bias, weight_in, weight_mix, weight_up, weight_down)]
    result, pullback, denominators = jax.vjp(run, *floats, has_aux=True)
    gradients = pullback(cotangent.astype(jnp.float32))
    logs = jnp.log(denominators)
    return (result.astype(jnp.bfloat16), gradients[0], gradients[1], gradients[2], gradients[2][LAYERS - 1, 1], gradients[3], gradients[4], gradients[5], gradients[6], jnp.max(logs), jnp.mean(logs))
```

```python
import functools
import types

import jax
import jax.numpy as jnp
from jax import lax
from jax.experimental import pallas as pl
from jax.experimental.pallas import tpu as pltpu
from jax.sharding import PartitionSpec as P

HD = 64
EPS_NORM = 1e-05
EPS_DEN = 1e-06
MESH = pl.DeviceIdType.MESH
BF = jnp.bfloat16
F32 = jnp.float32
LAG_FIRST, LAG_SECOND, LAG_CORE, LAG_READY = 2, 4, 6, 7
RING = 4
ROOT_HALF = 0.7071067811865476
ROOT_TAU = 0.3989422804014327


def sizes_of(mesh, tokens, weight_in, weight_up):
    s = types.SimpleNamespace()
    s.R, s.Z = mesh.shape["rows"], mesh.shape["feat"]
    chips = s.R // 2
    s.NX = 1
    while s.NX * s.NX < chips:
        s.NX *= 2
    s.NY = chips // s.NX
    s.T, s.D = tokens.shape
    s.L = weight_in.shape[0]
    s.PC = weight_in.shape[3]
    s.PR = s.D // s.R
    s.NJ = weight_up.shape[2] // s.PC
    s.NU = 4 + 2 * s.NJ
    s.U = s.L * s.NU
    s.NP = s.PC // 128
    s.MR = s.NP * HD + 16
    s.NQ = s.NY * s.NX
    return s


def place(s):
    r, z = lax.axis_index("rows"), lax.axis_index("feat")
    return r, z, r // (2 * s.NX), (r // 2) % s.NX, r % 2


def row_at(s, y, x, c):
    return (y * s.NX + x) * 2 + c


def greet(s, r, z):
    barrier = pltpu.get_barrier_semaphore()
    peers = [((r + d) % s.R, z) for d in range(1, s.R)] + [(r, (z + d) % s.Z) for d in range(1, s.Z)]
    for peer in peers:
        pl.semaphore_signal(barrier, inc=1, device_id=peer, device_id_type=MESH)
    pl.semaphore_wait(barrier, len(peers))


def remote(src, dst, send, recv, device):
    return pltpu.make_async_remote_copy(
        src_ref=src, dst_ref=dst, send_sem=send, recv_sem=recv, device_id=device, device_id_type=MESH
    )


def dot(a, b, dims=((1,), (0,))):
    return lax.dot_general(a, b, (dims, ((), ())), preferred_element_type=F32)


NT = ((1,), (1,))
TN = ((0,), (0,))


def norm_parts(v):
    center = jnp.mean(v, axis=-1, keepdims=True)
    shifted = v - center
    spread = jnp.mean(shifted * shifted, axis=-1, keepdims=True)
    inv = lax.rsqrt(spread + EPS_NORM)
    return shifted * inv, inv


def weight_gather(s, h, r, z, y, x, c):
    half = s.PR // 2
    F, piece = h["whole"], h["piece"]
    rows = (pl.ds(0, half), pl.ds(half, half))

    def z_copies(u):
        return [
            remote(
                piece.at[u // s.NU, u % s.NU],
                F.at[u, s.Z - d - 1, y, x, c],
                h["z_send"].at[u % RING, d - 1],
                h["z_recv"].at[u, s.Z - d - 1],
                (r, (z + d) % s.Z),
            )
            for d in range(1, s.Z)
        ]

    def first(u):
        out = []
        for d in range(1, s.NX):
            at = F.at[u, :, y, x, c, rows[0]]
            out.append(remote(at, at, h["x_send"].at[u % RING, 0, d - 1], h["x_recv"].at[u, 0, s.NX - d - 1],
                              (row_at(s, y, (x + d) % s.NX, c), z)))
        for d in range(1, s.NY):
            at = F.at[u, :, y, x, c, rows[1]]
            out.append(remote(at, at, h["y_send"].at[u % RING, 0, d - 1], h["y_recv"].at[u, 0, s.NY - d - 1],
                              (row_at(s, (y + d) % s.NY, x, c), z)))
        return out

    def first_landing(u):
        out = []
        for d in range(1, s.NX):
            at = F.at[u, :, y, (x + d) % s.NX, c, rows[0]]
            out.append(remote(at, at, h["x_send"].at[u % RING, 0, d - 1], h["x_recv"].at[u, 0, d - 1], (r, z)))
        for d in range(1, s.NY):
            at = F.at[u, :, (y + d) % s.NY, x, c, rows[1]]
            out.append(remote(at, at, h["y_send"].at[u % RING, 0, d - 1], h["y_recv"].at[u, 0, d - 1], (r, z)))
        return out

    def second(u):
        out = []
        for d in range(1, s.NY):
            at = F.at[u, :, y, :, c, rows[0]]
            out.append(remote(at, at, h["y_send"].at[u % RING, 1, d - 1], h["y_recv"].at[u, 1, s.NY - d - 1],
                              (row_at(s, (y + d) % s.NY, x, c), z)))
        for d in range(1, s.NX):
            at = F.at[u, :, :, x, c, rows[1]]
            out.append(remote(at, at, h["x_send"].at[u % RING, 1, d - 1], h["x_recv"].at[u, 1, s.NX - d - 1],
                              (row_at(s, y, (x + d) % s.NX, c), z)))
        return out

    def second_landing(u):
        out = []
        for d in range(1, s.NY):
            at = F.at[u, :, (y + d) % s.NY, :, c, rows[0]]
            out.append(remote(at, at, h["y_send"].at[u % RING, 1, d - 1], h["y_recv"].at[u, 1, d - 1], (r, z)))
        for d in range(1, s.NX):
            at = F.at[u, :, :, (x + d) % s.NX, c, rows[1]]
            out.append(remote(at, at, h["x_send"].at[u % RING, 1, d - 1], h["x_recv"].at[u, 1, d - 1], (r, z)))
        return out

    def share(u):
        at = F.at[u, :, :, :, c]
        return remote(at, at, h["c_send"].at[u % RING], h["c_recv"].at[u], (row_at(s, y, x, 1 - c), z))

    def share_landing(u):
        at = F.at[u, :, :, :, 1 - c]
        return remote(at, at, h["c_send"].at[u % RING], h["c_recv"].at[u], (r, z))

    def z_landing(u):
        return [
            remote(piece.at[0, 0], F.at[u, k, y, x, c], h["z_send"].at[u % RING, 0], h["z_recv"].at[u, k], (r, z))
            for k in range(s.Z - 1)
        ]

    def inside(u, what):
        pl.when((u >= 0) & (u < s.U))(functools.partial(what, u))

    def stage_z(u):
        for cp in z_copies(u):
            cp.start()

    def stage_first(u):
        for cp in z_landing(u):
            cp.wait_recv()
        for cp in first(u):
            cp.start()

    def stage_second(u):
        for cp in first_landing(u):
            cp.wait_recv()
        for cp in second(u):
            cp.start()

    def stage_core(u):
        for cp in second_landing(u):
            cp.wait_recv()
        share(u).start()

    def stage_ready(u):
        share_landing(u).wait_recv()

    def tick(t):
        inside(t - RING, lambda u: [cp.wait_send() for cp in z_copies(u)] and None)
        inside(t, stage_z)
        inside(t - LAG_FIRST - RING, lambda u: [cp.wait_send() for cp in first(u)] and None)
        inside(t - LAG_FIRST, stage_first)
        inside(t - LAG_SECOND - RING, lambda u: [cp.wait_send() for cp in second(u)] and None)
        inside(t - LAG_SECOND, stage_second)
        inside(t - LAG_CORE - RING, lambda u: share(u).wait_send())
        inside(t - LAG_CORE, stage_core)
        inside(t - LAG_READY, stage_ready)

    def drain_all():
        @pl.loop(s.U + LAG_READY, s.U + LAG_CORE + RING)
        def _(t):
            tick(t)

    return tick, drain_all


def head_masks(s):
    lane = lax.broadcasted_iota(jnp.int32, (1, 128), 1)
    first = lane < HD
    return first, jnp.where(first, 1.0, 0.0), jnp.where(first, 0.0, 1.0)


def pair_ones():
    row = lax.broadcasted_iota(jnp.int32, (128, 128), 0) // HD
    col = lax.broadcasted_iota(jnp.int32, (128, 128), 1) // HD
    return jnp.where(row == col, 1.0, 0.0).astype(BF)


def lanes(at, width):
    return pl.ds(pl.multiple_of(at * width, width), width)


def prefix_rounds(s, h, l, r, z):
    msg, got, rows_got, back, out = h["msg"], h["r1"], h["r2"], h["pre"], h["r3"]

    def one(k):
        return remote(msg.at[k], got.at[s.Z - k], h["r1_send"].at[l, k], h["r1_recv"].at[l, s.Z - k], (r, (z + k) % s.Z))

    def two(d):
        return remote(rows_got.at[r], rows_got.at[r], h["r2_send"].at[l, d], h["r2_recv"].at[l, s.R - d],
                      ((r + d) % s.R, z))

    def two_landing(d):
        at = rows_got.at[(r + d) % s.R]
        return remote(at, at, h["r2_send"].at[l, d], h["r2_recv"].at[l, d], (r, z))

    def three(k):
        return remote(back.at[k], out.at[s.Z - k], h["r3_send"].at[l, k], h["r3_recv"].at[l, s.Z - k], (r, (z + k) % s.Z))

    def round_one():
        for k in range(1, s.Z):
            one(k).start()

    def round_two():
        for k in range(1, s.Z):
            remote(msg.at[k], got.at[k], h["r1_send"].at[l, k], h["r1_recv"].at[l, k], (r, z)).wait_recv()
        total = h["coef_a"][0] * msg[0].astype(F32)
        for k in range(1, s.Z):
            total = total + h["coef_a"][k] * got[k].astype(F32)
        rows_got[r] = total.astype(BF)
        for d in range(1, s.R):
            two(d).start()

    def round_three():
        for d in range(1, s.R):
            two_landing(d).wait_recv()
        for k in range(s.Z):
            total = h["coef_b"][k * s.Z] * msg[0].astype(F32)
            for j in range(1, s.Z):
                total = total + h["coef_b"][k * s.Z + j] * got[j].astype(F32)
            for q in range(s.R):
                total = total + h["coef_c"][k * s.R + q] * rows_got[q].astype(F32)
            if k == 0:
                out[0] = total.astype(BF)
            else:
                back[k] = total.astype(BF)
                three(k).start()

    def arrive():
        for k in range(1, s.Z):
            remote(back.at[k], out.at[k], h["r3_send"].at[l, k], h["r3_recv"].at[l, k], (r, z)).wait_recv()

    def settle():
        for k in range(1, s.Z):
            one(k).wait_send()
            three(k).wait_send()
        for d in range(1, s.R):
            two(d).wait_send()

    return round_one, round_two, round_three, arrive, settle


def pack_state(full, first):
    return jnp.where(first, full[:HD], full[HD:])


def unpack_state(packed, first):
    zero = jnp.zeros_like(packed)
    return jnp.concatenate([jnp.where(first, packed, zero), jnp.where(first, zero, packed)], axis=0)


def spread_rows(s, rows_list):
    at = lax.broadcasted_iota(jnp.int32, (16, 128), 0)
    block = jnp.zeros((16, 128), F32)
    for i, row in enumerate(rows_list):
        block = block + jnp.where(at == i, row, 0.0)
    return block


def pick_row(block, i):
    at = lax.broadcasted_iota(jnp.int32, (16, 128), 0)
    return jnp.sum(jnp.where(at == i, block.astype(F32), 0.0), axis=0, keepdims=True)


FWD_IN = ("tokens", "gain", "bias", "coef_a", "coef_b", "coef_c", "w_in", "w_mix", "w_up", "w_down")
FWD_OUT = ("output", "logs", "whole", "k_stream", "k_middle", "k_qkv", "k_mixed", "k_den", "k_state", "k_act", "k_slope",
           "k_normt", "s_mixed", "s_act")


def fwd_scratch(s):
    dma = pltpu.SemaphoreType.DMA
    return {
        "piece": pltpu.VMEM((s.L, s.NU, s.PR, s.PC), BF),
        "w": pltpu.VMEM((s.Z, s.NY, s.NX, 2, s.PR, s.PC), BF),
        "stream": pltpu.VMEM((s.T, s.D), F32),
        "acc": pltpu.VMEM((s.T, s.D), F32),
        "middle": pltpu.VMEM((s.T, s.D), F32),
        "den": pltpu.VMEM((s.T, s.D), F32),
        "nrm": pltpu.VMEM((s.T, s.D), BF),
        "nrmt": pltpu.VMEM((2, s.NY, s.NX, 2, s.PR, s.T), BF),
        "qkv": pltpu.VMEM((3, s.T, s.D), BF),
        "mixed": pltpu.VMEM((s.T, s.D), BF),
        "act": pltpu.VMEM((s.NJ, s.T, s.D), BF),
        "slope": pltpu.VMEM((s.NJ, s.T, s.D), BF),
        "msg": pltpu.VMEM((s.Z, s.MR, 128), BF),
        "r1": pltpu.VMEM((s.Z, s.MR, 128), BF),
        "r2": pltpu.VMEM((s.R, s.MR, 128), BF),
        "pre": pltpu.VMEM((s.Z, s.MR, 128), BF),
        "r3": pltpu.VMEM((s.Z, s.MR, 128), BF),
        "piece_sem": dma((2 + 2 * s.NJ,)),
        "w_sem": dma((s.Z,)),
        "z_send": dma((RING, s.Z - 1)),
        "z_recv": dma((s.U, s.Z - 1)),
        "x_send": dma((RING, 2, s.NX - 1)),
        "x_recv": dma((s.U, 2, s.NX - 1)),
        "y_send": dma((RING, 2, s.NY - 1)),
        "y_recv": dma((s.U, 2, s.NY - 1)),
        "c_send": dma((RING,)),
        "c_recv": dma((s.U,)),
        "r1_send": dma((s.L, s.Z)),
        "r1_recv": dma((s.L, s.Z)),
        "r2_send": dma((s.L, s.R)),
        "r2_recv": dma((s.L, s.R)),
        "r3_send": dma((s.L, s.Z)),
        "r3_recv": dma((s.L, s.Z)),
        "keep": dma((8,)),
        "keep_j": dma((2, s.NJ)),
        "sib_send": dma((3 + s.NJ,)),
        "sib_recv": dma((s.L, 3 + s.NJ)),
    }


def fwd_kernel(s, *refs):
    names = FWD_IN + FWD_OUT + tuple(fwd_scratch(s))
    h = dict(zip(names, refs, strict=True))
    r, z, y, x, c = place(s)
    sibling = (row_at(s, y, x, 1 - c), z)
    greet(s, r, z)
    tick, drain_all = weight_gather(s, h, r, z, y, x, c)
    first, _, _ = head_masks(s)

    pieces = [
        pltpu.make_async_copy(h["w_in"].at[:, :, y, x, c], h["piece"].at[:, 0:3], h["piece_sem"].at[0]),
        pltpu.make_async_copy(h["w_mix"].at[:, y, x, c], h["piece"].at[:, 3], h["piece_sem"].at[1]),
    ]
    for j in range(s.NJ):
        cols = pl.ds(j * s.PC, s.PC)
        pieces.append(pltpu.make_async_copy(h["w_up"].at[:, y, x, c, :, cols], h["piece"].at[:, 4 + j], h["piece_sem"].at[2 + j]))
        pieces.append(pltpu.make_async_copy(h["w_down"].at[:, y, x, c, :, cols], h["piece"].at[:, 4 + s.NJ + j],
                                            h["piece_sem"].at[2 + s.NJ + j]))
    for cp in pieces:
        cp.start()
    for cp in pieces:
        cp.wait()

    def own(kind, l, j):
        if kind == "in":
            src = h["w_in"].at[l, j]
        elif kind == "mix":
            src = h["w_mix"].at[l]
        else:
            src = h["w_" + kind].at[l, :, :, :, :, lanes(j, s.PC)]
        return pltpu.make_async_copy(src, h["w"].at[0], h["w_sem"].at[0])

    def load(u, k):
        return pltpu.make_async_copy(h["whole"].at[u, k - 1], h["w"].at[k], h["w_sem"].at[k])

    def with_unit(kind, l, j, u, advance, body):
        own(kind, l, j).start()
        advance()
        for k in range(1, s.Z):
            load(u, k).start()
        own(kind, l, j).wait()
        body(0, h["w"][0].reshape(s.D, s.PC))

        @pl.loop(1, s.Z)
        def _(k):
            load(u, k).wait()
            body(k, h["w"][k].reshape(s.D, s.PC))

    def normalize(l, n, source):
        xhat, _ = norm_parts(source)
        v = xhat * h["gain"][pl.ds(l * 2 + n, 1), :] + h["bias"][pl.ds(l * 2 + n, 1), :]
        h["nrm"][...] = v.astype(BF)
        h["nrmt"][n] = v.T.astype(BF).reshape(s.NY, s.NX, 2, s.PR, s.T)
        keep_norm(l, n).start()
        send_norm(l, n).start()

    def keep_norm(l, n):
        return pltpu.make_async_copy(h["nrmt"].at[n, :, :, c], h["k_normt"].at[l, n, 0], h["keep"].at[n])

    def send_norm(l, n):
        return remote(h["nrmt"].at[n, :, :, 1 - c], h["k_normt"].at[l, n, 1], h["sib_send"].at[n], h["sib_recv"].at[l, n],
                      sibling)

    def keep_one(l, name, index):
        return pltpu.make_async_copy(h[name], h["k_" + name].at[l], h["keep"].at[index])

    def send_mixed(l):
        return remote(h["mixed"], h["s_mixed"].at[l], h["sib_send"].at[2], h["sib_recv"].at[l, 2], sibling)

    def keep_act(l, j):
        return pltpu.make_async_copy(h["act"].at[j], h["k_act"].at[l, j], h["keep_j"].at[0, j])

    def keep_slope(l, j):
        return pltpu.make_async_copy(h["slope"].at[j], h["k_slope"].at[l, j], h["keep_j"].at[1, j])

    def send_act(l, j):
        return remote(h["act"].at[j], h["s_act"].at[l, j], h["sib_send"].at[3 + j], h["sib_recv"].at[l, 3 + j], sibling)

    h["stream"][...] = h["tokens"][...].astype(F32)
    h["logs"][...] = jnp.where(lax.broadcasted_iota(jnp.int32, (8, 128), 0) == 1, -jnp.inf, 0.0)
    ones = pair_ones()
    tall = jnp.ones((s.T, 128), BF)

    @pl.loop(0, LAG_READY)
    def _(t):
        tick(t)

    def one_layer(l, carry):
        base = l * s.NU
        keep_one(l, "stream", 2).start()
        normalize(l, 0, h["stream"][...])

        def project(kind, carry):
            u = base + kind

            def body(k, weight):
                v = dot(h["nrm"][...], weight)
                phi = jnp.where(v > 0, v + 1.0, jnp.exp(jnp.minimum(v, 0.0)))
                h["qkv"][kind, :, lanes(k, s.PC)] = jnp.where(kind < 2, phi, v).astype(BF)

            with_unit("in", l, kind, u, lambda: tick(u + LAG_READY), body)
            return carry

        lax.fori_loop(0, 3, project, 0)
        keep_one(l, "qkv", 3).start()
        round_one, round_two, round_three, arrive, settle = prefix_rounds(s, h, l, r, z)

        def local_state(k, carry):
            totals = []
            for i in range(s.NP):
                at = lanes(k * s.NP + i, 128)
                keys, vals = h["qkv"][1, :, at], h["qkv"][2, :, at]
                h["msg"][k, i * HD:(i + 1) * HD] = pack_state(dot(keys, vals, TN), first).astype(BF)
                totals.append(jnp.sum(keys.astype(F32), axis=0, keepdims=True))
            h["msg"][k, s.NP * HD:] = spread_rows(s, totals).astype(BF)
            return carry

        lax.fori_loop(0, s.Z, local_state, 0)
        round_one()
        tick(base + 3 + LAG_READY)
        round_two()
        tick(base + 4 + LAG_READY)
        round_three()
        tick(base + 5 + LAG_READY)
        arrive()
        keep_one(l, "r3", 7) if False else pltpu.make_async_copy(h["r3"], h["k_state"].at[l], h["keep"].at[7]).start()
        causal = (lax.broadcasted_iota(jnp.int32, (s.T, s.T), 1) <= lax.broadcasted_iota(jnp.int32, (s.T, s.T), 0))

        def attend(p, carry):
            k, i = p // s.NP, p % s.NP
            at = lanes(p, 128)
            query, key, value = h["qkv"][0, :, at], h["qkv"][1, :, at], h["qkv"][2, :, at]
            wide = query.astype(F32)
            value_ones = jnp.concatenate([value, tall], axis=1)
            zero = jnp.zeros_like(query)
            results = []
            for head in range(2):
                mine = first if head == 0 else jnp.logical_not(first)
                scores = dot(jnp.where(mine, query, zero), key, NT)
                weights = jnp.where(causal, scores, 0.0).astype(BF)
                results.append(dot(weights, value_ones))
            state = unpack_state(h["r3"][k, pl.ds(pl.multiple_of(i * HD, HD), HD), :], first)
            total = pick_row(h["r3"][k, s.NP * HD:, :], i)
            square = jnp.zeros((128, 128), BF)
            right = jnp.concatenate(
                [jnp.concatenate([state, square], axis=1), jnp.concatenate([square, ones], axis=1)], axis=0)
            left = jnp.concatenate([query, (wide * total).astype(BF)], axis=1)
            earlier = dot(left, right)
            num = jnp.where(first, results[0][:, :128], results[1][:, :128]) + earlier[:, :128]
            den = jnp.where(first, results[0][:, 128:], results[1][:, 128:]) + earlier[:, 128:] + EPS_DEN
            h["mixed"][:, at] = (num / den).astype(BF)
            h["den"][:, at] = den
            logs = jnp.log(den)
            h["logs"][0:1] += jnp.sum(logs, axis=0, keepdims=True)
            h["logs"][1:2] = jnp.maximum(h["logs"][1:2], jnp.max(logs, axis=0, keepdims=True))
            return carry

        half = s.Z * s.NP // 2
        lax.fori_loop(0, half, attend, 0)
        tick(base + 6 + LAG_READY)
        lax.fori_loop(half, s.Z * s.NP, attend, 0)
        settle()
        keep_one(l, "mixed", 4).start()
        send_mixed(l).start()
        keep_one(l, "den", 5).start()

        h["acc"][...] = jnp.zeros_like(h["acc"])

        def mix(k, weight):
            h["acc"][...] += dot(h["mixed"][:, lanes(k, s.PC)], weight, NT)

        with_unit("mix", l, 0, base + 3, lambda: None, mix)
        h["middle"][...] = h["stream"][...] + h["acc"][...]
        keep_one(l, "middle", 6).start()
        normalize(l, 1, h["middle"][...])

        def up(j, carry):
            u = base + 4 + j

            def body(k, weight):
                v = dot(h["nrm"][...], weight)
                cdf = 0.5 * (1.0 + lax.erf(v * ROOT_HALF))
                h["act"][j, :, lanes(k, s.PC)] = (v * cdf).astype(BF)
                h["slope"][j, :, lanes(k, s.PC)] = (cdf + v * (ROOT_TAU * jnp.exp(-0.5 * v * v))).astype(BF)

            with_unit("up", l, j, u, lambda: pl.when(j >= 3)(lambda: tick(u + LAG_READY)), body)
            keep_act(l, j).start()
            keep_slope(l, j).start()
            send_act(l, j).start()
            return carry

        lax.fori_loop(0, s.NJ, up, 0)
        h["acc"][...] = jnp.zeros_like(h["acc"])

        def down(j, carry):
            u = base + 4 + s.NJ + j

            def body(k, weight):
                h["acc"][...] += dot(h["act"][j, :, lanes(k, s.PC)], weight, NT)

            with_unit("down", l, j, u, lambda: tick(u + LAG_READY), body)
            return carry

        lax.fori_loop(0, s.NJ, down, 0)
        keep_one(l, "stream", 2).wait()
        h["stream"][...] = h["middle"][...] + h["acc"][...]
        for n in range(2):
            keep_norm(l, n).wait()
            send_norm(l, n).wait_send()
            send_norm(l, n).wait_recv()
        for name, index in (("qkv", 3), ("mixed", 4), ("den", 5), ("middle", 6)):
            keep_one(l, name, index).wait()
        pltpu.make_async_copy(h["r3"], h["k_state"].at[l], h["keep"].at[7]).wait()
        send_mixed(l).wait()

        def finish(j, carry):
            keep_act(l, j).wait()
            keep_slope(l, j).wait()
            send_act(l, j).wait()
            return carry

        lax.fori_loop(0, s.NJ, finish, 0)
        return carry

    lax.fori_loop(0, s.L, one_layer, 0)
    h["output"][...] = h["stream"][...].astype(BF)
    drain_all()


def split_rows(s, weight_in, *rest):
    cut = (s.NY, s.NX, 2, s.PR)
    turned = jnp.transpose(weight_in, (0, 2, 1, 3)).reshape((s.L, 3) + cut + (s.PC,))
    return (turned,) + tuple(w.reshape((s.L,) + cut + w.shape[2:]) for w in rest)


def forward_call(s, tokens, gain, bias, coefs, weights):
    vmem = pl.BlockSpec(memory_space=pltpu.VMEM)
    smem = pl.BlockSpec(memory_space=pltpu.SMEM)
    hbm = pl.BlockSpec(memory_space=pl.ANY)
    shape = jax.ShapeDtypeStruct
    outs = {
        "output": shape((s.T, s.D), BF),
        "logs": shape((8, 128), F32),
        "whole": shape((s.U, s.Z - 1, s.NY, s.NX, 2, s.PR, s.PC), BF),
        "k_stream": shape((s.L, s.T, s.D), F32),
        "k_middle": shape((s.L, s.T, s.D), F32),
        "k_qkv": shape((s.L, 3, s.T, s.D), BF),
        "k_mixed": shape((s.L, s.T, s.D), BF),
        "k_den": shape((s.L, s.T, s.D), F32),
        "k_state": shape((s.L, s.Z, s.MR, 128), BF),
        "k_act": shape((s.L, s.NJ, s.T, s.D), BF),
        "k_slope": shape((s.L, s.NJ, s.T, s.D), BF),
        "k_normt": shape((s.L, 2, 2, s.NY, s.NX, s.PR, s.T), BF),
        "s_mixed": shape((s.L, s.T, s.D), BF),
        "s_act": shape((s.L, s.NJ, s.T, s.D), BF),
    }
    out = pl.pallas_call(
        functools.partial(fwd_kernel, s),
        out_shape=[outs[name] for name in FWD_OUT],
        in_specs=[vmem] * 3 + [smem] * 3 + [hbm] * 4,
        out_specs=[vmem] * 2 + [hbm] * (len(FWD_OUT) - 2),
        scratch_shapes=list(fwd_scratch(s).values()),
        compiler_params=pltpu.CompilerParams(
            collective_id=0, has_side_effects=True, vmem_limit_bytes=56 * 1024 * 1024),
        name="forward",
    )(tokens, gain, bias, *coefs, *weights)
    return dict(zip(FWD_OUT, out, strict=True))


def segments_of_units(s, image_length, image_start):
    first = jnp.arange(s.R * s.Z, dtype=jnp.int32) * s.T
    live = (image_length > 0)[None, :]
    return (jnp.sum(((image_start[None, :] <= first[:, None]) & live).astype(jnp.int32), axis=1) - 1).reshape(s.R, s.Z)


def coefficients(s, image_length, image_start):
    seg = segments_of_units(s, image_length, image_start)
    r, z = lax.axis_index("rows"), lax.axis_index("feat")
    turn = (z + jnp.arange(s.Z)) % s.Z
    row = seg[r][turn]
    order = jnp.arange(s.R)
    f = lambda v: v.astype(F32).reshape(-1)
    same = row[:, None] == row[None, :]
    forward = (
        f(row == seg[r, s.Z - 1]),
        f(same & (turn[None, :] < turn[:, None])),
        f((seg[None, :, s.Z - 1] == row[:, None]) & (order[None, :] < r)),
    )
    backward = (
        f(row == seg[r, 0]),
        f(same & (turn[None, :] > turn[:, None])),
        f((seg[None, :, 0] == row[:, None]) & (order[None, :] > r)),
    )
    return forward, backward


HEADS = 16
HD = 64
LAYERS = 2
BLK = 512


EPS_NORM = 1e-05
EPS_DEN = 1e-06
HIGHEST = lax.Precision.HIGHEST


def carried_in(array, axis, join, neutral):
    place = lax.axis_index(axis)
    gathered = jax.tree.map(
        lambda a, kind: lax.all_gather(a.astype(kind), axis),
        array,
        (jnp.bfloat16, jnp.bfloat16, jnp.bfloat16),
    )
    state = jax.tree.map(lambda a, e: jnp.zeros_like(a) + jnp.asarray(e, a.dtype), array, neutral)

    def one(step, state):
        return join(
            state,
            jax.tree.map(
                lambda a, own: lax.dynamic_index_in_dim(a, step, 0, False).astype(own.dtype),
                gathered,
                array,
            ),
        )

    return lax.fori_loop(0, place, one, state)


def entering(array, axis, combine, identity):
    peers, mine = (lax.axis_size(axis), lax.axis_index(axis))
    everything = jax.tree.map(
        lambda part, kind: lax.all_gather(part.astype(kind), axis),
        array,
        jax.tree.map(lambda a: jnp.bfloat16 if a.dtype == jnp.float32 else a.dtype, array),
    )
    start = jax.tree.map(
        lambda part, zero: jnp.broadcast_to(jnp.asarray(zero, part.dtype), part.shape),
        array,
        identity,
    )

    def step(k, before):
        at = peers - 1 - k
        reached = at > mine
        new = combine(
            before, jax.tree.map(lambda part, own: part[at].astype(own.dtype), everything, array)
        )
        return jax.tree.map(lambda a, b: jnp.where(reached, a, b), new, before)

    return lax.fori_loop(0, peers, step, start)


def layer_norm(values, gain, bias):
    center = jnp.mean(values, axis=-1, keepdims=True)
    shifted = values - center
    spread = jnp.mean(shifted * shifted, axis=-1, keepdims=True)
    return shifted * lax.rsqrt(spread + EPS_NORM) * gain + bias


def feature(values):
    return jax.nn.elu(values) + 1.0


def image_rows(image_length, image_start, first, count):
    positions = first + jnp.arange(count, dtype=jnp.int32)
    live = (image_length > 0)[None, :]
    begun = (image_start[None, :] <= positions[:, None]) & live
    segment = jnp.sum(begun.astype(jnp.int32), axis=1) - 1
    opening = jnp.any((image_start[None, :] == positions[:, None]) & live, axis=1)
    return (segment, opening)


def block_masks(segment, opening):
    order = jnp.arange(segment.shape[0])
    same = ((segment[:, None] == segment[None, :]) & (order[None, :] <= order[:, None])).astype(
        jnp.float32
    )
    carried = ((segment == segment[0]) & jnp.logical_not(opening[0])).astype(jnp.float32)
    last = (segment == segment[-1]).astype(jnp.float32)
    return (same, carried, last)


def in_blocks(array, blocks):
    return array.reshape((blocks, array.shape[0] // blocks) + array.shape[1:])


def block_forward(carry, block):
    state, total = carry
    query_block, key_block, value_block, segment, opening = block
    same, carried, last = block_masks(segment, opening)
    scores = (
        jnp.einsum("ihc,jhc->hij", query_block, key_block, preferred_element_type=jnp.float32)
        * same[None]
    )
    weights = scores.astype(jnp.bfloat16)
    query_wide = query_block.astype(jnp.float32)
    numerator = jnp.einsum("hij,jhe->ihe", weights, value_block, preferred_element_type=jnp.float32)
    numerator = numerator + carried[:, None, None] * jnp.einsum(
        "ihc,hce->ihe", query_wide, state, precision=HIGHEST
    )
    denominator = (
        jnp.sum(scores, axis=2).T
        + carried[:, None] * jnp.einsum("ihc,hc->ih", query_wide, total, precision=HIGHEST)
        + EPS_DEN
    )
    keep = carried[-1]
    masked = key_block * last[:, None, None].astype(jnp.bfloat16)
    state_next = keep * state + jnp.einsum(
        "jhc,jhe->hce", masked, value_block, preferred_element_type=jnp.float32
    )
    total_next = keep * total + jnp.sum(masked.astype(jnp.float32), axis=0)
    return (
        (state_next, total_next),
        (numerator / denominator[:, :, None], denominator, state, total),
    )


def block_backward(carry, block):
    state_grad, total_grad = carry
    (
        query_block,
        key_block,
        value_block,
        segment,
        opening,
        state,
        total,
        numerator_grad,
        denominator_grad,
    ) = block
    same, carried, last = block_masks(segment, opening)
    query_wide = query_block.astype(jnp.float32)
    key_wide = key_block.astype(jnp.float32)
    value_wide = value_block.astype(jnp.float32)
    numerator_wide = numerator_grad.astype(jnp.float32)
    scores = (
        jnp.einsum("ihc,jhc->hij", query_block, key_block, preferred_element_type=jnp.float32)
        * same[None]
    )
    weights = scores.astype(jnp.bfloat16)
    weight_grad = jnp.einsum(
        "ihe,jhe->hij", numerator_grad, value_block, preferred_element_type=jnp.float32
    )
    score_grad = ((weight_grad + denominator_grad.T[:, :, None]) * same[None]).astype(jnp.bfloat16)
    value_grad = jnp.einsum(
        "hij,ihe->jhe", weights, numerator_grad, preferred_element_type=jnp.float32
    )
    query_grad = jnp.einsum(
        "hij,jhc->ihc", score_grad, key_block, preferred_element_type=jnp.float32
    )
    query_grad = query_grad + carried[:, None, None] * (
        jnp.einsum("ihe,hce->ihc", numerator_wide, state, precision=HIGHEST)
        + denominator_grad[:, :, None] * total[None]
    )
    key_grad = jnp.einsum(
        "hij,ihc->jhc", score_grad, query_block, preferred_element_type=jnp.float32
    )
    last_wide = last[:, None, None]
    key_grad = key_grad + last_wide * (
        jnp.einsum("hce,jhe->jhc", state_grad, value_wide, precision=HIGHEST) + total_grad[None]
    )
    value_grad = value_grad + last_wide * jnp.einsum(
        "jhc,hce->jhe", key_wide, state_grad, precision=HIGHEST
    )
    keep = carried[-1]
    state_prior = keep * state_grad + jnp.einsum(
        "ihc,ihe->hce", query_wide * carried[:, None, None], numerator_wide, precision=HIGHEST
    )
    total_prior = keep * total_grad + jnp.einsum(
        "ih,ihc->hc", denominator_grad * carried[:, None], query_wide, precision=HIGHEST
    )
    return ((state_prior, total_prior), (query_grad, key_grad, value_grad))


def rows_times(left, weight):
    return jnp.einsum("te,de->td", left, weight, preferred_element_type=jnp.float32)


def gather_rows(normed):
    return lax.all_gather(normed, "feat", axis=0, tiled=True)


def sum_branch(left, weight):
    return lax.psum_scatter(
        rows_times(left, weight).astype(jnp.bfloat16), "feat", scatter_dimension=0, tiled=True
    ).astype(jnp.float32)


def gather_grads(gradient):
    return lax.all_gather(gradient, "feat", axis=0, tiled=True)


def sum_inputs(left, weight):
    return lax.psum_scatter(
        rows_times(left, weight).astype(jnp.bfloat16), "feat", scatter_dimension=0, tiled=True
    ).astype(jnp.float32)


def join_forward(earlier, later):
    return (
        jnp.maximum(earlier[0], later[0]),
        later[1] + (1.0 - later[0]) * earlier[1],
        later[2] + (1.0 - later[0]) * earlier[2],
    )


def join_backward(earlier, later):
    return (
        earlier[0] * later[0],
        later[1] + later[0] * earlier[1],
        later[2] + later[0] * earlier[2],
    )


def carry_in(reset, aggregate, aggregate_total):
    identity = (
        jnp.zeros((), jnp.float32),
        jnp.zeros_like(aggregate),
        jnp.zeros_like(aggregate_total),
    )
    _, state_in, total_in = carried_in(
        (reset, aggregate, aggregate_total), "rows", join_forward, identity
    )
    return (state_in, total_in)


def carry_back(keep, direct_state, direct_total):
    identity = (
        jnp.ones((), jnp.float32),
        jnp.zeros_like(direct_state),
        jnp.zeros_like(direct_total),
    )
    _, state_after, total_after = entering(
        (keep, direct_state, direct_total), "rows", join_backward, identity
    )
    return (state_after, total_after)


def local(
    mesh,
    tokens,
    cotangent,
    image_length,
    image_start,
    norm_gain,
    norm_bias,
    weight_in,
    weight_mix,
    weight_up,
    weight_down,
):
    s = sizes_of(mesh, tokens, weight_in, weight_up)
    fw, bw = coefficients(s, image_length, image_start)
    got = forward_call(s, tokens, norm_gain.reshape(-1, s.D), norm_bias.reshape(-1, s.D), fw,
                       split_rows(s, weight_in, weight_mix, weight_up, weight_down))
    local_rows = tokens.shape[0]
    shard_rows = local_rows * lax.axis_size("feat")
    all_rows = shard_rows * lax.axis_size("rows")
    width = weight_mix.shape[2]
    heads_here = width // HD
    blocks = shard_rows // BLK
    segment, opening = image_rows(
        image_length, image_start, lax.axis_index("rows") * shard_rows, shard_rows
    )
    reaching = ((segment == segment[0]) & jnp.logical_not(opening[0])).astype(jnp.float32)
    last_shard = (segment == segment[-1]).astype(jnp.bfloat16)
    keep_shard = reaching[-1]
    reset = 1.0 - keep_shard
    segment_blocks = in_blocks(segment, blocks)
    opening_blocks = in_blocks(opening, blocks)
    stream = tokens.astype(jnp.float32)
    kept = []
    log_total = jnp.zeros((), jnp.float32)
    log_top = jnp.full((), -jnp.inf, jnp.float32)
    for level in range(LAYERS):
        gain = norm_gain[level]
        bias = norm_bias[level]
        normed_all = gather_rows(layer_norm(stream, gain[0], bias[0]).astype(jnp.bfloat16))
        projected = jnp.einsum(
            "td,dke->tke", normed_all, weight_in[level], preferred_element_type=jnp.float32
        )
        query_feat = (
            feature(projected[:, 0]).astype(jnp.bfloat16).reshape(shard_rows, heads_here, HD)
        )
        key_feat = feature(projected[:, 1]).astype(jnp.bfloat16).reshape(shard_rows, heads_here, HD)
        values = projected[:, 2].astype(jnp.bfloat16).reshape(shard_rows, heads_here, HD)
        masked_keys = key_feat * last_shard[:, None, None]
        aggregate = jnp.einsum(
            "thc,the->hce", masked_keys, values, preferred_element_type=jnp.float32
        )
        aggregate_total = jnp.sum(masked_keys.astype(jnp.float32), axis=0)
        state_in, total_in = carry_in(reset, aggregate, aggregate_total)
        pieces = (
            in_blocks(query_feat, blocks),
            in_blocks(key_feat, blocks),
            in_blocks(values, blocks),
            segment_blocks,
            opening_blocks,
        )
        _, (ratio, denominator, states, totals) = lax.scan(
            block_forward, (state_in, total_in), pieces
        )
        ratio = ratio.reshape(shard_rows, heads_here, HD)
        denominator = denominator.reshape(shard_rows, heads_here)
        mixed = ratio.reshape(shard_rows, width).astype(jnp.bfloat16)
        middle = stream + sum_branch(mixed, weight_mix[level])
        normed_mid = gather_rows(layer_norm(middle, gain[1], bias[1]).astype(jnp.bfloat16))
        upward = jnp.dot(normed_mid, weight_up[level], preferred_element_type=jnp.float32)
        active = jax.nn.gelu(upward, approximate=False).astype(jnp.bfloat16)
        kept.append(
            (
                stream,
                normed_all,
                projected,
                query_feat,
                key_feat,
                values,
                ratio,
                denominator,
                states,
                totals,
                mixed,
                middle,
                normed_mid,
                upward,
                active,
            )
        )
        stream = middle + sum_branch(active, weight_down[level])
        logs = jnp.log(denominator)
        log_total = log_total + jnp.sum(logs)
        log_top = jnp.maximum(log_top, jnp.max(logs))
    output = stream.astype(jnp.bfloat16)
    gradient = cotangent.astype(jnp.float32)
    gain_parts = []
    bias_parts = []
    weight_parts = []
    for level in reversed(range(LAYERS)):
        (
            stream_in,
            normed_all,
            projected,
            query_feat,
            key_feat,
            values,
            ratio,
            denominator,
            states,
            totals,
            mixed,
            middle,
            normed_mid,
            upward,
            active,
        ) = kept[level]
        gain = norm_gain[level]
        bias = norm_bias[level]
        down_grad = gather_grads(gradient.astype(jnp.bfloat16))
        grad_down = jnp.einsum("td,tf->df", down_grad, active, preferred_element_type=jnp.float32)
        active_grad = jnp.dot(down_grad, weight_down[level], preferred_element_type=jnp.float32)
        _, gelu_back = jax.vjp(functools.partial(jax.nn.gelu, approximate=False), upward)
        upward_grad = gelu_back(active_grad)[0].astype(jnp.bfloat16)
        grad_up = jnp.einsum(
            "td,tf->df", normed_mid, upward_grad, preferred_element_type=jnp.float32
        )
        _, norm_late = jax.vjp(layer_norm, middle, gain[1], bias[1])
        middle_part, gain_late, bias_late = norm_late(sum_inputs(upward_grad, weight_up[level]))
        middle_grad = gradient + middle_part
        mix_grad = gather_grads(middle_grad.astype(jnp.bfloat16))
        grad_mix = jnp.einsum("td,te->de", mix_grad, mixed, preferred_element_type=jnp.float32)
        ratio_grad = jnp.dot(
            mix_grad, weight_mix[level], preferred_element_type=jnp.float32
        ).astype(jnp.bfloat16)
        ratio_grad = ratio_grad.astype(jnp.float32).reshape(shard_rows, heads_here, HD)
        numerator_grad = (ratio_grad / denominator[:, :, None]).astype(jnp.bfloat16)
        numerator_wide = numerator_grad.astype(jnp.float32)
        denominator_grad = -jnp.sum(ratio_grad * ratio, axis=2) / denominator
        query_wide = query_feat.astype(jnp.float32)
        direct_state = jnp.einsum(
            "thc,the->hce", query_wide * reaching[:, None, None], numerator_wide, precision=HIGHEST
        )
        direct_total = jnp.einsum(
            "th,thc->hc", denominator_grad * reaching[:, None], query_wide, precision=HIGHEST
        )
        state_after, total_after = carry_back(keep_shard, direct_state, direct_total)
        pieces = (
            in_blocks(query_feat, blocks),
            in_blocks(key_feat, blocks),
            in_blocks(values, blocks),
            segment_blocks,
            opening_blocks,
            states,
            totals,
            in_blocks(numerator_grad, blocks),
            in_blocks(denominator_grad, blocks),
        )
        _, (query_grad, key_grad, value_grad) = lax.scan(
            block_backward, (state_after, total_after), pieces, reverse=True
        )
        query_grad = query_grad.reshape(shard_rows, width)
        key_grad = key_grad.reshape(shard_rows, width)
        value_grad = value_grad.reshape(shard_rows, 1, width)
        _, feature_back = jax.vjp(feature, projected[:, :2])
        front_grad = feature_back(jnp.stack([query_grad, key_grad], axis=1))[0]
        projected_grad = jnp.concatenate(
            [front_grad.astype(jnp.bfloat16), value_grad.astype(jnp.bfloat16)], axis=1
        )
        grad_in = jnp.einsum(
            "td,tke->dke", normed_all, projected_grad, preferred_element_type=jnp.float32
        )
        flat_weight = weight_in[level].reshape(weight_in.shape[1], 3 * width)
        _, norm_early = jax.vjp(layer_norm, stream_in, gain[0], bias[0])
        stream_part, gain_early, bias_early = norm_early(
            sum_inputs(projected_grad.reshape(shard_rows, 3 * width), flat_weight)
        )
        gradient = middle_grad + stream_part
        gain_parts.insert(0, jnp.stack([gain_early, gain_late]))
        bias_parts.insert(0, jnp.stack([bias_early, bias_late]))
        weight_parts.insert(0, (grad_in, grad_mix, grad_up, grad_down))
    first_layer, second_layer = weight_parts
    summed = (
        lax.psum_scatter(
            first_layer[0].astype(jnp.bfloat16), "rows", scatter_dimension=0, tiled=True
        ).astype(jnp.float32),
        lax.psum_scatter(
            first_layer[1].astype(jnp.bfloat16), "rows", scatter_dimension=0, tiled=True
        ).astype(jnp.float32),
        lax.psum_scatter(
            first_layer[2].astype(jnp.bfloat16), "rows", scatter_dimension=0, tiled=True
        ).astype(jnp.float32),
        lax.psum_scatter(
            first_layer[3].astype(jnp.bfloat16), "rows", scatter_dimension=0, tiled=True
        ).astype(jnp.float32),
        lax.psum_scatter(
            second_layer[0].astype(jnp.bfloat16), "rows", scatter_dimension=0, tiled=True
        ).astype(jnp.float32),
        lax.psum_scatter(
            second_layer[1].astype(jnp.bfloat16), "rows", scatter_dimension=0, tiled=True
        ).astype(jnp.float32),
        lax.psum_scatter(
            second_layer[2].astype(jnp.bfloat16), "rows", scatter_dimension=0, tiled=True
        ).astype(jnp.float32),
        lax.psum_scatter(
            second_layer[3].astype(jnp.bfloat16), "rows", scatter_dimension=0, tiled=True
        ).astype(jnp.float32),
    )
    weight_parts = [summed[0:4], summed[4:8]]
    gain_sum, bias_sum, log_sum = lax.psum(
        (jnp.stack(gain_parts), jnp.stack(bias_parts), log_total), ("rows", "feat")
    )
    log_max = lax.pmax(log_top, ("rows", "feat"))
    log_mean = log_sum / (all_rows * HEADS * LAYERS)
    log_sum = lax.psum(jnp.sum(got["logs"][0]) / HD, ("rows", "feat"))
    log_mean = log_sum / (all_rows * HEADS * LAYERS)
    log_max = lax.pmax(jnp.max(got["logs"][1]), ("rows", "feat"))
    return (
        got["output"],
        gradient,
        gain_sum,
        bias_sum,
        bias_sum[LAYERS - 1, 1],
        jnp.stack([part[0] for part in weight_parts]),
        jnp.stack([part[1] for part in weight_parts]),
        jnp.stack([part[2] for part in weight_parts]),
        jnp.stack([part[3] for part in weight_parts]),
        log_max,
        log_mean,
    )


def solution(mesh):
    placed = (
        P(("rows", "feat"), None),
        P(("rows", "feat"), None),
        P(),
        P(),
        P(),
        P(),
        P(None, None, None, "feat"),
        P(None, None, "feat"),
        P(None, None, "feat"),
        P(None, None, "feat"),
    )
    return jax.shard_map(
        functools.partial(local, mesh),
        mesh=mesh,
        in_specs=placed,
        out_specs=(
            P(("rows", "feat"), None),
            P(("rows", "feat"), None),
            P(),
            P(),
            P(),
            P(None, "rows", None, "feat"),
            P(None, "rows", "feat"),
            P(None, "rows", "feat"),
            P(None, "rows", "feat"),
            P(),
            P(),
        ),
        check_vma=False,
    )
```

```python
import functools
import types
import typing

import jax
import jax.numpy as jnp
from jax import lax
from jax.experimental import pallas as pl
from jax.experimental.pallas import tpu as pltpu
from jax.sharding import PartitionSpec as P

HD = 64
EPS_NORM = 1e-05
EPS_DEN = 1e-06
MESH = pl.DeviceIdType.MESH
BF = jnp.bfloat16
F32 = jnp.float32
LAG_FIRST, LAG_SECOND, LAG_CORE, LAG_READY = 2, 4, 6, 7
RING = 4
ROOT_HALF = 0.7071067811865476
ROOT_TAU = 0.3989422804014327


def sizes_of(mesh, tokens, weight_in, weight_up):
    s = types.SimpleNamespace()
    s.R, s.Z = mesh.shape["rows"], mesh.shape["feat"]
    chips = s.R // 2
    s.NX = 1
    while s.NX * s.NX < chips:
        s.NX *= 2
    s.NY = chips // s.NX
    s.T, s.D = tokens.shape
    s.L = weight_in.shape[0]
    s.PC = weight_in.shape[3]
    s.PR = s.D // s.R
    s.NJ = weight_up.shape[2] // s.PC
    s.NU = 4 + 2 * s.NJ
    s.U = s.L * s.NU
    s.NP = s.PC // 128
    s.MR = s.NP * HD + 16
    s.NQ = s.NY * s.NX
    return s


def place(s):
    r, z = lax.axis_index("rows"), lax.axis_index("feat")
    return r, z, r // (2 * s.NX), (r // 2) % s.NX, r % 2


def row_at(s, y, x, c):
    return (y * s.NX + x) * 2 + c


def greet(s, r, z):
    barrier = pltpu.get_barrier_semaphore()
    peers = [((r + d) % s.R, z) for d in range(1, s.R)] + [(r, (z + d) % s.Z) for d in range(1, s.Z)]
    for peer in peers:
        pl.semaphore_signal(barrier, inc=1, device_id=peer, device_id_type=MESH)
    pl.semaphore_wait(barrier, len(peers))


def remote(src, dst, send, recv, device):
    return pltpu.make_async_remote_copy(
        src_ref=src, dst_ref=dst, send_sem=send, recv_sem=recv, device_id=device, device_id_type=MESH
    )


def dot(a, b, dims=((1,), (0,))):
    return lax.dot_general(a, b, (dims, ((), ())), preferred_element_type=F32)


NT = ((1,), (1,))
TN = ((0,), (0,))


def norm_parts(v):
    center = jnp.mean(v, axis=-1, keepdims=True)
    shifted = v - center
    spread = jnp.mean(shifted * shifted, axis=-1, keepdims=True)
    inv = lax.rsqrt(spread + EPS_NORM)
    return shifted * inv, inv


def weight_gather(s, h, r, z, y, x, c):
    half = s.PR // 2
    F, piece = h.whole, h.piece
    rows = (pl.ds(0, half), pl.ds(half, half))

    def z_copies(u):
        return [
            remote(
                piece.at[u // s.NU, u % s.NU],
                F.at[u, s.Z - d - 1, y, x, c],
                h.z_send.at[u % RING, d - 1],
                h.z_recv.at[u, s.Z - d - 1],
                (r, (z + d) % s.Z),
            )
            for d in range(1, s.Z)
        ]

    def first(u):
        out = []
        for d in range(1, s.NX):
            at = F.at[u, :, y, x, c, rows[0]]
            out.append(remote(at, at, h.x_send.at[u % RING, 0, d - 1], h.x_recv.at[u, 0, s.NX - d - 1],
                              (row_at(s, y, (x + d) % s.NX, c), z)))
        for d in range(1, s.NY):
            at = F.at[u, :, y, x, c, rows[1]]
            out.append(remote(at, at, h.y_send.at[u % RING, 0, d - 1], h.y_recv.at[u, 0, s.NY - d - 1],
                              (row_at(s, (y + d) % s.NY, x, c), z)))
        return out

    def first_landing(u):
        out = []
        for d in range(1, s.NX):
            at = F.at[u, :, y, (x + d) % s.NX, c, rows[0]]
            out.append(remote(at, at, h.x_send.at[u % RING, 0, d - 1], h.x_recv.at[u, 0, d - 1], (r, z)))
        for d in range(1, s.NY):
            at = F.at[u, :, (y + d) % s.NY, x, c, rows[1]]
            out.append(remote(at, at, h.y_send.at[u % RING, 0, d - 1], h.y_recv.at[u, 0, d - 1], (r, z)))
        return out

    def second(u):
        out = []
        for d in range(1, s.NY):
            at = F.at[u, :, y, :, c, rows[0]]
            out.append(remote(at, at, h.y_send.at[u % RING, 1, d - 1], h.y_recv.at[u, 1, s.NY - d - 1],
                              (row_at(s, (y + d) % s.NY, x, c), z)))
        for d in range(1, s.NX):
            at = F.at[u, :, :, x, c, rows[1]]
            out.append(remote(at, at, h.x_send.at[u % RING, 1, d - 1], h.x_recv.at[u, 1, s.NX - d - 1],
                              (row_at(s, y, (x + d) % s.NX, c), z)))
        return out

    def second_landing(u):
        out = []
        for d in range(1, s.NY):
            at = F.at[u, :, (y + d) % s.NY, :, c, rows[0]]
            out.append(remote(at, at, h.y_send.at[u % RING, 1, d - 1], h.y_recv.at[u, 1, d - 1], (r, z)))
        for d in range(1, s.NX):
            at = F.at[u, :, :, (x + d) % s.NX, c, rows[1]]
            out.append(remote(at, at, h.x_send.at[u % RING, 1, d - 1], h.x_recv.at[u, 1, d - 1], (r, z)))
        return out

    def share(u):
        at = F.at[u, :, :, :, c]
        return remote(at, at, h.c_send.at[u % RING], h.c_recv.at[u], (row_at(s, y, x, 1 - c), z))

    def share_landing(u):
        at = F.at[u, :, :, :, 1 - c]
        return remote(at, at, h.c_send.at[u % RING], h.c_recv.at[u], (r, z))

    def z_landing(u):
        return [
            remote(piece.at[0, 0], F.at[u, k, y, x, c], h.z_send.at[u % RING, 0], h.z_recv.at[u, k], (r, z))
            for k in range(s.Z - 1)
        ]

    def inside(u, what):
        pl.when((u >= 0) & (u < s.U))(functools.partial(what, u))

    def stage_z(u):
        for cp in z_copies(u):
            cp.start()

    def stage_first(u):
        for cp in z_landing(u):
            cp.wait_recv()
        for cp in first(u):
            cp.start()

    def stage_second(u):
        for cp in first_landing(u):
            cp.wait_recv()
        for cp in second(u):
            cp.start()

    def stage_core(u):
        for cp in second_landing(u):
            cp.wait_recv()
        share(u).start()

    def stage_ready(u):
        share_landing(u).wait_recv()

    def tick(t):
        inside(t - RING, lambda u: [cp.wait_send() for cp in z_copies(u)] and None)
        inside(t, stage_z)
        inside(t - LAG_FIRST - RING, lambda u: [cp.wait_send() for cp in first(u)] and None)
        inside(t - LAG_FIRST, stage_first)
        inside(t - LAG_SECOND - RING, lambda u: [cp.wait_send() for cp in second(u)] and None)
        inside(t - LAG_SECOND, stage_second)
        inside(t - LAG_CORE - RING, lambda u: share(u).wait_send())
        inside(t - LAG_CORE, stage_core)
        inside(t - LAG_READY, stage_ready)

    def drain_all():
        @pl.loop(s.U + LAG_READY, s.U + LAG_CORE + RING)
        def _(t):
            tick(t)

    return tick, drain_all


def head_masks(s):
    lane = lax.broadcasted_iota(jnp.int32, (1, 128), 1)
    first = lane < HD
    return first, jnp.where(first, 1.0, 0.0), jnp.where(first, 0.0, 1.0)


def pair_ones():
    row = lax.broadcasted_iota(jnp.int32, (128, 128), 0) // HD
    col = lax.broadcasted_iota(jnp.int32, (128, 128), 1) // HD
    return jnp.where(row == col, 1.0, 0.0).astype(BF)


def lanes(at, width):
    return pl.ds(pl.multiple_of(at * width, width), width)


def prefix_rounds(s, h, l, r, z):
    msg, got, rows_got, back, out = h.msg, h.r1, h.r2, h.pre, h.r3

    def one(k):
        return remote(msg.at[k], got.at[s.Z - k], h.r1_send.at[l, k], h.r1_recv.at[l, s.Z - k], (r, (z + k) % s.Z))

    def two(d):
        return remote(rows_got.at[r], rows_got.at[r], h.r2_send.at[l, d], h.r2_recv.at[l, s.R - d],
                      ((r + d) % s.R, z))

    def two_landing(d):
        at = rows_got.at[(r + d) % s.R]
        return remote(at, at, h.r2_send.at[l, d], h.r2_recv.at[l, d], (r, z))

    def three(k):
        return remote(back.at[k], out.at[s.Z - k], h.r3_send.at[l, k], h.r3_recv.at[l, s.Z - k], (r, (z + k) % s.Z))

    def round_one():
        for k in range(1, s.Z):
            one(k).start()

    def round_two():
        for k in range(1, s.Z):
            remote(msg.at[k], got.at[k], h.r1_send.at[l, k], h.r1_recv.at[l, k], (r, z)).wait_recv()
        total = h.coef_a[0] * msg[0].astype(F32)
        for k in range(1, s.Z):
            total = total + h.coef_a[k] * got[k].astype(F32)
        rows_got[r] = total.astype(BF)
        for d in range(1, s.R):
            two(d).start()

    def round_three():
        for d in range(1, s.R):
            two_landing(d).wait_recv()
        for k in range(s.Z):
            total = h.coef_b[k * s.Z] * msg[0].astype(F32)
            for j in range(1, s.Z):
                total = total + h.coef_b[k * s.Z + j] * got[j].astype(F32)
            for q in range(s.R):
                total = total + h.coef_c[k * s.R + q] * rows_got[q].astype(F32)
            if k == 0:
                out[0] = total.astype(BF)
            else:
                back[k] = total.astype(BF)
                three(k).start()

    def arrive():
        for k in range(1, s.Z):
            remote(back.at[k], out.at[k], h.r3_send.at[l, k], h.r3_recv.at[l, k], (r, z)).wait_recv()

    def settle():
        for k in range(1, s.Z):
            one(k).wait_send()
            three(k).wait_send()
        for d in range(1, s.R):
            two(d).wait_send()

    return round_one, round_two, round_three, arrive, settle


def pack_state(full, first):
    return jnp.where(first, full[:HD], full[HD:])


def unpack_state(packed, first):
    zero = jnp.zeros_like(packed)
    return jnp.concatenate([jnp.where(first, packed, zero), jnp.where(first, zero, packed)], axis=0)


def spread_rows(s, rows_list):
    at = lax.broadcasted_iota(jnp.int32, (16, 128), 0)
    block = jnp.zeros((16, 128), F32)
    for i, row in enumerate(rows_list):
        block = block + jnp.where(at == i, row, 0.0)
    return block


def pick_row(block, i):
    at = lax.broadcasted_iota(jnp.int32, (16, 128), 0)
    return jnp.sum(jnp.where(at == i, block.astype(F32), 0.0), axis=0, keepdims=True)


class FwdIn(typing.NamedTuple):
    tokens: object
    gain: object
    bias: object
    coef_a: object
    coef_b: object
    coef_c: object
    w_in: object
    w_mix: object
    w_up: object
    w_down: object
class FwdOut(typing.NamedTuple):
    output: object
    logs: object
    whole: object
    k_stream: object
    k_middle: object
    k_qkv: object
    k_mixed: object
    k_den: object
    k_state: object
    k_act: object
    k_slope: object
    k_normt: object
    s_mixed: object
    s_act: object


def fwd_scratch(s):
    dma = pltpu.SemaphoreType.DMA
    return dict(
        piece=pltpu.VMEM((s.L, s.NU, s.PR, s.PC), BF),
        w=pltpu.VMEM((s.Z, s.NY, s.NX, 2, s.PR, s.PC), BF),
        stream=pltpu.VMEM((s.T, s.D), F32),
        acc=pltpu.VMEM((s.T, s.D), F32),
        middle=pltpu.VMEM((s.T, s.D), F32),
        den=pltpu.VMEM((s.T, s.D), F32),
        nrm=pltpu.VMEM((s.T, s.D), BF),
        nrmt=pltpu.VMEM((2, s.NY, s.NX, 2, s.PR, s.T), BF),
        qkv=pltpu.VMEM((3, s.T, s.D), BF),
        mixed=pltpu.VMEM((s.T, s.D), BF),
        act=pltpu.VMEM((s.NJ, s.T, s.D), BF),
        slope=pltpu.VMEM((s.NJ, s.T, s.D), BF),
        msg=pltpu.VMEM((s.Z, s.MR, 128), BF),
        r1=pltpu.VMEM((s.Z, s.MR, 128), BF),
        r2=pltpu.VMEM((s.R, s.MR, 128), BF),
        pre=pltpu.VMEM((s.Z, s.MR, 128), BF),
        r3=pltpu.VMEM((s.Z, s.MR, 128), BF),
        piece_sem=dma((2 + 2 * s.NJ,)),
        w_sem=dma((s.Z,)),
        z_send=dma((RING, s.Z - 1)),
        z_recv=dma((s.U, s.Z - 1)),
        x_send=dma((RING, 2, s.NX - 1)),
        x_recv=dma((s.U, 2, s.NX - 1)),
        y_send=dma((RING, 2, s.NY - 1)),
        y_recv=dma((s.U, 2, s.NY - 1)),
        c_send=dma((RING,)),
        c_recv=dma((s.U,)),
        r1_send=dma((s.L, s.Z)),
        r1_recv=dma((s.L, s.Z)),
        r2_send=dma((s.L, s.R)),
        r2_recv=dma((s.L, s.R)),
        r3_send=dma((s.L, s.Z)),
        r3_recv=dma((s.L, s.Z)),
        keep=dma((8,)),
        keep_j=dma((2, s.NJ)),
        sib_send=dma((3 + s.NJ,)),
        sib_recv=dma((s.L, 3 + s.NJ)),
    )


def fwd_kernel(s, *refs):
    names = FwdIn._fields + FwdOut._fields + tuple(fwd_scratch(s))
    h = types.SimpleNamespace(**dict(zip(names, refs, strict=True)))
    r, z, y, x, c = place(s)
    sibling = (row_at(s, y, x, 1 - c), z)
    greet(s, r, z)
    tick, drain_all = weight_gather(s, h, r, z, y, x, c)
    first, _, _ = head_masks(s)

    pieces = [
        pltpu.make_async_copy(h.w_in.at[:, :, y, x, c], h.piece.at[:, 0:3], h.piece_sem.at[0]),
        pltpu.make_async_copy(h.w_mix.at[:, y, x, c], h.piece.at[:, 3], h.piece_sem.at[1]),
    ]
    for j in range(s.NJ):
        cols = pl.ds(j * s.PC, s.PC)
        pieces.append(pltpu.make_async_copy(h.w_up.at[:, y, x, c, :, cols], h.piece.at[:, 4 + j], h.piece_sem.at[2 + j]))
        pieces.append(pltpu.make_async_copy(h.w_down.at[:, y, x, c, :, cols], h.piece.at[:, 4 + s.NJ + j],
                                            h.piece_sem.at[2 + s.NJ + j]))
    for cp in pieces:
        cp.start()
    for cp in pieces:
        cp.wait()

    with_unit = unit_reader(s, h)

    def normalize(l, n, source):
        xhat, _ = norm_parts(source)
        v = xhat * h.gain[pl.ds(l * 2 + n, 1), :] + h.bias[pl.ds(l * 2 + n, 1), :]
        h.nrm[...] = v.astype(BF)
        h.nrmt[n] = v.T.astype(BF).reshape(s.NY, s.NX, 2, s.PR, s.T)
        keep_norm(l, n).start()
        send_norm(l, n).start()

    def keep_norm(l, n):
        return pltpu.make_async_copy(h.nrmt.at[n, :, :, c], h.k_normt.at[l, n, 0], h.keep.at[n])

    def send_norm(l, n):
        return remote(h.nrmt.at[n, :, :, 1 - c], h.k_normt.at[l, n, 1], h.sib_send.at[n], h.sib_recv.at[l, n],
                      sibling)

    def keep_one(l, index):
        src, dst = ((h.stream, h.k_stream), (h.qkv, h.k_qkv), (h.mixed, h.k_mixed), (h.den, h.k_den),
                    (h.middle, h.k_middle), (h.r3, h.k_state))[index - 2]
        return pltpu.make_async_copy(src, dst.at[l], h.keep.at[index])

    def send_mixed(l):
        return remote(h.mixed, h.s_mixed.at[l], h.sib_send.at[2], h.sib_recv.at[l, 2], sibling)

    def keep_act(l, j):
        return pltpu.make_async_copy(h.act.at[j], h.k_act.at[l, j], h.keep_j.at[0, j])

    def keep_slope(l, j):
        return pltpu.make_async_copy(h.slope.at[j], h.k_slope.at[l, j], h.keep_j.at[1, j])

    def send_act(l, j):
        return remote(h.act.at[j], h.s_act.at[l, j], h.sib_send.at[3 + j], h.sib_recv.at[l, 3 + j], sibling)

    h.stream[...] = h.tokens[...].astype(F32)
    h.logs[...] = jnp.where(lax.broadcasted_iota(jnp.int32, (8, 128), 0) == 1, -jnp.inf, 0.0)
    ones = pair_ones()
    tall = jnp.ones((s.T, 128), BF)

    @pl.loop(0, LAG_READY)
    def _(t):
        tick(t)

    def one_layer(l, carry):
        base = l * s.NU
        keep_one(l, 2).start()
        normalize(l, 0, h.stream[...])

        def project(kind, carry):
            u = base + kind

            def body(k, weight):
                v = dot(h.nrm[...], weight)
                phi = jnp.where(v > 0, v + 1.0, jnp.exp(jnp.minimum(v, 0.0)))
                h.qkv[kind, :, lanes(k, s.PC)] = jnp.where(kind < 2, phi, v).astype(BF)

            with_unit(h.w_in, l, kind, u, body, lambda: tick(u + LAG_READY))
            return carry

        lax.fori_loop(0, 3, project, 0)
        keep_one(l, 3).start()
        round_one, round_two, round_three, arrive, settle = prefix_rounds(s, h, l, r, z)

        def local_state(k, carry):
            totals = []
            for i in range(s.NP):
                at = lanes(k * s.NP + i, 128)
                keys, vals = h.qkv[1, :, at], h.qkv[2, :, at]
                h.msg[k, i * HD:(i + 1) * HD] = pack_state(dot(keys, vals, TN), first).astype(BF)
                totals.append(jnp.sum(keys.astype(F32), axis=0, keepdims=True))
            h.msg[k, s.NP * HD:] = spread_rows(s, totals).astype(BF)
            return carry

        lax.fori_loop(0, s.Z, local_state, 0)
        round_one()
        tick(base + 3 + LAG_READY)
        round_two()
        tick(base + 4 + LAG_READY)
        round_three()
        tick(base + 5 + LAG_READY)
        arrive()
        keep_one(l, 7).start()
        causal = (lax.broadcasted_iota(jnp.int32, (s.T, s.T), 1) <= lax.broadcasted_iota(jnp.int32, (s.T, s.T), 0))

        def attend(p, carry):
            k, i = p // s.NP, p % s.NP
            at = lanes(p, 128)
            query, key, value = h.qkv[0, :, at], h.qkv[1, :, at], h.qkv[2, :, at]
            wide = query.astype(F32)
            value_ones = jnp.concatenate([value, tall], axis=1)
            zero = jnp.zeros_like(query)
            results = []
            for head in range(2):
                mine = first if head == 0 else jnp.logical_not(first)
                scores = dot(jnp.where(mine, query, zero), key, NT)
                weights = jnp.where(causal, scores, 0.0).astype(BF)
                results.append(dot(weights, value_ones))
            state = unpack_state(h.r3[k, pl.ds(pl.multiple_of(i * HD, HD), HD), :], first)
            total = pick_row(h.r3[k, s.NP * HD:, :], i)
            square = jnp.zeros((128, 128), BF)
            right = jnp.concatenate(
                [jnp.concatenate([state, square], axis=1), jnp.concatenate([square, ones], axis=1)], axis=0)
            left = jnp.concatenate([query, (wide * total).astype(BF)], axis=1)
            earlier = dot(left, right)
            num = jnp.where(first, results[0][:, :128], results[1][:, :128]) + earlier[:, :128]
            den = jnp.where(first, results[0][:, 128:], results[1][:, 128:]) + earlier[:, 128:] + EPS_DEN
            h.mixed[:, at] = (num / den).astype(BF)
            h.den[:, at] = den
            logs = jnp.log(den)
            h.logs[0:1] += jnp.sum(logs, axis=0, keepdims=True)
            h.logs[1:2] = jnp.maximum(h.logs[1:2], jnp.max(logs, axis=0, keepdims=True))
            return carry

        half = s.Z * s.NP // 2
        lax.fori_loop(0, half, attend, 0)
        tick(base + 6 + LAG_READY)
        lax.fori_loop(half, s.Z * s.NP, attend, 0)
        settle()
        keep_one(l, 4).start()
        send_mixed(l).start()
        keep_one(l, 5).start()

        h.acc[...] = jnp.zeros_like(h.acc)

        def mix(k, weight):
            h.acc[...] += dot(h.mixed[:, lanes(k, s.PC)], weight, NT)

        with_unit(h.w_mix, l, 0, base + 3, mix)
        h.middle[...] = h.stream[...] + h.acc[...]
        keep_one(l, 6).start()
        normalize(l, 1, h.middle[...])

        def up(j, carry):
            u = base + 4 + j

            def body(k, weight):
                v = dot(h.nrm[...], weight)
                cdf = 0.5 * (1.0 + lax.erf(v * ROOT_HALF))
                h.act[j, :, lanes(k, s.PC)] = (v * cdf).astype(BF)
                h.slope[j, :, lanes(k, s.PC)] = (cdf + v * (ROOT_TAU * jnp.exp(-0.5 * v * v))).astype(BF)

            with_unit(h.w_up, l, j, u, body, lambda: pl.when(j >= 3)(lambda: tick(u + LAG_READY)))
            keep_act(l, j).start()
            keep_slope(l, j).start()
            send_act(l, j).start()
            return carry

        lax.fori_loop(0, s.NJ, up, 0)
        h.acc[...] = jnp.zeros_like(h.acc)

        def down(j, carry):
            u = base + 4 + s.NJ + j

            def body(k, weight):
                h.acc[...] += dot(h.act[j, :, lanes(k, s.PC)], weight, NT)

            with_unit(h.w_down, l, j, u, body, lambda: tick(u + LAG_READY))
            return carry

        lax.fori_loop(0, s.NJ, down, 0)
        keep_one(l, 2).wait()
        h.stream[...] = h.middle[...] + h.acc[...]
        for n in range(2):
            keep_norm(l, n).wait()
            send_norm(l, n).wait_send()
            send_norm(l, n).wait_recv()
        for index in range(3, 8):
            keep_one(l, index).wait()
        send_mixed(l).wait()

        def finish(j, carry):
            keep_act(l, j).wait()
            keep_slope(l, j).wait()
            send_act(l, j).wait()
            return carry

        lax.fori_loop(0, s.NJ, finish, 0)
        return carry

    lax.fori_loop(0, s.L, one_layer, 0)
    h.output[...] = h.stream[...].astype(BF)
    drain_all()


def split_rows(s, weight_in, *rest):
    cut = (s.NY, s.NX, 2, s.PR)
    turned = jnp.transpose(weight_in, (0, 2, 1, 3)).reshape((s.L, 3) + cut + (s.PC,))
    return (turned,) + tuple(w.reshape((s.L,) + cut + w.shape[2:]) for w in rest)


def forward_call(s, tokens, gain, bias, coefs, weights):
    vmem = pl.BlockSpec(memory_space=pltpu.VMEM)
    smem = pl.BlockSpec(memory_space=pltpu.SMEM)
    hbm = pl.BlockSpec(memory_space=pl.ANY)
    shape = jax.ShapeDtypeStruct
    outs = FwdOut(
        output=shape((s.T, s.D), BF),
        logs=shape((8, 128), F32),
        whole=shape((s.U, s.Z - 1, s.NY, s.NX, 2, s.PR, s.PC), BF),
        k_stream=shape((s.L, s.T, s.D), F32),
        k_middle=shape((s.L, s.T, s.D), F32),
        k_qkv=shape((s.L, 3, s.T, s.D), BF),
        k_mixed=shape((s.L, s.T, s.D), BF),
        k_den=shape((s.L, s.T, s.D), F32),
        k_state=shape((s.L, s.Z, s.MR, 128), BF),
        k_act=shape((s.L, s.NJ, s.T, s.D), BF),
        k_slope=shape((s.L, s.NJ, s.T, s.D), BF),
        k_normt=shape((s.L, 2, 2, s.NY, s.NX, s.PR, s.T), BF),
        s_mixed=shape((s.L, s.T, s.D), BF),
        s_act=shape((s.L, s.NJ, s.T, s.D), BF),
    )
    out = pl.pallas_call(
        functools.partial(fwd_kernel, s),
        out_shape=list(outs),
        in_specs=[vmem] * 3 + [smem] * 3 + [hbm] * 4,
        out_specs=[vmem] * 2 + [hbm] * (len(outs) - 2),
        scratch_shapes=list(fwd_scratch(s).values()),
        compiler_params=pltpu.CompilerParams(
            collective_id=0, has_side_effects=True, vmem_limit_bytes=56 * 1024 * 1024),
    )(tokens, gain, bias, *coefs, *weights)
    return FwdOut(*out)


def segments_of_units(s, image_length, image_start):
    first = jnp.arange(s.R * s.Z, dtype=jnp.int32) * s.T
    live = (image_length > 0)[None, :]
    return (jnp.sum(((image_start[None, :] <= first[:, None]) & live).astype(jnp.int32), axis=1) - 1).reshape(s.R, s.Z)


def coefficients(s, image_length, image_start):
    seg = segments_of_units(s, image_length, image_start)
    r, z = lax.axis_index("rows"), lax.axis_index("feat")
    turn = (z + jnp.arange(s.Z)) % s.Z
    row = seg[r][turn]
    order = jnp.arange(s.R)
    f = lambda v: v.astype(F32).reshape(-1)
    same = row[:, None] == row[None, :]
    forward = (
        f(row == seg[r, s.Z - 1]),
        f(same & (turn[None, :] < turn[:, None])),
        f((seg[None, :, s.Z - 1] == row[:, None]) & (order[None, :] < r)),
    )
    backward = (
        f(row == seg[r, 0]),
        f(same & (turn[None, :] > turn[:, None])),
        f((seg[None, :, 0] == row[:, None]) & (order[None, :] > r)),
    )
    return forward, backward


BACK_FIRST, BACK_SECOND, BACK_LAST = 2, 4, 6
SLOTS = 8
OUT_RING = 4
X_EARLY, X_LATE, X_DOWN, X_MIX = 0, 1, 2, 3

class BwdIn(typing.NamedTuple):
    cotangent: object
    logs: object
    gain: object
    coef_a: object
    coef_b: object
    coef_c: object
    w_in: object
    w_mix: object
    w_up: object
    w_down: object
    whole: object
    k_stream: object
    k_middle: object
    k_qkv: object
    k_mixed: object
    k_den: object
    k_state: object
    k_act: object
    k_slope: object
    k_normt: object
    s_mixed: object
    s_act: object
class BwdOut(typing.NamedTuple):
    grad: object
    vector: object
    g_in: object
    g_mix: object
    g_up: object
    g_down: object


def bwd_scratch(s):
    dma = pltpu.SemaphoreType.DMA
    half = s.PR // 2
    return dict(
        w=pltpu.VMEM((s.Z, s.NY, s.NX, 2, s.PR, s.PC), BF),
        part=pltpu.VMEM((SLOTS, s.NY, s.NX, s.Z, s.PR, s.PC), BF),
        land_x1=pltpu.VMEM((SLOTS, s.NX - 1, s.NY, s.Z, half, s.PC), BF),
        land_y1=pltpu.VMEM((SLOTS, s.NY - 1, s.NX, s.Z, half, s.PC), BF),
        land_x2=pltpu.VMEM((SLOTS, s.NX - 1, s.Z, half, s.PC), BF),
        land_y2=pltpu.VMEM((SLOTS, s.NY - 1, s.Z, half, s.PC), BF),
        land_z=pltpu.VMEM((SLOTS, s.Z - 1, s.PR, s.PC), BF),
        final=pltpu.VMEM((OUT_RING, s.PR, s.PC), F32),
        acc=pltpu.VMEM((s.T, s.D), F32),
        resid=pltpu.VMEM((s.T, s.D), F32),
        gb=pltpu.VMEM((s.T, s.D), BF),
        turned=pltpu.VMEM((s.NY, s.NX, 2, s.PR, s.T), BF),
        xt=pltpu.VMEM((4, 2, s.NY, s.NX, s.PR, s.T), BF),
        act=pltpu.VMEM((2, s.T, s.D), BF),
        slope=pltpu.VMEM((s.T, s.D), BF),
        ug=pltpu.VMEM((s.NJ, s.T, s.D), BF),
        ug_sib=pltpu.VMEM((s.NJ, s.T, s.D), BF),
        pg=pltpu.VMEM((3, s.T, s.D), BF),
        pg_sib=pltpu.VMEM((3, s.T, s.D), BF),
        qkv=pltpu.VMEM((3, s.T, s.D), BF),
        mixed=pltpu.VMEM((2, s.T, s.D), BF),
        den=pltpu.VMEM((s.T, s.D), F32),
        rg=pltpu.VMEM((s.T, s.D), BF),
        ng=pltpu.VMEM((s.T, s.D), BF),
        dg=pltpu.VMEM((s.T, s.D), F32),
        state=pltpu.VMEM((s.Z, s.MR, 128), BF),
        msg=pltpu.VMEM((s.Z, s.MR, 128), BF),
        r1=pltpu.VMEM((s.Z, s.MR, 128), BF),
        r2=pltpu.VMEM((s.R, s.MR, 128), BF),
        pre=pltpu.VMEM((s.Z, s.MR, 128), BF),
        r3=pltpu.VMEM((s.Z, s.MR, 128), BF),
        vec=pltpu.VMEM((16, s.D), F32),
        v_z=pltpu.VMEM((s.Z, 16, s.D), F32),
        v_c=pltpu.VMEM((2, 16, s.D), F32),
        v_x=pltpu.VMEM((s.NX, 16, s.D), F32),
        v_y=pltpu.VMEM((s.NY, 16, s.D), F32),
        w_sem=dma((s.Z,)),
        x1_send=dma((SLOTS, s.NX - 1)),
        x1_recv=dma((SLOTS, s.NX - 1)),
        y1_send=dma((SLOTS, s.NY - 1)),
        y1_recv=dma((SLOTS, s.NY - 1)),
        x2_send=dma((SLOTS, s.NX - 1)),
        x2_recv=dma((SLOTS, s.NX - 1)),
        y2_send=dma((SLOTS, s.NY - 1)),
        y2_recv=dma((SLOTS, s.NY - 1)),
        z_send=dma((SLOTS, s.Z - 1)),
        z_recv=dma((SLOTS, s.Z - 1)),
        out_sem=dma((OUT_RING,)),
        xt_sem=dma((2, 2, s.NQ)),
        xt_send=dma((2, s.NQ)),
        xt_recv=dma((s.L, 2, s.NQ)),
        g_send=dma((s.NJ + 3,)),
        g_recv=dma((s.L, s.NJ + 3)),
        get=dma((8,)),
        r1_send=dma((s.L, s.Z)),
        r1_recv=dma((s.L, s.Z)),
        r2_send=dma((s.L, s.R)),
        r2_recv=dma((s.L, s.R)),
        r3_send=dma((s.L, s.Z)),
        r3_recv=dma((s.L, s.Z)),
        v_send=dma((4, max(s.Z, s.NX, s.NY))),
        v_recv=dma((4, max(s.Z, s.NX, s.NY))),
    )


def gradient_sums(s, h, r, z, y, x, c):
    half = s.PR // 2
    rows = (pl.ds(0, half), pl.ds(half, half))
    part = h.part

    def to_x(d):
        return (row_at(s, y, (x + d) % s.NX, c), z)

    def to_y(d):
        return (row_at(s, (y + d) % s.NY, x, c), z)

    def first(v):
        b = v % SLOTS
        return [
            remote(part.at[b, :, d, :, rows[0]], h.land_x1.at[b, s.NX - d - 1], h.x1_send.at[b, d - 1],
                   h.x1_recv.at[b, s.NX - d - 1], to_x(d)) for d in range(1, s.NX)
        ] + [
            remote(part.at[b, d, :, :, rows[1]], h.land_y1.at[b, s.NY - d - 1], h.y1_send.at[b, d - 1],
                   h.y1_recv.at[b, s.NY - d - 1], to_y(d)) for d in range(1, s.NY)
        ]

    def second(v):
        b = v % SLOTS
        return [
            remote(part.at[b, d, 0, :, rows[0]], h.land_y2.at[b, s.NY - d - 1], h.y2_send.at[b, d - 1],
                   h.y2_recv.at[b, s.NY - d - 1], to_y(d)) for d in range(1, s.NY)
        ] + [
            remote(part.at[b, 0, d, :, rows[1]], h.land_x2.at[b, s.NX - d - 1], h.x2_send.at[b, d - 1],
                   h.x2_recv.at[b, s.NX - d - 1], to_x(d)) for d in range(1, s.NX)
        ]

    def last(v):
        b = v % SLOTS
        return [
            remote(part.at[b, 0, 0, d], h.land_z.at[b, s.Z - d - 1], h.z_send.at[b, d - 1],
                   h.z_recv.at[b, s.Z - d - 1], (r, (z + d) % s.Z)) for d in range(1, s.Z)
        ]

    def stage_second(v):
        b = v % SLOTS
        for cp in first(v):
            cp.wait_recv()

        def add(k, carry):
            for dy in range(s.NY):
                total = part[b, dy, 0, k, :half].astype(F32)
                for i in range(s.NX - 1):
                    total = total + h.land_x1[b, i, dy, k].astype(F32)
                part[b, dy, 0, k, :half] = total.astype(BF)
            for dx in range(s.NX):
                total = part[b, 0, dx, k, half:].astype(F32)
                for i in range(s.NY - 1):
                    total = total + h.land_y1[b, i, dx, k].astype(F32)
                part[b, 0, dx, k, half:] = total.astype(BF)
            return carry

        lax.fori_loop(0, s.Z, add, 0)
        for cp in second(v):
            cp.start()

    def stage_last(v):
        b = v % SLOTS
        for cp in second(v):
            cp.wait_recv()

        def add(k, carry):
            total = part[b, 0, 0, k, :half].astype(F32)
            for i in range(s.NY - 1):
                total = total + h.land_y2[b, i, k].astype(F32)
            part[b, 0, 0, k, :half] = total.astype(BF)
            total = part[b, 0, 0, k, half:].astype(F32)
            for i in range(s.NX - 1):
                total = total + h.land_x2[b, i, k].astype(F32)
            part[b, 0, 0, k, half:] = total.astype(BF)
            return carry

        lax.fori_loop(0, s.Z, add, 0)
        for cp in last(v):
            cp.start()

    def out_copy(at, o):
        return pltpu.make_async_copy(h.final.at[o], at, h.out_sem.at[o])

    def stage_out(v):
        b, o = v % SLOTS, v % OUT_RING
        for cp in last(v):
            cp.wait_recv()

        @pl.when(v >= OUT_RING)
        def _():
            out_copy(h.g_mix.at[0], o).wait()

        total = part[b, 0, 0, 0].astype(F32)
        for i in range(s.Z - 1):
            total = total + h.land_z[b, i].astype(F32)
        h.final[o] = total
        l, q = s.L - 1 - v // s.NU, v % s.NU
        wide = 2 * s.NJ
        pl.when((q < wide) & (q % 2 == 0))(lambda: out_copy(h.g_down.at[l, :, lanes(q // 2, s.PC)], o).start())
        pl.when((q < wide) & (q % 2 == 1))(lambda: out_copy(h.g_up.at[l, :, lanes(q // 2, s.PC)], o).start())
        pl.when(q == wide)(lambda: out_copy(h.g_mix.at[l], o).start())
        pl.when(q > wide)(lambda: out_copy(h.g_in.at[l, q - wide - 1], o).start())

    def inside(v, what):
        pl.when((v >= 0) & (v < s.U))(functools.partial(what, v))

    def wait_sends(v):
        for cp in first(v) + second(v) + last(v):
            cp.wait_send()

    def tick(t):
        def start(v):
            for cp in first(v):
                cp.start()

        inside(t, start)
        inside(t - BACK_FIRST, stage_second)
        inside(t - BACK_SECOND, stage_last)
        inside(t - BACK_LAST, stage_out)

    def produce(v, which, own, sibling):
        b = v % SLOTS
        inside(v - SLOTS, wait_sends)
        left = [h.xt[which, i].reshape(s.NQ * s.PR, s.T) for i in range(2)]

        def block(k, carry):
            at = lanes(k, s.PC)
            total = dot(left[0], own[:, at]) + dot(left[1], sibling[:, at])
            part[b, :, :, k] = total.astype(BF).reshape(s.NY, s.NX, s.PR, s.PC)
            return carry

        lax.fori_loop(0, s.Z, block, 0)
        tick(v)

    def drain():
        @pl.loop(s.U, s.U + BACK_LAST)
        def _(t):
            tick(t)

    def settle():
        @pl.loop(s.U - SLOTS, s.U)
        def _(v):
            wait_sends(v)

        for o in range(OUT_RING):
            out_copy(h.g_mix.at[0], o).wait()

    return produce, drain, settle


def bwd_kernel(s, *refs):
    names = BwdIn._fields + BwdOut._fields + tuple(bwd_scratch(s))
    h = types.SimpleNamespace(**dict(zip(names, refs, strict=True)))
    r, z, y, x, c = place(s)
    sibling = (row_at(s, y, x, 1 - c), z)
    greet(s, r, z)
    produce, drain, settle_sums = gradient_sums(s, h, r, z, y, x, c)
    first, _, _ = head_masks(s)
    ones = pair_ones()
    tall = jnp.ones((s.T, 128), BF)
    with_unit = unit_reader(s, h)
    squares = [(dy, dx) for dy in range(s.NY) for dx in range(s.NX)]

    def get(src, dst, index):
        return pltpu.make_async_copy(src, dst, h.get.at[index])

    def xt_loads(l):
        return [
            pltpu.make_async_copy(h.k_normt.at[l, n, i, (y + dy) % s.NY, (x + dx) % s.NX], h.xt.at[n, i, dy, dx],
                                  h.xt_sem.at[n, i, q])
            for n in range(2) for i in range(2) for q, (dy, dx) in enumerate(squares)
        ]

    def xt_sends(l, which):
        return [
            remote(h.turned.at[(y + dy) % s.NY, (x + dx) % s.NX, 1 - c], h.xt.at[which, 1, dy, dx],
                   h.xt_send.at[which - 2, q], h.xt_recv.at[l, which - 2, q], sibling)
            for q, (dy, dx) in enumerate(squares)
        ]

    def turn(l, which):
        wide = h.grad[...]
        h.gb[...] = wide.astype(BF)
        h.turned[...] = wide.T.astype(BF).reshape(s.NY, s.NX, 2, s.PR, s.T)
        for cp in xt_sends(l, which):
            cp.start()
        for dy, dx in squares:
            h.xt[which, 0, dy, dx] = h.turned[(y + dy) % s.NY, (x + dx) % s.NX, c]
        for cp in xt_sends(l, which):
            cp.wait_recv()

    def g_send(l, src, dst, j, index):
        return remote(src.at[j], dst.at[j], h.g_send.at[index], h.g_recv.at[l, index], sibling)

    def norm_back(l, n):
        back = h.acc[...]
        xhat, inv = norm_parts(h.resid[...])
        at = l * 2 + n
        h.vec[pl.ds(at, 1)] = jnp.sum(back * xhat, axis=0, keepdims=True)
        h.vec[pl.ds(2 * s.L + at, 1)] = jnp.sum(back, axis=0, keepdims=True)
        scaled = back * h.gain[pl.ds(at, 1), :]
        mean = jnp.mean(scaled, axis=-1, keepdims=True)
        along = jnp.mean(scaled * xhat, axis=-1, keepdims=True)
        h.grad[...] += inv * (scaled - mean - xhat * along)

    h.grad[...] = h.cotangent[...].astype(F32)
    h.vec[...] = jnp.zeros_like(h.vec)
    h.vec[4 * s.L:4 * s.L + 2, :128] = h.logs[0:2]

    def one_layer(li, carry):
        l = s.L - 1 - li
        base = li * s.NU
        unit = l * s.NU
        loads = [
            get(h.k_qkv.at[l], h.qkv, 0),
            get(h.k_mixed.at[l], h.mixed.at[0], 1),
            get(h.s_mixed.at[l], h.mixed.at[1], 2),
            get(h.k_den.at[l], h.den, 3),
            get(h.k_state.at[l], h.state, 4),
        ]
        act_loads = lambda j: [get(h.k_act.at[l, j], h.act.at[0], 5), get(h.s_act.at[l, j], h.act.at[1], 6)]
        slope_load = lambda j: get(h.k_slope.at[l, j], h.slope, 7)
        for cp in act_loads(0) + [slope_load(0)] + loads + xt_loads(l):
            cp.start()
        turn(l, X_DOWN)
        h.acc[...] = jnp.zeros_like(h.acc)
        for cp in xt_loads(l):
            cp.wait()

        def feed_back(j, carry):
            for cp in act_loads(j):
                cp.wait()
            produce(base + 2 * j, X_DOWN, h.act.at[0], h.act.at[1])

            @pl.when(j + 1 < s.NJ)
            def _():
                for cp in act_loads(j + 1):
                    cp.start()

            slope_load(j).wait()

            def body(k, weight):
                at = lanes(k, s.PC)
                h.ug[j, :, at] = (dot(h.gb[...], weight) * h.slope[:, at].astype(F32)).astype(BF)

            with_unit(h.w_down, l, j, unit + 4 + s.NJ + j, body)

            @pl.when(j + 1 < s.NJ)
            def _():
                slope_load(j + 1).start()

            g_send(l, h.ug, h.ug_sib, j, j).start()

            def body_up(k, weight):
                h.acc[...] += dot(h.ug[j, :, lanes(k, s.PC)], weight, NT)

            with_unit(h.w_up, l, j, unit + 4 + j, body_up)
            g_send(l, h.ug, h.ug_sib, j, j).wait_recv()
            produce(base + 2 * j + 1, X_LATE, h.ug.at[j], h.ug_sib.at[j])
            return carry

        lax.fori_loop(0, s.NJ, feed_back, 0)
        middle = get(h.k_middle.at[l], h.resid, 5)
        middle.start()
        for cp in xt_sends(l, X_DOWN):
            cp.wait_send()
        middle.wait()
        norm_back(l, 1)
        turn(l, X_MIX)
        stream = get(h.k_stream.at[l], h.resid, 5)
        stream.start()

        def body_mix(k, weight):
            h.rg[:, lanes(k, s.PC)] = dot(h.gb[...], weight).astype(BF)

        with_unit(h.w_mix, l, 0, unit + 3, body_mix)
        for cp in loads:
            cp.wait()
        round_one, round_two, round_three, arrive, settle = prefix_rounds(s, h, l, r, z)

        def local_state(k, carry):
            totals = []
            for i in range(s.NP):
                at = lanes(k * s.NP + i, 128)
                query, wide = h.qkv[0, :, at], h.rg[:, at].astype(F32)
                den = h.den[:, at]
                num = (wide / den).astype(BF)
                product = wide * h.mixed[0, :, at].astype(F32)
                high = product.astype(BF)
                low = (product - high.astype(F32)).astype(BF)
                slope = -(dot(high, ones) + dot(low, ones)) / den
                h.ng[:, at] = num
                h.dg[:, at] = slope
                h.msg[k, i * HD:(i + 1) * HD] = pack_state(dot(query, num, TN), first).astype(BF)
                totals.append(jnp.sum(query.astype(F32) * slope, axis=0, keepdims=True))
            h.msg[k, s.NP * HD:] = spread_rows(s, totals).astype(BF)
            return carry

        lax.fori_loop(0, s.Z, local_state, 0)
        round_one()
        produce(base + 2 * s.NJ, X_MIX, h.mixed.at[0], h.mixed.at[1])
        round_two()
        round_three()
        arrive()
        causal = (lax.broadcasted_iota(jnp.int32, (s.T, s.T), 1) <= lax.broadcasted_iota(jnp.int32, (s.T, s.T), 0))
        lane = lax.broadcasted_iota(jnp.int32, (1, 128), 1)

        def attend_back(p, carry):
            k, i = p // s.NP, p % s.NP
            at = lanes(p, 128)
            query, key, value, num = h.qkv[0, :, at], h.qkv[1, :, at], h.qkv[2, :, at], h.ng[:, at]
            slope = h.dg[:, at]
            high = slope.astype(BF)
            low = (slope - high.astype(F32)).astype(BF)
            zero = jnp.zeros_like(query)
            value_ones = jnp.concatenate([value, tall], axis=1)
            rows = pl.ds(pl.multiple_of(i * HD, HD), HD)
            state = unpack_state(h.state[k, rows, :], first)
            after = unpack_state(h.r3[k, rows, :], first)
            total = pick_row(h.state[k, s.NP * HD:, :], i)
            total_after = pick_row(h.r3[k, s.NP * HD:, :], i)
            value_grad = dot(key, after)
            query_grad = dot(num, state, NT) + slope * total
            key_grad = dot(value, after, NT) + total_after
            for head in range(2):
                mine = first if head == 0 else jnp.logical_not(first)
                query_mine = jnp.where(mine, query, zero)
                num_mine = jnp.where(mine, num, zero)
                key_mine = jnp.where(mine, key, zero)
                weights = jnp.where(causal, dot(query_mine, key, NT), 0.0).astype(BF)
                extra = jnp.where(lane == head * HD, high, jnp.where(lane == head * HD + 1, low, zero))
                score = dot(jnp.concatenate([num_mine, extra], axis=1), value_ones, NT)
                score = jnp.where(causal, score, 0.0).astype(BF)
                value_grad = value_grad + dot(weights, num_mine, TN)
                query_grad = query_grad + dot(score, key_mine)
                key_grad = key_grad + dot(score, query_mine, TN)
            h.pg[0, :, at] = (query_grad * jnp.minimum(query.astype(F32), 1.0)).astype(BF)
            h.pg[1, :, at] = (key_grad * jnp.minimum(key.astype(F32), 1.0)).astype(BF)
            h.pg[2, :, at] = value_grad.astype(BF)
            return carry

        lax.fori_loop(0, s.Z * s.NP, attend_back, 0)
        settle()
        for kind in range(3):
            g_send(l, h.pg, h.pg_sib, kind, s.NJ + kind).start()
        h.acc[...] = jnp.zeros_like(h.acc)

        def project_back(kind, carry):
            def body(k, weight):
                h.acc[...] += dot(h.pg[kind, :, lanes(k, s.PC)], weight, NT)

            with_unit(h.w_in, l, kind, unit + kind, body)
            g_send(l, h.pg, h.pg_sib, kind, s.NJ + kind).wait_recv()
            produce(base + 2 * s.NJ + 1 + kind, X_EARLY, h.pg.at[kind], h.pg_sib.at[kind])
            return carry

        lax.fori_loop(0, 3, project_back, 0)
        stream.wait()
        norm_back(l, 0)
        for cp in xt_sends(l, X_MIX):
            cp.wait_send()
        for j in range(s.NJ):
            g_send(l, h.ug, h.ug_sib, j, j).wait_send()
        for kind in range(3):
            g_send(l, h.pg, h.pg_sib, kind, s.NJ + kind).wait_send()
        return carry

    lax.fori_loop(0, s.L, one_layer, 0)

    source = h.vec[...]
    top = lax.broadcasted_iota(jnp.int32, (16, s.D), 0) == 4 * s.L + 1
    stages = (
        (h.v_z, s.Z, z, lambda d: (r, (z + d) % s.Z)),
        (h.v_c, 2, c, lambda d: sibling),
        (h.v_x, s.NX, x, lambda d: (row_at(s, y, (x + d) % s.NX, c), z)),
        (h.v_y, s.NY, y, lambda d: (row_at(s, (y + d) % s.NY, x, c), z)),
    )
    pending = []
    for i, (slots, count, me, peer) in enumerate(stages):
        slots[me] = source
        for d in range(1, count):
            at = slots.at[me]
            cp = remote(at, at, h.v_send.at[i, d], h.v_recv.at[i, count - d], peer(d))
            cp.start()
            pending.append(cp)
        for d in range(1, count):
            at = slots.at[(me + d) % count]
            remote(at, at, h.v_send.at[i, d], h.v_recv.at[i, d], (r, z)).wait_recv()
        total, largest = slots[0], slots[0]
        for k in range(1, count):
            total = total + slots[k]
            largest = jnp.maximum(largest, slots[k])
        source = jnp.where(top, largest, total)
    h.vector[...] = source
    for cp in pending:
        cp.wait_send()
    drain()
    settle_sums()


def unit_reader(s, h):
    def own(kind, l, j):
        if kind is h.w_in:
            src = h.w_in.at[l, j]
        elif kind is h.w_mix:
            src = h.w_mix.at[l]
        else:
            src = kind.at[l, :, :, :, :, lanes(j, s.PC)]
        return pltpu.make_async_copy(src, h.w.at[0], h.w_sem.at[0])

    def load(u, k):
        return pltpu.make_async_copy(h.whole.at[u, k - 1], h.w.at[k], h.w_sem.at[k])

    def with_unit(kind, l, j, u, body, advance=lambda: None):
        own(kind, l, j).start()
        advance()
        for k in range(1, s.Z):
            load(u, k).start()
        own(kind, l, j).wait()
        body(0, h.w[0].reshape(s.D, s.PC))

        @pl.loop(1, s.Z)
        def _(k):
            load(u, k).wait()
            body(k, h.w[k].reshape(s.D, s.PC))

    return with_unit


def backward_call(s, cotangent, kept, gain, coefs, weights):
    vmem = pl.BlockSpec(memory_space=pltpu.VMEM)
    smem = pl.BlockSpec(memory_space=pltpu.SMEM)
    hbm = pl.BlockSpec(memory_space=pl.ANY)
    shape = jax.ShapeDtypeStruct
    outs = [
        shape((s.T, s.D), F32),
        shape((16, s.D), F32),
        shape((s.L, 3, s.PR, s.PC), F32),
        shape((s.L, s.PR, s.PC), F32),
        shape((s.L, s.PR, s.NJ * s.PC), F32),
        shape((s.L, s.PR, s.NJ * s.PC), F32),
    ]
    saved = list(kept[2:])
    out = pl.pallas_call(
        functools.partial(bwd_kernel, s),
        out_shape=outs,
        in_specs=[vmem] * 3 + [smem] * 3 + [hbm] * (4 + len(saved)),
        out_specs=[vmem] * 2 + [hbm] * 4,
        scratch_shapes=list(bwd_scratch(s).values()),
        compiler_params=pltpu.CompilerParams(
            collective_id=1, has_side_effects=True, vmem_limit_bytes=60 * 1024 * 1024),
    )(cotangent, kept.logs, gain, *coefs, *weights, *saved)
    return BwdOut(*out)


def local(mesh, tokens, cotangent, image_length, image_start, norm_gain, norm_bias, weight_in, weight_mix, weight_up,
          weight_down):
    s = sizes_of(mesh, tokens, weight_in, weight_up)
    ahead, behind = coefficients(s, image_length, image_start)
    gain, bias = norm_gain.reshape(-1, s.D), norm_bias.reshape(-1, s.D)
    weights = split_rows(s, weight_in, weight_mix, weight_up, weight_down)
    kept = forward_call(s, tokens, gain, bias, ahead, weights)
    got = backward_call(s, cotangent, kept, gain, behind, weights)
    vector = got.vector
    grad_gain = vector[:2 * s.L].reshape(norm_gain.shape)
    grad_bias = vector[2 * s.L:4 * s.L].reshape(norm_bias.shape)
    heads = s.D // HD
    log_mean = jnp.sum(vector[4 * s.L, :128]) / (HD * s.R * s.Z * s.T * heads * s.L)
    log_max = jnp.max(vector[4 * s.L + 1, :128])
    return (
        kept.output,
        got.grad,
        grad_gain,
        grad_bias,
        grad_bias[s.L - 1, 1],
        jnp.transpose(got.g_in, (0, 2, 1, 3)),
        got.g_mix,
        got.g_up,
        got.g_down,
        log_max,
        log_mean,
    )


def solution(mesh):
    pixels = P(("rows", "feat"), None)
    placed = (pixels, pixels, P(), P(), P(), P(), P(None, None, None, "feat"), P(None, None, "feat"), P(None, None, "feat"),
              P(None, None, "feat"))
    return jax.shard_map(
        functools.partial(local, mesh),
        mesh=mesh,
        in_specs=placed,
        out_specs=(pixels, pixels, P(), P(), P(), P(None, "rows", None, "feat"), P(None, "rows", "feat"),
                   P(None, "rows", "feat"), P(None, "rows", "feat"), P(), P()),
        check_vma=False,
    )
```

```python
import functools
import types
import typing

import jax
import jax.numpy as jnp
from jax import lax
from jax.experimental import pallas as pl
from jax.experimental.pallas import tpu as pltpu
from jax.sharding import PartitionSpec as P

HD = 64
EPS_NORM = 1e-05
EPS_DEN = 1e-06
MESH = pl.DeviceIdType.MESH
BF = jnp.bfloat16
F32 = jnp.float32
LAG_FIRST, LAG_SECOND, LAG_CORE, LAG_READY = 2, 3, 4, 5
RING = 4
ROOT_HALF = 0.7071067811865476
ROOT_TAU = 0.3989422804014327


def sizes_of(mesh, tokens, weight_in, weight_up):
    s = types.SimpleNamespace()
    s.R, s.Z = mesh.shape["rows"], mesh.shape["feat"]
    chips = s.R // 2
    s.NX = 1
    while s.NX * s.NX < chips:
        s.NX *= 2
    s.NY = chips // s.NX
    s.T, s.D = tokens.shape
    s.L = weight_in.shape[0]
    s.PC = weight_in.shape[3]
    s.PR = s.D // s.R
    s.NJ = weight_up.shape[2] // s.PC
    s.NU = 4 + 2 * s.NJ
    s.U = s.L * s.NU
    s.NP = s.PC // 128
    s.MR = s.NP * HD + 16
    s.NQ = s.NY * s.NX
    return s


def place(s):
    r, z = lax.axis_index("rows"), lax.axis_index("feat")
    return r, z, r // (2 * s.NX), (r // 2) % s.NX, r % 2


def row_at(s, y, x, c):
    return (y * s.NX + x) * 2 + c


def greet(s, r, z):
    barrier = pltpu.get_barrier_semaphore()
    peers = [((r + d) % s.R, z) for d in range(1, s.R)] + [(r, (z + d) % s.Z) for d in range(1, s.Z)]
    for peer in peers:
        pl.semaphore_signal(barrier, inc=1, device_id=peer, device_id_type=MESH)
    pl.semaphore_wait(barrier, len(peers))


def remote(src, dst, send, recv, device):
    return pltpu.make_async_remote_copy(
        src_ref=src, dst_ref=dst, send_sem=send, recv_sem=recv, device_id=device, device_id_type=MESH
    )


def dot(a, b, dims=((1,), (0,))):
    return lax.dot_general(a, b, (dims, ((), ())), preferred_element_type=F32)


NT = ((1,), (1,))
TN = ((0,), (0,))


def norm_parts(v):
    center = jnp.mean(v, axis=-1, keepdims=True)
    shifted = v - center
    spread = jnp.mean(shifted * shifted, axis=-1, keepdims=True)
    inv = lax.rsqrt(spread + EPS_NORM)
    return shifted * inv, inv


def weight_gather(s, h, r, z, y, x, c):
    half = s.PR // 2
    F, piece = h.whole, h.piece
    rows = (pl.ds(0, half), pl.ds(half, half))

    def z_copies(u):
        return [
            remote(
                piece.at[u // s.NU, u % s.NU],
                F.at[u, s.Z - d - 1, y, x, c],
                h.z_send.at[u % RING, d - 1],
                h.z_recv.at[u, s.Z - d - 1],
                (r, (z + d) % s.Z),
            )
            for d in range(1, s.Z)
        ]

    def first(u):
        out = []
        for d in range(1, s.NX):
            at = F.at[u, :, y, x, c, rows[0]]
            out.append(remote(at, at, h.x_send.at[u % RING, 0, d - 1], h.x_recv.at[u, 0, s.NX - d - 1],
                              (row_at(s, y, (x + d) % s.NX, c), z)))
        for d in range(1, s.NY):
            at = F.at[u, :, y, x, c, rows[1]]
            out.append(remote(at, at, h.y_send.at[u % RING, 0, d - 1], h.y_recv.at[u, 0, s.NY - d - 1],
                              (row_at(s, (y + d) % s.NY, x, c), z)))
        return out

    def first_landing(u):
        out = []
        for d in range(1, s.NX):
            at = F.at[u, :, y, (x + d) % s.NX, c, rows[0]]
            out.append(remote(at, at, h.x_send.at[u % RING, 0, d - 1], h.x_recv.at[u, 0, d - 1], (r, z)))
        for d in range(1, s.NY):
            at = F.at[u, :, (y + d) % s.NY, x, c, rows[1]]
            out.append(remote(at, at, h.y_send.at[u % RING, 0, d - 1], h.y_recv.at[u, 0, d - 1], (r, z)))
        return out

    def second(u):
        out = []
        for d in range(1, s.NY):
            at = F.at[u, :, y, :, c, rows[0]]
            out.append(remote(at, at, h.y_send.at[u % RING, 1, d - 1], h.y_recv.at[u, 1, s.NY - d - 1],
                              (row_at(s, (y + d) % s.NY, x, c), z)))
        for d in range(1, s.NX):
            at = F.at[u, :, :, x, c, rows[1]]
            out.append(remote(at, at, h.x_send.at[u % RING, 1, d - 1], h.x_recv.at[u, 1, s.NX - d - 1],
                              (row_at(s, y, (x + d) % s.NX, c), z)))
        return out

    def second_landing(u):
        out = []
        for d in range(1, s.NY):
            at = F.at[u, :, (y + d) % s.NY, :, c, rows[0]]
            out.append(remote(at, at, h.y_send.at[u % RING, 1, d - 1], h.y_recv.at[u, 1, d - 1], (r, z)))
        for d in range(1, s.NX):
            at = F.at[u, :, :, (x + d) % s.NX, c, rows[1]]
            out.append(remote(at, at, h.x_send.at[u % RING, 1, d - 1], h.x_recv.at[u, 1, d - 1], (r, z)))
        return out

    def share(u):
        at = F.at[u, :, :, :, c]
        return remote(at, at, h.c_send.at[u % RING], h.c_recv.at[u], (row_at(s, y, x, 1 - c), z))

    def share_landing(u):
        at = F.at[u, :, :, :, 1 - c]
        return remote(at, at, h.c_send.at[u % RING], h.c_recv.at[u], (r, z))

    def z_landing(u):
        return [
            remote(piece.at[0, 0], F.at[u, k, y, x, c], h.z_send.at[u % RING, 0], h.z_recv.at[u, k], (r, z))
            for k in range(s.Z - 1)
        ]

    def inside(u, what):
        pl.when((u >= 0) & (u < s.U))(functools.partial(what, u))

    def stage_z(u):
        for cp in z_copies(u):
            cp.start()

    def stage_first(u):
        for cp in z_landing(u):
            cp.wait_recv()
        for cp in first(u):
            cp.start()

    def stage_second(u):
        for cp in first_landing(u):
            cp.wait_recv()
        for cp in second(u):
            cp.start()

    def stage_core(u):
        for cp in second_landing(u):
            cp.wait_recv()
        share(u).start()

    def stage_ready(u):
        share_landing(u).wait_recv()

    def tick(t):
        inside(t - RING, lambda u: [cp.wait_send() for cp in z_copies(u)] and None)
        inside(t, stage_z)
        inside(t - LAG_FIRST - RING, lambda u: [cp.wait_send() for cp in first(u)] and None)
        inside(t - LAG_FIRST, stage_first)
        inside(t - LAG_SECOND - RING, lambda u: [cp.wait_send() for cp in second(u)] and None)
        inside(t - LAG_SECOND, stage_second)
        inside(t - LAG_CORE - RING, lambda u: share(u).wait_send())
        inside(t - LAG_CORE, stage_core)
        inside(t - LAG_READY, stage_ready)

    def drain_all():
        @pl.loop(s.U + LAG_READY, s.U + LAG_CORE + RING)
        def _(t):
            tick(t)

    return tick, drain_all


def head_masks(s):
    lane = lax.broadcasted_iota(jnp.int32, (1, 128), 1)
    first = lane < HD
    return first, jnp.where(first, 1.0, 0.0), jnp.where(first, 0.0, 1.0)


def pair_ones():
    row = lax.broadcasted_iota(jnp.int32, (128, 128), 0) // HD
    col = lax.broadcasted_iota(jnp.int32, (128, 128), 1) // HD
    return jnp.where(row == col, 1.0, 0.0).astype(BF)


def lanes(at, width):
    return pl.ds(pl.multiple_of(at * width, width), width)


def prefix_rounds(s, h, l, r, z, way):
    at = way * s.L + l
    msg, got, rows_got, back, out = h.msg, h.r1, h.r2, h.pre, h.r3

    def one(k):
        return remote(msg.at[k], got.at[s.Z - k], h.r1_send.at[at, k], h.r1_recv.at[at, s.Z - k], (r, (z + k) % s.Z))

    def two(d):
        return remote(rows_got.at[r], rows_got.at[r], h.r2_send.at[at, d], h.r2_recv.at[at, s.R - d],
                      ((r + d) % s.R, z))

    def two_landing(d):
        spot = rows_got.at[(r + d) % s.R]
        return remote(spot, spot, h.r2_send.at[at, d], h.r2_recv.at[at, d], (r, z))

    def three(k):
        return remote(back.at[k], out.at[s.Z - k], h.r3_send.at[at, k], h.r3_recv.at[at, s.Z - k], (r, (z + k) % s.Z))

    def round_one():
        for k in range(1, s.Z):
            one(k).start()

    def round_two():
        for k in range(1, s.Z):
            remote(msg.at[k], got.at[k], h.r1_send.at[at, k], h.r1_recv.at[at, k], (r, z)).wait_recv()
        total = h.coef_a[way * s.Z] * msg[0].astype(F32)
        for k in range(1, s.Z):
            total = total + h.coef_a[way * s.Z + k] * got[k].astype(F32)
        rows_got[r] = total.astype(BF)
        for d in range(1, s.R):
            two(d).start()

    def round_three():
        for d in range(1, s.R):
            two_landing(d).wait_recv()
        for k in range(s.Z):
            total = h.coef_b[(way * s.Z + k) * s.Z] * msg[0].astype(F32)
            for j in range(1, s.Z):
                total = total + h.coef_b[(way * s.Z + k) * s.Z + j] * got[j].astype(F32)
            for q in range(s.R):
                total = total + h.coef_c[(way * s.Z + k) * s.R + q] * rows_got[q].astype(F32)
            if k == 0:
                out[0] = total.astype(BF)
            else:
                back[k] = total.astype(BF)
                three(k).start()

    def arrive():
        for k in range(1, s.Z):
            remote(back.at[k], out.at[k], h.r3_send.at[at, k], h.r3_recv.at[at, k], (r, z)).wait_recv()

    def settle():
        for k in range(1, s.Z):
            one(k).wait_send()
            three(k).wait_send()
        for d in range(1, s.R):
            two(d).wait_send()

    return round_one, round_two, round_three, arrive, settle


def weigh_kernel(s, length, begin, gain, bias, coef_a, coef_b, coef_c, gain_out, bias_out):
    r, z = lax.axis_index("rows"), lax.axis_index("feat")
    for l in range(s.L):
        gain_out[2 * l:2 * l + 2] = gain[l]
        bias_out[2 * l:2 * l + 2] = bias[l]
    rows = range(s.R)
    turn = [(z + k) % s.Z for k in range(s.Z)]
    spots = [(r * s.Z + k) * s.T for k in turn] + [(r * s.Z + s.Z - 1) * s.T, r * s.Z * s.T]
    spots += [(q * s.Z + s.Z - 1) * s.T for q in rows] + [q * s.Z * s.T for q in rows]

    def count(n, begun):
        start, live = begin[n], jnp.where(length[n] > 0, 1, 0)
        return tuple(v + jnp.where(start <= at, live, 0) for v, at in zip(begun, spots))

    found = lax.fori_loop(0, begin.shape[0], count, tuple(jnp.int32(0) for _ in spots))
    mine, ends, row_ends = found[:s.Z], found[s.Z:s.Z + 2], (found[s.Z + 2:s.Z + 2 + s.R], found[s.Z + 2 + s.R:])
    for way in range(2):
        for k in range(s.Z):
            coef_a[way * s.Z + k] = jnp.where(mine[k] == ends[way], 1.0, 0.0)
            for j in range(s.Z):
                order = turn[j] < turn[k] if way == 0 else turn[j] > turn[k]
                coef_b[(way * s.Z + k) * s.Z + j] = jnp.where((mine[k] == mine[j]) & order, 1.0, 0.0)
            for q in rows:
                order = q < r if way == 0 else q > r
                coef_c[(way * s.Z + k) * s.R + q] = jnp.where((mine[k] == row_ends[way][q]) & order, 1.0, 0.0)


def weigh_units(s, image_length, image_start, gain, bias):
    vmem = pl.BlockSpec(memory_space=pltpu.VMEM)
    smem = pl.BlockSpec(memory_space=pltpu.SMEM)
    shape = jax.ShapeDtypeStruct
    return pl.pallas_call(
        functools.partial(weigh_kernel, s),
        out_shape=[shape((2 * s.Z,), F32), shape((2 * s.Z * s.Z,), F32), shape((2 * s.Z * s.R,), F32),
                   shape((2 * s.L, s.D), F32), shape((2 * s.L, s.D), F32)],
        in_specs=[smem] * 2 + [vmem] * 2,
        out_specs=[smem] * 3 + [vmem] * 2,
    )(image_length, image_start, gain, bias)


def pack_state(full, first):
    return jnp.where(first, full[:HD], full[HD:])


def unpack_state(packed, first):
    zero = jnp.zeros_like(packed)
    return jnp.concatenate([jnp.where(first, packed, zero), jnp.where(first, zero, packed)], axis=0)


def spread_rows(s, rows_list):
    at = lax.broadcasted_iota(jnp.int32, (16, 128), 0)
    block = jnp.zeros((16, 128), F32)
    for i, row in enumerate(rows_list):
        block = block + jnp.where(at == i, row, 0.0)
    return block


def pick_row(block, i):
    at = lax.broadcasted_iota(jnp.int32, (16, 128), 0)
    return jnp.sum(jnp.where(at == i, block.astype(F32), 0.0), axis=0, keepdims=True)


class Inputs(typing.NamedTuple):
    tokens: object
    cotangent: object
    gain: object
    bias: object
    coef_a: object
    coef_b: object
    coef_c: object
    w_in: object
    w_mix: object
    w_up: object
    w_down: object


class Outputs(typing.NamedTuple):
    output: object
    grad: object
    vector: object
    g_in: object
    g_mix: object
    g_up: object
    g_down: object
    whole: object
    k_stream: object
    k_middle: object
    k_qkv: object
    k_mixed: object
    k_den: object
    k_state: object
    k_act: object
    k_slope: object
    k_normt: object
    s_mixed: object
    s_act: object


def forward_scratch(s):
    dma = pltpu.SemaphoreType.DMA
    return dict(
        logs=pltpu.VMEM((8, 128), F32),
        piece=pltpu.VMEM((s.L, s.NU, s.PR, s.PC), BF),
        w=pltpu.VMEM((s.Z, s.NY, s.NX, 2, s.PR, s.PC), BF),
        stream=pltpu.VMEM((s.T, s.D), F32),
        acc=pltpu.VMEM((s.T, s.D), F32),
        middle=pltpu.VMEM((s.T, s.D), F32),
        den=pltpu.VMEM((s.T, s.D), F32),
        nrm=pltpu.VMEM((s.T, s.D), BF),
        nrmt=pltpu.VMEM((2, s.NY, s.NX, 2, s.PR, s.T), BF),
        qkv=pltpu.VMEM((3, s.T, s.D), BF),
        mixed=pltpu.VMEM((s.T, s.D), BF),
        act=pltpu.VMEM((s.NJ, s.T, s.D), BF),
        slope=pltpu.VMEM((s.NJ, s.T, s.D), BF),
        msg=pltpu.VMEM((s.Z, s.MR, 128), BF),
        r1=pltpu.VMEM((s.Z, s.MR, 128), BF),
        r2=pltpu.VMEM((s.R, s.MR, 128), BF),
        pre=pltpu.VMEM((s.Z, s.MR, 128), BF),
        r3=pltpu.VMEM((s.Z, s.MR, 128), BF),
        piece_sem=dma((2 + 2 * s.NJ,)),
        w_sem=dma((s.Z,)),
        z_send=dma((RING, s.Z - 1)),
        z_recv=dma((s.U, s.Z - 1)),
        x_send=dma((RING, 2, s.NX - 1)),
        x_recv=dma((s.U, 2, s.NX - 1)),
        y_send=dma((RING, 2, s.NY - 1)),
        y_recv=dma((s.U, 2, s.NY - 1)),
        c_send=dma((RING,)),
        c_recv=dma((s.U,)),
        r1_send=dma((2 * s.L, s.Z)),
        r1_recv=dma((2 * s.L, s.Z)),
        r2_send=dma((2 * s.L, s.R)),
        r2_recv=dma((2 * s.L, s.R)),
        r3_send=dma((2 * s.L, s.Z)),
        r3_recv=dma((2 * s.L, s.Z)),
        keep=dma((8,)),
        keep_j=dma((2, s.NJ)),
        sib_send=dma((3 + s.NJ,)),
        sib_recv=dma((s.L, 3 + s.NJ)),
    )


def forward_part(s, h, spots, tick, with_unit, early):
    r, z, y, x, c = spots
    sibling = (row_at(s, y, x, 1 - c), z)
    first, _, _ = head_masks(s)

    def normalize(l, n, source):
        xhat, _ = norm_parts(source)
        v = xhat * h.gain[pl.ds(l * 2 + n, 1), :] + h.bias[pl.ds(l * 2 + n, 1), :]
        h.nrm[...] = v.astype(BF)
        h.nrmt[n] = v.T.astype(BF).reshape(s.NY, s.NX, 2, s.PR, s.T)
        keep_norm(l, n).start()
        send_norm(l, n).start()

    def keep_norm(l, n):
        return pltpu.make_async_copy(h.nrmt.at[n, :, :, c], h.k_normt.at[l, n, 0], h.keep.at[n])

    def send_norm(l, n):
        return remote(h.nrmt.at[n, :, :, 1 - c], h.k_normt.at[l, n, 1], h.sib_send.at[n], h.sib_recv.at[l, n],
                      sibling)

    def keep_one(l, index):
        src, dst = ((h.stream, h.k_stream), (h.qkv, h.k_qkv), (h.mixed, h.k_mixed), (h.den, h.k_den),
                    (h.middle, h.k_middle), (h.r3, h.k_state))[index - 2]
        return pltpu.make_async_copy(src, dst.at[l], h.keep.at[index])

    def send_mixed(l):
        return remote(h.mixed, h.s_mixed.at[l], h.sib_send.at[2], h.sib_recv.at[l, 2], sibling)

    def keep_act(l, j):
        return pltpu.make_async_copy(h.act.at[j], h.k_act.at[l, j], h.keep_j.at[0, j])

    def keep_slope(l, j):
        return pltpu.make_async_copy(h.slope.at[j], h.k_slope.at[l, j], h.keep_j.at[1, j])

    def send_act(l, j):
        return remote(h.act.at[j], h.s_act.at[l, j], h.sib_send.at[3 + j], h.sib_recv.at[l, 3 + j], sibling)

    ones = pair_ones()
    tall = jnp.ones((s.T, 128), BF)
    h.logs[...] = jnp.where(lax.broadcasted_iota(jnp.int32, (8, 128), 0) == 1, -jnp.inf, 0.0)
    tick(0)
    tick(1)
    early()
    tick(2)
    h.stream[...] = h.tokens[...].astype(F32)

    @pl.loop(3, LAG_READY)
    def _(t):
        tick(t)

    def one_layer(l, carry):
        base = l * s.NU
        keep_one(l, 2).start()
        normalize(l, 0, h.stream[...])

        def project(kind, carry):
            u = base + kind

            def body(k, weight):
                v = dot(h.nrm[...], weight)
                phi = jnp.where(v > 0, v + 1.0, jnp.exp(jnp.minimum(v, 0.0)))
                h.qkv[kind, :, lanes(k, s.PC)] = jnp.where(kind < 2, phi, v).astype(BF)

            with_unit(h.w_in, l, kind, u, body, lambda: tick(u + LAG_READY))
            return carry

        lax.fori_loop(0, 3, project, 0)
        keep_one(l, 3).start()
        round_one, round_two, round_three, arrive, settle = prefix_rounds(s, h, l, r, z, 0)

        def local_state(k, carry):
            totals = []
            for i in range(s.NP):
                at = lanes(k * s.NP + i, 128)
                keys, vals = h.qkv[1, :, at], h.qkv[2, :, at]
                h.msg[k, i * HD:(i + 1) * HD] = pack_state(dot(keys, vals, TN), first).astype(BF)
                totals.append(jnp.sum(keys.astype(F32), axis=0, keepdims=True))
            h.msg[k, s.NP * HD:] = spread_rows(s, totals).astype(BF)
            return carry

        lax.fori_loop(0, s.Z, local_state, 0)
        round_one()
        tick(base + 3 + LAG_READY)
        round_two()
        tick(base + 4 + LAG_READY)
        round_three()
        tick(base + 5 + LAG_READY)
        arrive()
        keep_one(l, 7).start()
        causal = (lax.broadcasted_iota(jnp.int32, (s.T, s.T), 1) <= lax.broadcasted_iota(jnp.int32, (s.T, s.T), 0))

        def attend(p, carry):
            k, i = p // s.NP, p % s.NP
            at = lanes(p, 128)
            query, key, value = h.qkv[0, :, at], h.qkv[1, :, at], h.qkv[2, :, at]
            wide = query.astype(F32)
            value_ones = jnp.concatenate([value, tall], axis=1)
            zero = jnp.zeros_like(query)
            results = []
            for head in range(2):
                mine = first if head == 0 else jnp.logical_not(first)
                scores = dot(jnp.where(mine, query, zero), key, NT)
                weights = jnp.where(causal, scores, 0.0).astype(BF)
                results.append(dot(weights, value_ones))
            state = unpack_state(h.r3[k, pl.ds(pl.multiple_of(i * HD, HD), HD), :], first)
            total = pick_row(h.r3[k, s.NP * HD:, :], i)
            square = jnp.zeros((128, 128), BF)
            right = jnp.concatenate(
                [jnp.concatenate([state, square], axis=1), jnp.concatenate([square, ones], axis=1)], axis=0)
            left = jnp.concatenate([query, (wide * total).astype(BF)], axis=1)
            earlier = dot(left, right)
            num = jnp.where(first, results[0][:, :128], results[1][:, :128]) + earlier[:, :128]
            den = jnp.where(first, results[0][:, 128:], results[1][:, 128:]) + earlier[:, 128:] + EPS_DEN
            h.mixed[:, at] = (num / den).astype(BF)
            h.den[:, at] = den
            logs = jnp.log(den)
            h.logs[0:1] += jnp.sum(logs, axis=0, keepdims=True)
            h.logs[1:2] = jnp.maximum(h.logs[1:2], jnp.max(logs, axis=0, keepdims=True))
            return carry

        half = s.Z * s.NP // 2
        lax.fori_loop(0, half, attend, 0)
        tick(base + 6 + LAG_READY)
        lax.fori_loop(half, s.Z * s.NP, attend, 0)
        settle()
        keep_one(l, 4).start()
        send_mixed(l).start()
        keep_one(l, 5).start()

        h.acc[...] = jnp.zeros_like(h.acc)

        def mix(k, weight):
            h.acc[...] += dot(h.mixed[:, lanes(k, s.PC)], weight, NT)

        with_unit(h.w_mix, l, 0, base + 3, mix)
        h.middle[...] = h.stream[...] + h.acc[...]
        keep_one(l, 6).start()
        normalize(l, 1, h.middle[...])

        def up(j, carry):
            u = base + 4 + j

            def body(k, weight):
                v = dot(h.nrm[...], weight)
                cdf = 0.5 * (1.0 + lax.erf(v * ROOT_HALF))
                h.act[j, :, lanes(k, s.PC)] = (v * cdf).astype(BF)
                h.slope[j, :, lanes(k, s.PC)] = (cdf + v * (ROOT_TAU * jnp.exp(-0.5 * v * v))).astype(BF)

            with_unit(h.w_up, l, j, u, body, lambda: pl.when(j >= 3)(lambda: tick(u + LAG_READY)))
            keep_act(l, j).start()
            keep_slope(l, j).start()
            send_act(l, j).start()
            return carry

        lax.fori_loop(0, s.NJ, up, 0)
        keep_one(l, 2).wait()
        h.stream[...] = h.middle[...]

        def down(j, carry):
            u = base + 4 + s.NJ + j

            def body(k, weight):
                h.stream[...] += dot(h.act[j, :, lanes(k, s.PC)], weight, NT)

            with_unit(h.w_down, l, j, u, body, lambda: tick(u + LAG_READY))
            return carry

        @pl.when(l + 1 < s.L)
        def _():
            lax.fori_loop(0, s.NJ, down, 0)

        for n in range(2):
            keep_norm(l, n).wait()
            send_norm(l, n).wait_send()
            send_norm(l, n).wait_recv()
        for index in range(3, 8):
            keep_one(l, index).wait()
        send_mixed(l).wait()

        def finish(j, carry):
            keep_act(l, j).wait()
            keep_slope(l, j).wait()
            send_act(l, j).wait()
            return carry

        lax.fori_loop(0, s.NJ, finish, 0)
        return carry

    lax.fori_loop(0, s.L, one_layer, 0)


def split_rows(s, weight_in, *rest):
    cut = (s.NY, s.NX, 2, s.PR)
    turned = jnp.transpose(weight_in, (0, 2, 1, 3)).reshape((s.L, 3) + cut + (s.PC,))
    return (turned,) + tuple(w.reshape((s.L,) + cut + w.shape[2:]) for w in rest)


BACK_FIRST, BACK_SECOND, BACK_LAST = 1, 2, 4
SLOTS = 8
OUT_RING = 4
X_EARLY, X_LATE, X_DOWN, X_MIX = 0, 1, 2, 3

def backward_scratch(s):
    dma = pltpu.SemaphoreType.DMA
    half = s.PR // 2
    return dict(
        part=pltpu.VMEM((SLOTS, s.NY, s.NX, s.Z, s.PR, s.PC), BF),
        land_x1=pltpu.VMEM((SLOTS, s.NX - 1, s.NY, s.Z, half, s.PC), BF),
        land_y1=pltpu.VMEM((SLOTS, s.NY - 1, s.NX, s.Z, half, s.PC), BF),
        land_x2=pltpu.VMEM((SLOTS, s.NX - 1, s.Z, half, s.PC), BF),
        land_y2=pltpu.VMEM((SLOTS, s.NY - 1, s.Z, half, s.PC), BF),
        land_z=pltpu.VMEM((SLOTS, s.Z - 1, s.PR, s.PC), BF),
        final=pltpu.VMEM((OUT_RING, s.PR, s.PC), F32),
        resid=pltpu.VMEM((s.T, s.D), F32),
        gb=pltpu.VMEM((s.T, s.D), BF),
        turned=pltpu.VMEM((s.NY, s.NX, 2, s.PR, s.T), BF),
        xt=pltpu.VMEM((4, 2, s.NY, s.NX, s.PR, s.T), BF),
        b_act=pltpu.VMEM((2, s.T, s.D), BF),
        b_slope=pltpu.VMEM((s.T, s.D), BF),
        ug=pltpu.VMEM((s.NJ, s.T, s.D), BF),
        ug_sib=pltpu.VMEM((s.NJ, s.T, s.D), BF),
        pg=pltpu.VMEM((3, s.T, s.D), BF),
        pg_sib=pltpu.VMEM((3, s.T, s.D), BF),
        b_mixed=pltpu.VMEM((2, s.T, s.D), BF),
        rg=pltpu.VMEM((s.T, s.D), BF),
        ng=pltpu.VMEM((s.T, s.D), BF),
        dg=pltpu.VMEM((s.T, s.D), F32),
        state=pltpu.VMEM((s.Z, s.MR, 128), BF),
        vec=pltpu.VMEM((16, s.D), F32),
        v_z=pltpu.VMEM((s.Z, 16, s.D), F32),
        v_c=pltpu.VMEM((2, 16, s.D), F32),
        v_x=pltpu.VMEM((s.NX, 16, s.D), F32),
        v_y=pltpu.VMEM((s.NY, 16, s.D), F32),
        x1_send=dma((SLOTS, s.NX - 1)),
        x1_recv=dma((SLOTS, s.NX - 1)),
        y1_send=dma((SLOTS, s.NY - 1)),
        y1_recv=dma((SLOTS, s.NY - 1)),
        x2_send=dma((SLOTS, s.NX - 1)),
        x2_recv=dma((SLOTS, s.NX - 1)),
        y2_send=dma((SLOTS, s.NY - 1)),
        y2_recv=dma((SLOTS, s.NY - 1)),
        bz_send=dma((SLOTS, s.Z - 1)),
        bz_recv=dma((SLOTS, s.Z - 1)),
        out_sem=dma((OUT_RING,)),
        xt_sem=dma((2, 2, s.NQ)),
        xt_send=dma((2, s.NQ)),
        xt_recv=dma((s.L, 2, s.NQ)),
        g_send=dma((s.NJ + 3,)),
        g_recv=dma((s.L, s.NJ + 3)),
        get=dma((8,)),
        v_send=dma((4, max(s.Z, s.NX, s.NY))),
        v_recv=dma((4, max(s.Z, s.NX, s.NY))),
    )


def gradient_sums(s, h, r, z, y, x, c):
    half = s.PR // 2
    rows = (pl.ds(0, half), pl.ds(half, half))
    part = h.part

    def to_x(d):
        return (row_at(s, y, (x + d) % s.NX, c), z)

    def to_y(d):
        return (row_at(s, (y + d) % s.NY, x, c), z)

    def first(v):
        b = v % SLOTS
        return [
            remote(part.at[b, :, d, :, rows[0]], h.land_x1.at[b, s.NX - d - 1], h.x1_send.at[b, d - 1],
                   h.x1_recv.at[b, s.NX - d - 1], to_x(d)) for d in range(1, s.NX)
        ] + [
            remote(part.at[b, d, :, :, rows[1]], h.land_y1.at[b, s.NY - d - 1], h.y1_send.at[b, d - 1],
                   h.y1_recv.at[b, s.NY - d - 1], to_y(d)) for d in range(1, s.NY)
        ]

    def second(v):
        b = v % SLOTS
        return [
            remote(part.at[b, d, 0, :, rows[0]], h.land_y2.at[b, s.NY - d - 1], h.y2_send.at[b, d - 1],
                   h.y2_recv.at[b, s.NY - d - 1], to_y(d)) for d in range(1, s.NY)
        ] + [
            remote(part.at[b, 0, d, :, rows[1]], h.land_x2.at[b, s.NX - d - 1], h.x2_send.at[b, d - 1],
                   h.x2_recv.at[b, s.NX - d - 1], to_x(d)) for d in range(1, s.NX)
        ]

    def last(v):
        b = v % SLOTS
        return [
            remote(part.at[b, 0, 0, d], h.land_z.at[b, s.Z - d - 1], h.bz_send.at[b, d - 1],
                   h.bz_recv.at[b, s.Z - d - 1], (r, (z + d) % s.Z)) for d in range(1, s.Z)
        ]

    def stage_second(v):
        b = v % SLOTS
        for cp in first(v):
            cp.wait_recv()

        def add(k, carry):
            for dy in range(s.NY):
                total = part[b, dy, 0, k, :half].astype(F32)
                for i in range(s.NX - 1):
                    total = total + h.land_x1[b, i, dy, k].astype(F32)
                part[b, dy, 0, k, :half] = total.astype(BF)
            for dx in range(s.NX):
                total = part[b, 0, dx, k, half:].astype(F32)
                for i in range(s.NY - 1):
                    total = total + h.land_y1[b, i, dx, k].astype(F32)
                part[b, 0, dx, k, half:] = total.astype(BF)
            return carry

        lax.fori_loop(0, s.Z, add, 0)
        for cp in second(v):
            cp.start()

    def stage_last(v):
        b = v % SLOTS
        for cp in second(v):
            cp.wait_recv()

        def add(k, carry):
            total = part[b, 0, 0, k, :half].astype(F32)
            for i in range(s.NY - 1):
                total = total + h.land_y2[b, i, k].astype(F32)
            part[b, 0, 0, k, :half] = total.astype(BF)
            total = part[b, 0, 0, k, half:].astype(F32)
            for i in range(s.NX - 1):
                total = total + h.land_x2[b, i, k].astype(F32)
            part[b, 0, 0, k, half:] = total.astype(BF)
            return carry

        lax.fori_loop(0, s.Z, add, 0)
        for cp in last(v):
            cp.start()

    def out_copy(at, o):
        return pltpu.make_async_copy(h.final.at[o], at, h.out_sem.at[o])

    def stage_out(v):
        b, o = v % SLOTS, v % OUT_RING
        for cp in last(v):
            cp.wait_recv()

        @pl.when(v >= OUT_RING)
        def _():
            out_copy(h.g_mix.at[0], o).wait()

        total = part[b, 0, 0, 0].astype(F32)
        for i in range(s.Z - 1):
            total = total + h.land_z[b, i].astype(F32)
        h.final[o] = total
        l, q = s.L - 1 - v // s.NU, v % s.NU
        wide = 2 * s.NJ
        pl.when(q < s.NJ)(lambda: out_copy(h.g_down.at[l, :, lanes(q, s.PC)], o).start())
        pl.when((q >= s.NJ) & (q < wide))(lambda: out_copy(h.g_up.at[l, :, lanes(q - s.NJ, s.PC)], o).start())
        pl.when(q == wide)(lambda: out_copy(h.g_mix.at[l], o).start())
        pl.when(q > wide)(lambda: out_copy(h.g_in.at[l, q - wide - 1], o).start())

    def inside(v, what):
        pl.when((v >= 0) & (v < s.U))(functools.partial(what, v))

    def wait_sends(v):
        for cp in first(v) + second(v) + last(v):
            cp.wait_send()

    def tick(t):
        def start(v):
            for cp in first(v):
                cp.start()

        inside(t, start)
        inside(t - BACK_FIRST, stage_second)
        inside(t - BACK_SECOND, stage_last)
        inside(t - BACK_LAST, stage_out)

    def produce(v, which, own, sibling):
        b = v % SLOTS
        inside(v - SLOTS, wait_sends)
        left = [h.xt[which, i].reshape(s.NQ * s.PR, s.T) for i in range(2)]

        def block(k, carry):
            at = lanes(k, s.PC)
            total = dot(left[0], own[:, at]) + dot(left[1], sibling[:, at])
            part[b, :, :, k] = total.astype(BF).reshape(s.NY, s.NX, s.PR, s.PC)
            return carry

        lax.fori_loop(0, s.Z, block, 0)
        tick(v)

    def drain():
        @pl.loop(s.U + 4, s.U + max(BACK_LAST + 1, 4))
        def _(t):
            tick(t)

    def settle():
        @pl.loop(s.U - SLOTS, s.U)
        def _(v):
            wait_sends(v)

        for o in range(OUT_RING):
            out_copy(h.g_mix.at[0], o).wait()

    return produce, tick, drain, settle


def backward_part(s, h, spots, tick_weights, with_unit, sums):
    r, z, y, x, c = spots
    produce, tick, drain, settle_sums = sums
    sibling = (row_at(s, y, x, 1 - c), z)
    first, _, _ = head_masks(s)
    ones = pair_ones()
    tall = jnp.ones((s.T, 128), BF)
    squares = [(dy, dx) for dy in range(s.NY) for dx in range(s.NX)]

    def get(src, dst, index):
        return pltpu.make_async_copy(src, dst, h.get.at[index])

    def xt_loads(l):
        return [
            pltpu.make_async_copy(h.k_normt.at[l, n, i, (y + dy) % s.NY, (x + dx) % s.NX], h.xt.at[n, i, dy, dx],
                                  h.xt_sem.at[n, i, q])
            for n in range(2) for i in range(2) for q, (dy, dx) in enumerate(squares)
        ]

    def xt_sends(l, which):
        return [
            remote(h.turned.at[(y + dy) % s.NY, (x + dx) % s.NX, 1 - c], h.xt.at[which, 1, dy, dx],
                   h.xt_send.at[which - 2, q], h.xt_recv.at[l, which - 2, q], sibling)
            for q, (dy, dx) in enumerate(squares)
        ]

    def turn(l, which):
        wide = h.grad[...]
        h.gb[...] = wide.astype(BF)
        h.turned[...] = wide.T.astype(BF).reshape(s.NY, s.NX, 2, s.PR, s.T)
        for cp in xt_sends(l, which):
            cp.start()
        for dy, dx in squares:
            h.xt[which, 0, dy, dx] = h.turned[(y + dy) % s.NY, (x + dx) % s.NX, c]
    def g_send(l, src, dst, j, index):
        return remote(src.at[j], dst.at[j], h.g_send.at[index], h.g_recv.at[l, index], sibling)

    def norm_back(l, n):
        back = h.acc[...]
        xhat, inv = norm_parts(h.resid[...])
        at = l * 2 + n
        h.vec[pl.ds(at, 1)] = jnp.sum(back * xhat, axis=0, keepdims=True)
        h.vec[pl.ds(2 * s.L + at, 1)] = jnp.sum(back, axis=0, keepdims=True)
        scaled = back * h.gain[pl.ds(l * 2 + n, 1), :]
        mean = jnp.mean(scaled, axis=-1, keepdims=True)
        along = jnp.mean(scaled * xhat, axis=-1, keepdims=True)
        h.grad[...] += inv * (scaled - mean - xhat * along)

    def early():
        h.grad[...] = h.cotangent[...].astype(F32)
        turn(s.L - 1, X_DOWN)

    def one_layer(li, carry):
        l = s.L - 1 - li
        base = li * s.NU
        unit = l * s.NU
        loads = [
            get(h.k_qkv.at[l], h.qkv, 0),
            get(h.k_mixed.at[l], h.b_mixed.at[0], 1),
            get(h.s_mixed.at[l], h.b_mixed.at[1], 2),
            get(h.k_den.at[l], h.den, 3),
            get(h.k_state.at[l], h.state, 4),
        ]
        act_loads = lambda j: [get(h.k_act.at[l, j], h.b_act.at[0], 5), get(h.s_act.at[l, j], h.b_act.at[1], 6)]
        slope_load = lambda j: get(h.k_slope.at[l, j], h.b_slope, 7)
        for cp in act_loads(0) + [slope_load(0)] + loads + xt_loads(l):
            cp.start()
        h.acc[...] = jnp.zeros_like(h.acc)
        for cp in xt_loads(l):
            cp.wait()
        for cp in xt_sends(l, X_DOWN):
            cp.wait_recv()

        def feed_back(j, carry):
            for cp in act_loads(j):
                cp.wait()
            produce(base + j, X_DOWN, h.b_act.at[0], h.b_act.at[1])
            slope_load(j).wait()

            def body(k, weight):
                at = lanes(k, s.PC)
                h.ug[j, :, at] = (dot(h.gb[...], weight) * h.b_slope[:, at].astype(F32)).astype(BF)

                @pl.when(li == 0)
                def _():
                    h.stream[...] += dot(h.b_act[0, :, at], weight, NT)

            u = unit + 4 + s.NJ + j
            with_unit(h.w_down, l, j, u, body, lambda: pl.when(li == 0)(lambda: tick_weights(u + LAG_READY)))

            @pl.when(j + 1 < s.NJ)
            def _():
                for cp in act_loads(j + 1):
                    cp.start()


            @pl.when(j + 1 < s.NJ)
            def _():
                slope_load(j + 1).start()

            g_send(l, h.ug, h.ug_sib, j, j).start()

            def body_up(k, weight):
                h.acc[...] += dot(h.ug[j, :, lanes(k, s.PC)], weight, NT)

            with_unit(h.w_up, l, j, unit + 4 + j, body_up)
            return carry

        def produce_up(j):
            g_send(l, h.ug, h.ug_sib, j, j).wait_recv()
            produce(base + s.NJ + j, X_LATE, h.ug.at[j], h.ug_sib.at[j])

        lax.fori_loop(0, s.NJ, feed_back, 0)
        produce_up(0)
        middle = get(h.k_middle.at[l], h.resid, 5)
        middle.start()
        for cp in xt_sends(l, X_DOWN):
            cp.wait_send()
        middle.wait()
        norm_back(l, 1)
        turn(l, X_MIX)
        for cp in xt_sends(l, X_MIX):
            cp.wait_recv()
        stream = get(h.k_stream.at[l], h.resid, 5)
        stream.start()

        def body_mix(k, weight):
            h.rg[:, lanes(k, s.PC)] = dot(h.gb[...], weight).astype(BF)

        with_unit(h.w_mix, l, 0, unit + 3, body_mix)
        for cp in loads:
            cp.wait()
        round_one, round_two, round_three, arrive, settle = prefix_rounds(s, h, l, r, z, 1)

        def local_state(k, carry):
            totals = []
            for i in range(s.NP):
                at = lanes(k * s.NP + i, 128)
                query, wide = h.qkv[0, :, at], h.rg[:, at].astype(F32)
                den = h.den[:, at]
                num = (wide / den).astype(BF)
                product = wide * h.b_mixed[0, :, at].astype(F32)
                high = product.astype(BF)
                low = (product - high.astype(F32)).astype(BF)
                slope = -(dot(high, ones) + dot(low, ones)) / den
                h.ng[:, at] = num
                h.dg[:, at] = slope
                h.msg[k, i * HD:(i + 1) * HD] = pack_state(dot(query, num, TN), first).astype(BF)
                totals.append(jnp.sum(query.astype(F32) * slope, axis=0, keepdims=True))
            h.msg[k, s.NP * HD:] = spread_rows(s, totals).astype(BF)
            return carry

        lax.fori_loop(0, s.Z, local_state, 0)
        round_one()
        produce_up(1)
        round_two()
        produce_up(2)
        round_three()
        lax.fori_loop(3, s.NJ, lambda j, carry: (produce_up(j), carry)[1], 0)
        arrive()
        causal = (lax.broadcasted_iota(jnp.int32, (s.T, s.T), 1) <= lax.broadcasted_iota(jnp.int32, (s.T, s.T), 0))
        lane = lax.broadcasted_iota(jnp.int32, (1, 128), 1)

        def attend_back(p, carry):
            k, i = p // s.NP, p % s.NP
            at = lanes(p, 128)
            query, key, value, num = h.qkv[0, :, at], h.qkv[1, :, at], h.qkv[2, :, at], h.ng[:, at]
            slope = h.dg[:, at]
            high = slope.astype(BF)
            low = (slope - high.astype(F32)).astype(BF)
            zero = jnp.zeros_like(query)
            value_ones = jnp.concatenate([value, tall], axis=1)
            rows = pl.ds(pl.multiple_of(i * HD, HD), HD)
            state = unpack_state(h.state[k, rows, :], first)
            after = unpack_state(h.r3[k, rows, :], first)
            total = pick_row(h.state[k, s.NP * HD:, :], i)
            total_after = pick_row(h.r3[k, s.NP * HD:, :], i)
            value_grad = dot(key, after)
            query_grad = dot(num, state, NT) + slope * total
            key_grad = dot(value, after, NT) + total_after
            for head in range(2):
                mine = first if head == 0 else jnp.logical_not(first)
                query_mine = jnp.where(mine, query, zero)
                num_mine = jnp.where(mine, num, zero)
                key_mine = jnp.where(mine, key, zero)
                weights = jnp.where(causal, dot(query_mine, key, NT), 0.0).astype(BF)
                extra = jnp.where(lane == head * HD, high, jnp.where(lane == head * HD + 1, low, zero))
                score = dot(jnp.concatenate([num_mine, extra], axis=1), value_ones, NT)
                score = jnp.where(causal, score, 0.0).astype(BF)
                value_grad = value_grad + dot(weights, num_mine, TN)
                query_grad = query_grad + dot(score, key_mine)
                key_grad = key_grad + dot(score, query_mine, TN)
            h.pg[0, :, at] = (query_grad * jnp.minimum(query.astype(F32), 1.0)).astype(BF)
            h.pg[1, :, at] = (key_grad * jnp.minimum(key.astype(F32), 1.0)).astype(BF)
            h.pg[2, :, at] = value_grad.astype(BF)
            return carry

        half = s.Z * s.NP // 2
        lax.fori_loop(0, half, attend_back, 0)
        produce(base + 2 * s.NJ, X_MIX, h.b_mixed.at[0], h.b_mixed.at[1])
        lax.fori_loop(half, s.Z * s.NP, attend_back, 0)
        settle()
        for kind in range(3):
            g_send(l, h.pg, h.pg_sib, kind, s.NJ + kind).start()
        h.acc[...] = jnp.zeros_like(h.acc)

        def project_back(kind, carry):
            def body(k, weight):
                h.acc[...] += dot(h.pg[kind, :, lanes(k, s.PC)], weight, NT)

            with_unit(h.w_in, l, kind, unit + kind, body)
            g_send(l, h.pg, h.pg_sib, kind, s.NJ + kind).wait_recv()
            produce(base + 2 * s.NJ + 1 + kind, X_EARLY, h.pg.at[kind], h.pg_sib.at[kind])
            return carry

        lax.fori_loop(0, 3, project_back, 0)
        stream.wait()
        norm_back(l, 0)
        for cp in xt_sends(l, X_MIX):
            cp.wait_send()
        for j in range(s.NJ):
            g_send(l, h.ug, h.ug_sib, j, j).wait_send()
        for kind in range(3):
            g_send(l, h.pg, h.pg_sib, kind, s.NJ + kind).wait_send()

        @pl.when(li + 1 < s.L)
        def _():
            turn(l - 1, X_DOWN)

        return carry

    def run():
        lax.fori_loop(0, s.L, one_layer, 0)
        finish()

    def finish():
        h.vec[4 * s.L:4 * s.L + 2, :128] = h.logs[0:2]
        source = h.vec[...]
        top = lax.broadcasted_iota(jnp.int32, (16, s.D), 0) == 4 * s.L + 1
        stages = (
            (h.v_z, s.Z, z, lambda d: (r, (z + d) % s.Z)),
            (h.v_c, 2, c, lambda d: sibling),
            (h.v_x, s.NX, x, lambda d: (row_at(s, y, (x + d) % s.NX, c), z)),
            (h.v_y, s.NY, y, lambda d: (row_at(s, (y + d) % s.NY, x, c), z)),
        )
        pending = []
        for i, (slots, count, me, peer) in enumerate(stages):
            slots[me] = source
            for d in range(1, count):
                at = slots.at[me]
                cp = remote(at, at, h.v_send.at[i, d], h.v_recv.at[i, count - d], peer(d))
                cp.start()
                pending.append(cp)
            tick(s.U + i)
            for d in range(1, count):
                at = slots.at[(me + d) % count]
                remote(at, at, h.v_send.at[i, d], h.v_recv.at[i, d], (r, z)).wait_recv()
            total, largest = slots[0], slots[0]
            for k in range(1, count):
                total = total + slots[k]
                largest = jnp.maximum(largest, slots[k])
            source = jnp.where(top, largest, total)
        h.vector[...] = source
        for cp in pending:
            cp.wait_send()
        drain()
        settle_sums()

    return early, run


def unit_reader(s, h):
    def own(kind, l, j):
        if kind is h.w_in:
            src = h.w_in.at[l, j]
        elif kind is h.w_mix:
            src = h.w_mix.at[l]
        else:
            src = kind.at[l, :, :, :, :, lanes(j, s.PC)]
        return pltpu.make_async_copy(src, h.w.at[0], h.w_sem.at[0])

    def load(u, k):
        return pltpu.make_async_copy(h.whole.at[u, k - 1], h.w.at[k], h.w_sem.at[k])

    def with_unit(kind, l, j, u, body, advance=lambda: None):
        own(kind, l, j).start()
        advance()
        for k in range(1, s.Z):
            load(u, k).start()
        own(kind, l, j).wait()
        body(0, h.w[0].reshape(s.D, s.PC))

        @pl.loop(1, s.Z)
        def _(k):
            load(u, k).wait()
            body(k, h.w[k].reshape(s.D, s.PC))

    return with_unit


def kernel(s, *refs):
    scratch = forward_scratch(s) | backward_scratch(s)
    names = Inputs._fields + Outputs._fields + tuple(scratch)
    h = types.SimpleNamespace(**dict(zip(names, refs, strict=True)))
    spots = r, z, y, x, c = place(s)
    pieces = [
        pltpu.make_async_copy(h.w_in.at[:, :, y, x, c], h.piece.at[:, 0:3], h.piece_sem.at[0]),
        pltpu.make_async_copy(h.w_mix.at[:, y, x, c], h.piece.at[:, 3], h.piece_sem.at[1]),
    ]
    for j in range(s.NJ):
        cols = pl.ds(j * s.PC, s.PC)
        pieces.append(pltpu.make_async_copy(h.w_up.at[:, y, x, c, :, cols], h.piece.at[:, 4 + j], h.piece_sem.at[2 + j]))
        pieces.append(pltpu.make_async_copy(h.w_down.at[:, y, x, c, :, cols], h.piece.at[:, 4 + s.NJ + j],
                                            h.piece_sem.at[2 + s.NJ + j]))
    for cp in pieces:
        cp.start()
    greet(s, r, z)
    for cp in pieces:
        cp.wait()
    tick_weights, drain_weights = weight_gather(s, h, r, z, y, x, c)
    with_unit = unit_reader(s, h)
    sums = gradient_sums(s, h, r, z, y, x, c)
    early, backward = backward_part(s, h, spots, tick_weights, with_unit, sums)

    def before():
        h.vec[...] = jnp.zeros_like(h.vec)
        early()

    forward_part(s, h, spots, tick_weights, with_unit, before)
    backward()
    h.output[...] = h.stream[...].astype(BF)
    drain_weights()


def call(s, arrays):
    vmem = pl.BlockSpec(memory_space=pltpu.VMEM)
    smem = pl.BlockSpec(memory_space=pltpu.SMEM)
    hbm = pl.BlockSpec(memory_space=pl.ANY)
    shape = jax.ShapeDtypeStruct
    outs = Outputs(
        output=shape((s.T, s.D), BF),
        grad=shape((s.T, s.D), F32),
        vector=shape((16, s.D), F32),
        g_in=shape((s.L, 3, s.PR, s.PC), F32),
        g_mix=shape((s.L, s.PR, s.PC), F32),
        g_up=shape((s.L, s.PR, s.NJ * s.PC), F32),
        g_down=shape((s.L, s.PR, s.NJ * s.PC), F32),
        whole=shape((s.U, s.Z - 1, s.NY, s.NX, 2, s.PR, s.PC), BF),
        k_stream=shape((s.L, s.T, s.D), F32),
        k_middle=shape((s.L, s.T, s.D), F32),
        k_qkv=shape((s.L, 3, s.T, s.D), BF),
        k_mixed=shape((s.L, s.T, s.D), BF),
        k_den=shape((s.L, s.T, s.D), F32),
        k_state=shape((s.L, s.Z, s.MR, 128), BF),
        k_act=shape((s.L, s.NJ, s.T, s.D), BF),
        k_slope=shape((s.L, s.NJ, s.T, s.D), BF),
        k_normt=shape((s.L, 2, 2, s.NY, s.NX, s.PR, s.T), BF),
        s_mixed=shape((s.L, s.T, s.D), BF),
        s_act=shape((s.L, s.NJ, s.T, s.D), BF),
    )
    scratch = forward_scratch(s) | backward_scratch(s)
    out = pl.pallas_call(
        functools.partial(kernel, s),
        out_shape=list(outs),
        in_specs=[vmem] * 4 + [smem] * 3 + [hbm] * 4,
        out_specs=[vmem] * 3 + [hbm] * (len(outs) - 3),
        scratch_shapes=list(scratch.values()),
        compiler_params=pltpu.CompilerParams(
            collective_id=0, has_side_effects=True, vmem_limit_bytes=61 * 1024 * 1024),
    )(*arrays)
    return Outputs(*out)


def local(mesh, tokens, cotangent, image_length, image_start, norm_gain, norm_bias, weight_in, weight_mix, weight_up,
          weight_down):
    s = sizes_of(mesh, tokens, weight_in, weight_up)
    weights = split_rows(s, weight_in, weight_mix, weight_up, weight_down)
    *coefs, gain, bias = weigh_units(s, image_length, image_start, norm_gain, norm_bias)
    got = call(s, Inputs(tokens, cotangent, gain, bias, *coefs, *weights))
    vector = got.vector
    grad_gain = vector[:2 * s.L].reshape(norm_gain.shape)
    grad_bias = vector[2 * s.L:4 * s.L].reshape(norm_bias.shape)
    heads = s.D // HD
    log_mean = jnp.sum(vector[4 * s.L, :128]) / (HD * s.R * s.Z * s.T * heads * s.L)
    log_max = jnp.max(vector[4 * s.L + 1, :128])
    return (
        got.output,
        got.grad,
        grad_gain,
        grad_bias,
        grad_bias[s.L - 1, 1],
        jnp.transpose(got.g_in, (0, 2, 1, 3)),
        got.g_mix,
        got.g_up,
        got.g_down,
        log_max,
        log_mean,
    )


def solution(mesh):
    pixels = P(("rows", "feat"), None)
    placed = (pixels, pixels, P(), P(), P(), P(), P(None, None, None, "feat"), P(None, None, "feat"), P(None, None, "feat"),
              P(None, None, "feat"))
    return jax.shard_map(
        functools.partial(local, mesh),
        mesh=mesh,
        in_specs=placed,
        out_specs=(pixels, pixels, P(), P(), P(), P(None, "rows", None, "feat"), P(None, "rows", "feat"),
                   P(None, "rows", "feat"), P(None, "rows", "feat"), P(), P()),
        check_vma=False,
    )
```

```python
import functools
import types
import typing

import jax
import jax.numpy as jnp
from jax import lax
from jax.experimental import pallas as pl
from jax.experimental.pallas import tpu as pltpu
from jax.sharding import PartitionSpec as P

HD = 64
EPS_NORM = 1e-05
EPS_DEN = 1e-06
MESH = pl.DeviceIdType.MESH
BF = jnp.bfloat16
F32 = jnp.float32
LAG_FIRST, LAG_SECOND, LAG_CORE, LAG_READY = 2, 3, 4, 5
RING = 4
ROOT_HALF = 0.7071067811865476
ROOT_TAU = 0.3989422804014327


def sizes_of(mesh, tokens, weight_in, weight_up):
    s = types.SimpleNamespace()
    s.R, s.Z = mesh.shape["rows"], mesh.shape["feat"]
    chips = s.R // 2
    s.NX = 1
    while s.NX * s.NX < chips:
        s.NX *= 2
    s.NY = chips // s.NX
    s.T, s.D = tokens.shape
    s.L = weight_in.shape[0]
    s.PC = weight_in.shape[3]
    s.PR = s.D // s.R
    s.NJ = weight_up.shape[2] // s.PC
    s.NU = 4 + 2 * s.NJ
    s.U = s.L * s.NU
    s.NP = s.PC // 128
    s.MR = s.NP * HD + 16
    s.NQ = s.NY * s.NX
    return s


def place(s):
    r, z = lax.axis_index("rows"), lax.axis_index("feat")
    return r, z, r // (2 * s.NX), (r // 2) % s.NX, r % 2


def row_at(s, y, x, c):
    return (y * s.NX + x) * 2 + c


def greet(s, r, z):
    barrier = pltpu.get_barrier_semaphore()
    peers = [((r + d) % s.R, z) for d in range(1, s.R)] + [(r, (z + d) % s.Z) for d in range(1, s.Z)]
    for peer in peers:
        pl.semaphore_signal(barrier, inc=1, device_id=peer, device_id_type=MESH)
    pl.semaphore_wait(barrier, len(peers))


def remote(src, dst, send, recv, device):
    return pltpu.make_async_remote_copy(
        src_ref=src, dst_ref=dst, send_sem=send, recv_sem=recv, device_id=device, device_id_type=MESH
    )


def dot(a, b, dims=((1,), (0,))):
    return lax.dot_general(a, b, (dims, ((), ())), preferred_element_type=F32)


NT = ((1,), (1,))
TN = ((0,), (0,))


def norm_parts(v):
    center = jnp.mean(v, axis=-1, keepdims=True)
    shifted = v - center
    spread = jnp.mean(shifted * shifted, axis=-1, keepdims=True)
    inv = lax.rsqrt(spread + EPS_NORM)
    return shifted * inv, inv


def weight_gather(s, h, r, z, y, x, c):
    half = s.PR // 2
    F, piece = h.whole, h.piece
    rows = (pl.ds(0, half), pl.ds(half, half))

    def z_copies(u):
        return [
            remote(
                piece.at[u // s.NU, u % s.NU],
                F.at[u, s.Z - d - 1, y, x, c],
                h.z_send.at[u % RING, d - 1],
                h.z_recv.at[u, s.Z - d - 1],
                (r, (z + d) % s.Z),
            )
            for d in range(1, s.Z)
        ]

    def first(u):
        out = []
        for d in range(1, s.NX):
            at = F.at[u, :, y, x, c, rows[0]]
            out.append(remote(at, at, h.x_send.at[u % RING, 0, d - 1], h.x_recv.at[u, 0, s.NX - d - 1],
                              (row_at(s, y, (x + d) % s.NX, c), z)))
        for d in range(1, s.NY):
            at = F.at[u, :, y, x, c, rows[1]]
            out.append(remote(at, at, h.y_send.at[u % RING, 0, d - 1], h.y_recv.at[u, 0, s.NY - d - 1],
                              (row_at(s, (y + d) % s.NY, x, c), z)))
        return out

    def first_landing(u):
        out = []
        for d in range(1, s.NX):
            at = F.at[u, :, y, (x + d) % s.NX, c, rows[0]]
            out.append(remote(at, at, h.x_send.at[u % RING, 0, d - 1], h.x_recv.at[u, 0, d - 1], (r, z)))
        for d in range(1, s.NY):
            at = F.at[u, :, (y + d) % s.NY, x, c, rows[1]]
            out.append(remote(at, at, h.y_send.at[u % RING, 0, d - 1], h.y_recv.at[u, 0, d - 1], (r, z)))
        return out

    def second(u):
        out = []
        for d in range(1, s.NY):
            at = F.at[u, :, y, :, c, rows[0]]
            out.append(remote(at, at, h.y_send.at[u % RING, 1, d - 1], h.y_recv.at[u, 1, s.NY - d - 1],
                              (row_at(s, (y + d) % s.NY, x, c), z)))
        for d in range(1, s.NX):
            at = F.at[u, :, :, x, c, rows[1]]
            out.append(remote(at, at, h.x_send.at[u % RING, 1, d - 1], h.x_recv.at[u, 1, s.NX - d - 1],
                              (row_at(s, y, (x + d) % s.NX, c), z)))
        return out

    def second_landing(u):
        out = []
        for d in range(1, s.NY):
            at = F.at[u, :, (y + d) % s.NY, :, c, rows[0]]
            out.append(remote(at, at, h.y_send.at[u % RING, 1, d - 1], h.y_recv.at[u, 1, d - 1], (r, z)))
        for d in range(1, s.NX):
            at = F.at[u, :, :, (x + d) % s.NX, c, rows[1]]
            out.append(remote(at, at, h.x_send.at[u % RING, 1, d - 1], h.x_recv.at[u, 1, d - 1], (r, z)))
        return out

    def share(u):
        at = F.at[u, :, :, :, c]
        return remote(at, at, h.c_send.at[u % RING], h.c_recv.at[u], (row_at(s, y, x, 1 - c), z))

    def share_landing(u):
        at = F.at[u, :, :, :, 1 - c]
        return remote(at, at, h.c_send.at[u % RING], h.c_recv.at[u], (r, z))

    def z_landing(u):
        return [
            remote(piece.at[0, 0], F.at[u, k, y, x, c], h.z_send.at[u % RING, 0], h.z_recv.at[u, k], (r, z))
            for k in range(s.Z - 1)
        ]

    def inside(u, what):
        pl.when((u >= 0) & (u < s.U))(functools.partial(what, u))

    def stage_z(u):
        for cp in z_copies(u):
            cp.start()

    def stage_first(u):
        for cp in z_landing(u):
            cp.wait_recv()
        for cp in first(u):
            cp.start()

    def stage_second(u):
        for cp in first_landing(u):
            cp.wait_recv()
        for cp in second(u):
            cp.start()

    def stage_core(u):
        for cp in second_landing(u):
            cp.wait_recv()
        share(u).start()

    def stage_ready(u):
        share_landing(u).wait_recv()

    def tick(t):
        inside(t - RING, lambda u: [cp.wait_send() for cp in z_copies(u)] and None)
        inside(t, stage_z)
        inside(t - LAG_FIRST - RING, lambda u: [cp.wait_send() for cp in first(u)] and None)
        inside(t - LAG_FIRST, stage_first)
        inside(t - LAG_SECOND - RING, lambda u: [cp.wait_send() for cp in second(u)] and None)
        inside(t - LAG_SECOND, stage_second)
        inside(t - LAG_CORE - RING, lambda u: share(u).wait_send())
        inside(t - LAG_CORE, stage_core)
        inside(t - LAG_READY, stage_ready)

    def drain_all():
        @pl.loop(s.U + LAG_READY, s.U + LAG_CORE + RING)
        def _(t):
            tick(t)

    return tick, drain_all


def head_masks(s):
    lane = lax.broadcasted_iota(jnp.int32, (1, 128), 1)
    first = lane < HD
    return first, jnp.where(first, 1.0, 0.0), jnp.where(first, 0.0, 1.0)


def pair_ones():
    row = lax.broadcasted_iota(jnp.int32, (128, 128), 0) // HD
    col = lax.broadcasted_iota(jnp.int32, (128, 128), 1) // HD
    return jnp.where(row == col, 1.0, 0.0).astype(BF)


def lanes(at, width):
    return pl.ds(pl.multiple_of(at * width, width), width)


def prefix_rounds(s, h, l, r, z, way):
    at = way * s.L + l
    msg, got, rows_got, back, out = h.msg, h.r1, h.r2, h.pre, h.r3

    def one(k):
        return remote(msg.at[k], got.at[s.Z - k], h.r1_send.at[at, k], h.r1_recv.at[at, s.Z - k], (r, (z + k) % s.Z))

    def two(d):
        return remote(rows_got.at[r], rows_got.at[r], h.r2_send.at[at, d], h.r2_recv.at[at, s.R - d],
                      ((r + d) % s.R, z))

    def two_landing(d):
        spot = rows_got.at[(r + d) % s.R]
        return remote(spot, spot, h.r2_send.at[at, d], h.r2_recv.at[at, d], (r, z))

    def three(k):
        return remote(back.at[k], out.at[s.Z - k], h.r3_send.at[at, k], h.r3_recv.at[at, s.Z - k], (r, (z + k) % s.Z))

    def round_one():
        for k in range(1, s.Z):
            one(k).start()

    def round_two():
        for k in range(1, s.Z):
            remote(msg.at[k], got.at[k], h.r1_send.at[at, k], h.r1_recv.at[at, k], (r, z)).wait_recv()
        total = h.coef_a[way * s.Z] * msg[0].astype(F32)
        for k in range(1, s.Z):
            total = total + h.coef_a[way * s.Z + k] * got[k].astype(F32)
        rows_got[r] = total.astype(BF)
        for d in range(1, s.R):
            two(d).start()

    def round_three():
        for d in range(1, s.R):
            two_landing(d).wait_recv()
        for k in range(s.Z):
            total = h.coef_b[(way * s.Z + k) * s.Z] * msg[0].astype(F32)
            for j in range(1, s.Z):
                total = total + h.coef_b[(way * s.Z + k) * s.Z + j] * got[j].astype(F32)
            for q in range(s.R):
                total = total + h.coef_c[(way * s.Z + k) * s.R + q] * rows_got[q].astype(F32)
            if k == 0:
                out[0] = total.astype(BF)
            else:
                back[k] = total.astype(BF)
                three(k).start()

    def arrive():
        for k in range(1, s.Z):
            remote(back.at[k], out.at[k], h.r3_send.at[at, k], h.r3_recv.at[at, k], (r, z)).wait_recv()

    def settle():
        for k in range(1, s.Z):
            one(k).wait_send()
            three(k).wait_send()
        for d in range(1, s.R):
            two(d).wait_send()

    return round_one, round_two, round_three, arrive, settle


def weigh_kernel(s, length, begin, gain, bias, coef_a, coef_b, coef_c, gain_out, bias_out):
    r, z = lax.axis_index("rows"), lax.axis_index("feat")
    for l in range(s.L):
        gain_out[2 * l:2 * l + 2] = gain[l]
        bias_out[2 * l:2 * l + 2] = bias[l]
    rows = range(s.R)
    turn = [(z + k) % s.Z for k in range(s.Z)]
    spots = [(r * s.Z + k) * s.T for k in turn] + [(r * s.Z + s.Z - 1) * s.T, r * s.Z * s.T]
    spots += [(q * s.Z + s.Z - 1) * s.T for q in rows] + [q * s.Z * s.T for q in rows]

    def count(n, begun):
        start, live = begin[n], jnp.where(length[n] > 0, 1, 0)
        return tuple(v + jnp.where(start <= at, live, 0) for v, at in zip(begun, spots))

    found = lax.fori_loop(0, begin.shape[0], count, tuple(jnp.int32(0) for _ in spots))
    mine, ends, row_ends = found[:s.Z], found[s.Z:s.Z + 2], (found[s.Z + 2:s.Z + 2 + s.R], found[s.Z + 2 + s.R:])
    for way in range(2):
        for k in range(s.Z):
            coef_a[way * s.Z + k] = jnp.where(mine[k] == ends[way], 1.0, 0.0)
            for j in range(s.Z):
                order = turn[j] < turn[k] if way == 0 else turn[j] > turn[k]
                coef_b[(way * s.Z + k) * s.Z + j] = jnp.where((mine[k] == mine[j]) & order, 1.0, 0.0)
            for q in rows:
                order = q < r if way == 0 else q > r
                coef_c[(way * s.Z + k) * s.R + q] = jnp.where((mine[k] == row_ends[way][q]) & order, 1.0, 0.0)


def weigh_units(s, image_length, image_start, gain, bias):
    vmem = pl.BlockSpec(memory_space=pltpu.VMEM)
    smem = pl.BlockSpec(memory_space=pltpu.SMEM)
    shape = jax.ShapeDtypeStruct
    return pl.pallas_call(
        functools.partial(weigh_kernel, s),
        out_shape=[shape((2 * s.Z,), F32), shape((2 * s.Z * s.Z,), F32), shape((2 * s.Z * s.R,), F32),
                   shape((2 * s.L, s.D), F32), shape((2 * s.L, s.D), F32)],
        in_specs=[smem] * 2 + [vmem] * 2,
        out_specs=[smem] * 3 + [vmem] * 2,
    )(image_length, image_start, gain, bias)


def pack_state(full, first):
    return jnp.where(first, full[:HD], full[HD:])


def unpack_state(packed, first):
    zero = jnp.zeros_like(packed)
    return jnp.concatenate([jnp.where(first, packed, zero), jnp.where(first, zero, packed)], axis=0)


def spread_rows(s, rows_list):
    at = lax.broadcasted_iota(jnp.int32, (16, 128), 0)
    block = jnp.zeros((16, 128), F32)
    for i, row in enumerate(rows_list):
        block = block + jnp.where(at == i, row, 0.0)
    return block


def pick_row(block, i):
    at = lax.broadcasted_iota(jnp.int32, (16, 128), 0)
    return jnp.sum(jnp.where(at == i, block.astype(F32), 0.0), axis=0, keepdims=True)


class Inputs(typing.NamedTuple):
    tokens: object
    cotangent: object
    gain: object
    bias: object
    coef_a: object
    coef_b: object
    coef_c: object
    w_in: object
    w_mix: object
    w_up: object
    w_down: object


class Outputs(typing.NamedTuple):
    output: object
    grad: object
    vector: object
    g_in: object
    g_mix: object
    g_up: object
    g_down: object
    whole: object
    k_stream: object
    k_middle: object
    k_qkv: object
    k_mixed: object
    k_den: object
    k_state: object
    k_act: object
    k_slope: object
    k_normt: object
    s_mixed: object
    s_act: object


def forward_scratch(s):
    dma = pltpu.SemaphoreType.DMA
    return dict(
        logs=pltpu.VMEM((8, 128), F32),
        piece=pltpu.VMEM((s.L, s.NU, s.PR, s.PC), BF),
        w=pltpu.VMEM((s.Z, s.NY, s.NX, 2, s.PR, s.PC), BF),
        stream=pltpu.VMEM((s.T, s.D), F32),
        acc=pltpu.VMEM((s.T, s.D), F32),
        middle=pltpu.VMEM((s.T, s.D), F32),
        den=pltpu.VMEM((s.T, s.D), F32),
        nrm=pltpu.VMEM((s.T, s.D), BF),
        nrmt=pltpu.VMEM((2, s.NY, s.NX, 2, s.PR, s.T), BF),
        qkv=pltpu.VMEM((3, s.T, s.D), BF),
        mixed=pltpu.VMEM((s.T, s.D), BF),
        act=pltpu.VMEM((s.NJ, s.T, s.D), BF),
        slope=pltpu.VMEM((s.NJ, s.T, s.D), BF),
        msg=pltpu.VMEM((s.Z, s.MR, 128), BF),
        r1=pltpu.VMEM((s.Z, s.MR, 128), BF),
        r2=pltpu.VMEM((s.R, s.MR, 128), BF),
        pre=pltpu.VMEM((s.Z, s.MR, 128), BF),
        r3=pltpu.VMEM((s.Z, s.MR, 128), BF),
        piece_sem=dma((2 + 2 * s.NJ,)),
        w_sem=dma((s.Z,)),
        z_send=dma((RING, s.Z - 1)),
        z_recv=dma((s.U, s.Z - 1)),
        x_send=dma((RING, 2, s.NX - 1)),
        x_recv=dma((s.U, 2, s.NX - 1)),
        y_send=dma((RING, 2, s.NY - 1)),
        y_recv=dma((s.U, 2, s.NY - 1)),
        c_send=dma((RING,)),
        c_recv=dma((s.U,)),
        r1_send=dma((2 * s.L, s.Z)),
        r1_recv=dma((2 * s.L, s.Z)),
        r2_send=dma((2 * s.L, s.R)),
        r2_recv=dma((2 * s.L, s.R)),
        r3_send=dma((2 * s.L, s.Z)),
        r3_recv=dma((2 * s.L, s.Z)),
        keep=dma((8,)),
        keep_j=dma((2, s.NJ)),
        sib_send=dma((3 + s.NJ,)),
        sib_recv=dma((s.L, 3 + s.NJ)),
    )


def forward_part(s, h, spots, tick, with_unit, early):
    r, z, y, x, c = spots
    sibling = (row_at(s, y, x, 1 - c), z)
    first, _, _ = head_masks(s)

    def normalize(l, n, source):
        xhat, _ = norm_parts(source)
        v = xhat * h.gain[pl.ds(l * 2 + n, 1), :] + h.bias[pl.ds(l * 2 + n, 1), :]
        h.nrm[...] = v.astype(BF)
        h.nrmt[n] = v.T.astype(BF).reshape(s.NY, s.NX, 2, s.PR, s.T)
        keep_norm(l, n).start()
        send_norm(l, n).start()

    def keep_norm(l, n):
        return pltpu.make_async_copy(h.nrmt.at[n, :, :, c], h.k_normt.at[l, n, 0], h.keep.at[n])

    def send_norm(l, n):
        return remote(h.nrmt.at[n, :, :, 1 - c], h.k_normt.at[l, n, 1], h.sib_send.at[n], h.sib_recv.at[l, n],
                      sibling)

    def keep_one(l, index):
        src, dst = ((h.stream, h.k_stream), (h.qkv, h.k_qkv), (h.mixed, h.k_mixed), (h.den, h.k_den),
                    (h.middle, h.k_middle), (h.r3, h.k_state))[index - 2]
        return pltpu.make_async_copy(src, dst.at[l], h.keep.at[index])

    def send_mixed(l):
        return remote(h.mixed, h.s_mixed.at[l], h.sib_send.at[2], h.sib_recv.at[l, 2], sibling)

    def keep_act(l, j):
        return pltpu.make_async_copy(h.act.at[j], h.k_act.at[l, j], h.keep_j.at[0, j])

    def keep_slope(l, j):
        return pltpu.make_async_copy(h.slope.at[j], h.k_slope.at[l, j], h.keep_j.at[1, j])

    def send_act(l, j):
        return remote(h.act.at[j], h.s_act.at[l, j], h.sib_send.at[3 + j], h.sib_recv.at[l, 3 + j], sibling)

    ones = pair_ones()
    tall = jnp.ones((s.T, 128), BF)
    h.logs[...] = jnp.where(lax.broadcasted_iota(jnp.int32, (8, 128), 0) == 1, -jnp.inf, 0.0)
    tick(0)
    tick(1)
    early()
    tick(2)
    h.stream[...] = h.tokens[...].astype(F32)

    @pl.loop(3, LAG_READY)
    def _(t):
        tick(t)

    def one_layer(l, carry):
        base = l * s.NU
        keep_one(l, 2).start()
        normalize(l, 0, h.stream[...])

        def project(kind, carry):
            u = base + kind

            def body(k, weight):
                v = dot(h.nrm[...], weight)
                phi = jnp.where(v > 0, v + 1.0, jnp.exp(jnp.minimum(v, 0.0)))
                h.qkv[kind, :, lanes(k, s.PC)] = jnp.where(kind < 2, phi, v).astype(BF)

            with_unit(h.w_in, l, kind, u, body, lambda: tick(u + LAG_READY))
            return carry

        lax.fori_loop(0, 3, project, 0)
        keep_one(l, 3).start()
        round_one, round_two, round_three, arrive, settle = prefix_rounds(s, h, l, r, z, 0)

        def local_state(k, carry):
            totals = []
            for i in range(s.NP):
                at = lanes(k * s.NP + i, 128)
                keys, vals = h.qkv[1, :, at], h.qkv[2, :, at]
                h.msg[k, i * HD:(i + 1) * HD] = pack_state(dot(keys, vals, TN), first).astype(BF)
                totals.append(jnp.sum(keys.astype(F32), axis=0, keepdims=True))
            h.msg[k, s.NP * HD:] = spread_rows(s, totals).astype(BF)
            return carry

        lax.fori_loop(0, s.Z, local_state, 0)
        round_one()
        tick(base + 3 + LAG_READY)
        round_two()
        tick(base + 4 + LAG_READY)
        round_three()
        tick(base + 5 + LAG_READY)
        arrive()
        keep_one(l, 7).start()
        causal = (lax.broadcasted_iota(jnp.int32, (s.T, s.T), 1) <= lax.broadcasted_iota(jnp.int32, (s.T, s.T), 0))

        def attend(p, carry):
            k, i = p // s.NP, p % s.NP
            at = lanes(p, 128)
            query, key, value = h.qkv[0, :, at], h.qkv[1, :, at], h.qkv[2, :, at]
            wide = query.astype(F32)
            value_ones = jnp.concatenate([value, tall], axis=1)
            zero = jnp.zeros_like(query)
            results = []
            for head in range(2):
                mine = first if head == 0 else jnp.logical_not(first)
                scores = dot(jnp.where(mine, query, zero), key, NT)
                weights = jnp.where(causal, scores, 0.0).astype(BF)
                results.append(dot(weights, value_ones))
            state = unpack_state(h.r3[k, pl.ds(pl.multiple_of(i * HD, HD), HD), :], first)
            total = pick_row(h.r3[k, s.NP * HD:, :], i)
            square = jnp.zeros((128, 128), BF)
            right = jnp.concatenate(
                [jnp.concatenate([state, square], axis=1), jnp.concatenate([square, ones], axis=1)], axis=0)
            left = jnp.concatenate([query, (wide * total).astype(BF)], axis=1)
            earlier = dot(left, right)
            num = jnp.where(first, results[0][:, :128], results[1][:, :128]) + earlier[:, :128]
            den = jnp.where(first, results[0][:, 128:], results[1][:, 128:]) + earlier[:, 128:] + EPS_DEN
            h.mixed[:, at] = (num / den).astype(BF)
            h.den[:, at] = den
            logs = jnp.log(den)
            h.logs[0:1] += jnp.sum(logs, axis=0, keepdims=True)
            h.logs[1:2] = jnp.maximum(h.logs[1:2], jnp.max(logs, axis=0, keepdims=True))
            return carry

        half = s.Z * s.NP // 2
        lax.fori_loop(0, half, attend, 0)
        tick(base + 6 + LAG_READY)
        lax.fori_loop(half, s.Z * s.NP, attend, 0)
        settle()
        keep_one(l, 4).start()
        send_mixed(l).start()
        keep_one(l, 5).start()

        h.acc[...] = jnp.zeros_like(h.acc)

        def mix(k, weight):
            h.acc[...] += dot(h.mixed[:, lanes(k, s.PC)], weight, NT)

        with_unit(h.w_mix, l, 0, base + 3, mix)
        h.middle[...] = h.stream[...] + h.acc[...]
        keep_one(l, 6).start()
        normalize(l, 1, h.middle[...])

        def up(j, carry):
            u = base + 4 + j

            def body(k, weight):
                v = dot(h.nrm[...], weight)
                cdf = 0.5 * (1.0 + lax.erf(v * ROOT_HALF))
                h.act[j, :, lanes(k, s.PC)] = (v * cdf).astype(BF)
                h.slope[j, :, lanes(k, s.PC)] = (cdf + v * (ROOT_TAU * jnp.exp(-0.5 * v * v))).astype(BF)

            with_unit(h.w_up, l, j, u, body, lambda: pl.when(j >= 3)(lambda: tick(u + LAG_READY)))
            keep_act(l, j).start()
            keep_slope(l, j).start()
            send_act(l, j).start()
            return carry

        lax.fori_loop(0, s.NJ, up, 0)
        keep_one(l, 2).wait()
        h.stream[...] = h.middle[...]

        def down(j, carry):
            u = base + 4 + s.NJ + j

            def body(k, weight):
                h.stream[...] += dot(h.act[j, :, lanes(k, s.PC)], weight, NT)

            with_unit(h.w_down, l, j, u, body, lambda: tick(u + LAG_READY))
            return carry

        @pl.when(l + 1 < s.L)
        def _():
            lax.fori_loop(0, s.NJ, down, 0)

        for n in range(2):
            keep_norm(l, n).wait()
            send_norm(l, n).wait_send()
            send_norm(l, n).wait_recv()
        for index in range(3, 8):
            keep_one(l, index).wait()
        send_mixed(l).wait()

        def finish(j, carry):
            keep_act(l, j).wait()
            keep_slope(l, j).wait()
            send_act(l, j).wait()
            return carry

        lax.fori_loop(0, s.NJ, finish, 0)
        return carry

    lax.fori_loop(0, s.L, one_layer, 0)


def split_rows(s, weight_in, *rest):
    cut = (s.NY, s.NX, 2, s.PR)
    turned = jnp.transpose(weight_in, (0, 2, 1, 3)).reshape((s.L, 3) + cut + (s.PC,))
    return (turned,) + tuple(w.reshape((s.L,) + cut + w.shape[2:]) for w in rest)


BACK_FIRST, BACK_SECOND, BACK_LAST = 2, 4, 6
SLOTS = 8
OUT_RING = 4
X_EARLY, X_LATE, X_DOWN, X_MIX = 0, 1, 2, 3

def backward_scratch(s):
    dma = pltpu.SemaphoreType.DMA
    half = s.PR // 2
    return dict(
        part=pltpu.VMEM((SLOTS, s.NY, s.NX, s.Z, s.PR, s.PC), BF),
        land_x1=pltpu.VMEM((SLOTS, s.NX - 1, s.NY, s.Z, half, s.PC), BF),
        land_y1=pltpu.VMEM((SLOTS, s.NY - 1, s.NX, s.Z, half, s.PC), BF),
        land_x2=pltpu.VMEM((SLOTS, s.NX - 1, s.Z, half, s.PC), BF),
        land_y2=pltpu.VMEM((SLOTS, s.NY - 1, s.Z, half, s.PC), BF),
        land_z=pltpu.VMEM((SLOTS, s.Z - 1, s.PR, s.PC), BF),
        final=pltpu.VMEM((OUT_RING, s.PR, s.PC), F32),
        resid=pltpu.VMEM((s.T, s.D), F32),
        gb=pltpu.VMEM((s.T, s.D), BF),
        turned=pltpu.VMEM((s.NY, s.NX, 2, s.PR, s.T), BF),
        xt=pltpu.VMEM((4, 2, s.NY, s.NX, s.PR, s.T), BF),
        b_act=pltpu.VMEM((2, s.T, s.D), BF),
        b_slope=pltpu.VMEM((s.T, s.D), BF),
        ug=pltpu.VMEM((s.NJ, s.T, s.D), BF),
        ug_sib=pltpu.VMEM((s.NJ, s.T, s.D), BF),
        pg=pltpu.VMEM((3, s.T, s.D), BF),
        pg_sib=pltpu.VMEM((3, s.T, s.D), BF),
        b_mixed=pltpu.VMEM((2, s.T, s.D), BF),
        rg=pltpu.VMEM((s.T, s.D), BF),
        ng=pltpu.VMEM((s.T, s.D), BF),
        dg=pltpu.VMEM((s.T, s.D), F32),
        state=pltpu.VMEM((s.Z, s.MR, 128), BF),
        vec=pltpu.VMEM((16, s.D), F32),
        v_z=pltpu.VMEM((s.Z, 16, s.D), F32),
        v_c=pltpu.VMEM((2, 16, s.D), F32),
        v_x=pltpu.VMEM((s.NX, 16, s.D), F32),
        v_y=pltpu.VMEM((s.NY, 16, s.D), F32),
        x1_send=dma((SLOTS, s.NX - 1)),
        x1_recv=dma((SLOTS, s.NX - 1)),
        y1_send=dma((SLOTS, s.NY - 1)),
        y1_recv=dma((SLOTS, s.NY - 1)),
        x2_send=dma((SLOTS, s.NX - 1)),
        x2_recv=dma((SLOTS, s.NX - 1)),
        y2_send=dma((SLOTS, s.NY - 1)),
        y2_recv=dma((SLOTS, s.NY - 1)),
        bz_send=dma((SLOTS, s.Z - 1)),
        bz_recv=dma((SLOTS, s.Z - 1)),
        out_sem=dma((OUT_RING,)),
        xt_sem=dma((2, 2, s.NQ)),
        xt_send=dma((2, s.NQ)),
        xt_recv=dma((s.L, 2, s.NQ)),
        g_send=dma((s.NJ + 3,)),
        g_recv=dma((s.L, s.NJ + 3)),
        get=dma((8,)),
        v_send=dma((4, max(s.Z, s.NX, s.NY))),
        v_recv=dma((4, max(s.Z, s.NX, s.NY))),
    )


def gradient_sums(s, h, r, z, y, x, c):
    half = s.PR // 2
    rows = (pl.ds(0, half), pl.ds(half, half))
    part = h.part

    def to_x(d):
        return (row_at(s, y, (x + d) % s.NX, c), z)

    def to_y(d):
        return (row_at(s, (y + d) % s.NY, x, c), z)

    def first(v):
        b = v % SLOTS
        return [
            remote(part.at[b, :, d, :, rows[0]], h.land_x1.at[b, s.NX - d - 1], h.x1_send.at[b, d - 1],
                   h.x1_recv.at[b, s.NX - d - 1], to_x(d)) for d in range(1, s.NX)
        ] + [
            remote(part.at[b, d, :, :, rows[1]], h.land_y1.at[b, s.NY - d - 1], h.y1_send.at[b, d - 1],
                   h.y1_recv.at[b, s.NY - d - 1], to_y(d)) for d in range(1, s.NY)
        ]

    def second(v):
        b = v % SLOTS
        return [
            remote(part.at[b, d, 0, :, rows[0]], h.land_y2.at[b, s.NY - d - 1], h.y2_send.at[b, d - 1],
                   h.y2_recv.at[b, s.NY - d - 1], to_y(d)) for d in range(1, s.NY)
        ] + [
            remote(part.at[b, 0, d, :, rows[1]], h.land_x2.at[b, s.NX - d - 1], h.x2_send.at[b, d - 1],
                   h.x2_recv.at[b, s.NX - d - 1], to_x(d)) for d in range(1, s.NX)
        ]

    def last(v):
        b = v % SLOTS
        return [
            remote(part.at[b, 0, 0, d], h.land_z.at[b, s.Z - d - 1], h.bz_send.at[b, d - 1],
                   h.bz_recv.at[b, s.Z - d - 1], (r, (z + d) % s.Z)) for d in range(1, s.Z)
        ]

    def stage_second(v):
        b = v % SLOTS
        for cp in first(v):
            cp.wait_recv()

        def add(k, carry):
            for dy in range(s.NY):
                total = part[b, dy, 0, k, :half].astype(F32)
                for i in range(s.NX - 1):
                    total = total + h.land_x1[b, i, dy, k].astype(F32)
                part[b, dy, 0, k, :half] = total.astype(BF)
            for dx in range(s.NX):
                total = part[b, 0, dx, k, half:].astype(F32)
                for i in range(s.NY - 1):
                    total = total + h.land_y1[b, i, dx, k].astype(F32)
                part[b, 0, dx, k, half:] = total.astype(BF)
            return carry

        lax.fori_loop(0, s.Z, add, 0)
        for cp in second(v):
            cp.start()

    def stage_last(v):
        b = v % SLOTS
        for cp in second(v):
            cp.wait_recv()

        def add(k, carry):
            total = part[b, 0, 0, k, :half].astype(F32)
            for i in range(s.NY - 1):
                total = total + h.land_y2[b, i, k].astype(F32)
            part[b, 0, 0, k, :half] = total.astype(BF)
            total = part[b, 0, 0, k, half:].astype(F32)
            for i in range(s.NX - 1):
                total = total + h.land_x2[b, i, k].astype(F32)
            part[b, 0, 0, k, half:] = total.astype(BF)
            return carry

        lax.fori_loop(0, s.Z, add, 0)
        for cp in last(v):
            cp.start()

    def out_copy(at, o):
        return pltpu.make_async_copy(h.final.at[o], at, h.out_sem.at[o])

    def stage_out(v):
        b, o = v % SLOTS, v % OUT_RING
        for cp in last(v):
            cp.wait_recv()

        @pl.when(v >= OUT_RING)
        def _():
            out_copy(h.g_mix.at[0], o).wait()

        total = part[b, 0, 0, 0].astype(F32)
        for i in range(s.Z - 1):
            total = total + h.land_z[b, i].astype(F32)
        h.final[o] = total
        l, q = s.L - 1 - v // s.NU, v % s.NU
        wide = 2 * s.NJ
        pl.when(q < s.NJ)(lambda: out_copy(h.g_down.at[l, :, lanes(q, s.PC)], o).start())
        pl.when((q >= s.NJ) & (q < wide))(lambda: out_copy(h.g_up.at[l, :, lanes(q - s.NJ, s.PC)], o).start())
        pl.when(q == wide)(lambda: out_copy(h.g_mix.at[l], o).start())
        pl.when(q > wide)(lambda: out_copy(h.g_in.at[l, q - wide - 1], o).start())

    def inside(v, what):
        pl.when((v >= 0) & (v < s.U))(functools.partial(what, v))

    def wait_sends(v):
        for cp in first(v) + second(v) + last(v):
            cp.wait_send()

    def tick(t):
        def start(v):
            for cp in first(v):
                cp.start()

        inside(t, start)
        inside(t - BACK_FIRST, stage_second)
        inside(t - BACK_SECOND, stage_last)
        inside(t - BACK_LAST, stage_out)

    def produce(v, which, own, sibling):
        b = v % SLOTS
        inside(v - SLOTS, wait_sends)
        left = [h.xt[which, i].reshape(s.NQ * s.PR, s.T) for i in range(2)]

        def block(k, carry):
            at = lanes(k, s.PC)
            total = dot(left[0], own[:, at]) + dot(left[1], sibling[:, at])
            part[b, :, :, k] = total.astype(BF).reshape(s.NY, s.NX, s.PR, s.PC)
            return carry

        lax.fori_loop(0, s.Z, block, 0)
        tick(v)

    def drain():
        @pl.loop(s.U + 4, s.U + max(BACK_LAST, 4))
        def _(t):
            tick(t)

    def settle():
        @pl.loop(s.U - SLOTS, s.U)
        def _(v):
            wait_sends(v)

        for o in range(OUT_RING):
            out_copy(h.g_mix.at[0], o).wait()

    return produce, tick, drain, settle


def backward_part(s, h, spots, tick_weights, with_unit, sums):
    r, z, y, x, c = spots
    produce, tick, drain, settle_sums = sums
    sibling = (row_at(s, y, x, 1 - c), z)
    first, _, _ = head_masks(s)
    ones = pair_ones()
    tall = jnp.ones((s.T, 128), BF)
    squares = [(dy, dx) for dy in range(s.NY) for dx in range(s.NX)]

    def get(src, dst, index):
        return pltpu.make_async_copy(src, dst, h.get.at[index])

    def xt_loads(l):
        return [
            pltpu.make_async_copy(h.k_normt.at[l, n, i, (y + dy) % s.NY, (x + dx) % s.NX], h.xt.at[n, i, dy, dx],
                                  h.xt_sem.at[n, i, q])
            for n in range(2) for i in range(2) for q, (dy, dx) in enumerate(squares)
        ]

    def xt_sends(l, which):
        return [
            remote(h.turned.at[(y + dy) % s.NY, (x + dx) % s.NX, 1 - c], h.xt.at[which, 1, dy, dx],
                   h.xt_send.at[which - 2, q], h.xt_recv.at[l, which - 2, q], sibling)
            for q, (dy, dx) in enumerate(squares)
        ]

    def turn(l, which):
        wide = h.grad[...]
        h.gb[...] = wide.astype(BF)
        h.turned[...] = wide.T.astype(BF).reshape(s.NY, s.NX, 2, s.PR, s.T)
        for cp in xt_sends(l, which):
            cp.start()
        for dy, dx in squares:
            h.xt[which, 0, dy, dx] = h.turned[(y + dy) % s.NY, (x + dx) % s.NX, c]
    def g_send(l, src, dst, j, index):
        return remote(src.at[j], dst.at[j], h.g_send.at[index], h.g_recv.at[l, index], sibling)

    def norm_back(l, n):
        back = h.acc[...]
        xhat, inv = norm_parts(h.resid[...])
        at = l * 2 + n
        h.vec[pl.ds(at, 1)] = jnp.sum(back * xhat, axis=0, keepdims=True)
        h.vec[pl.ds(2 * s.L + at, 1)] = jnp.sum(back, axis=0, keepdims=True)
        scaled = back * h.gain[pl.ds(l * 2 + n, 1), :]
        mean = jnp.mean(scaled, axis=-1, keepdims=True)
        along = jnp.mean(scaled * xhat, axis=-1, keepdims=True)
        h.grad[...] += inv * (scaled - mean - xhat * along)

    def early():
        h.grad[...] = h.cotangent[...].astype(F32)
        turn(s.L - 1, X_DOWN)

    def one_layer(li, carry):
        l = s.L - 1 - li
        base = li * s.NU
        unit = l * s.NU
        loads = [
            get(h.k_qkv.at[l], h.qkv, 0),
            get(h.k_mixed.at[l], h.b_mixed.at[0], 1),
            get(h.s_mixed.at[l], h.b_mixed.at[1], 2),
            get(h.k_den.at[l], h.den, 3),
            get(h.k_state.at[l], h.state, 4),
        ]
        act_loads = lambda j: [get(h.k_act.at[l, j], h.b_act.at[0], 5), get(h.s_act.at[l, j], h.b_act.at[1], 6)]
        slope_load = lambda j: get(h.k_slope.at[l, j], h.b_slope, 7)
        for cp in act_loads(0) + [slope_load(0)] + loads + xt_loads(l):
            cp.start()
        h.acc[...] = jnp.zeros_like(h.acc)
        for cp in xt_loads(l):
            cp.wait()
        for cp in xt_sends(l, X_DOWN):
            cp.wait_recv()

        def feed_back(j, carry):
            for cp in act_loads(j):
                cp.wait()
            produce(base + j, X_DOWN, h.b_act.at[0], h.b_act.at[1])
            slope_load(j).wait()

            def body(k, weight):
                at = lanes(k, s.PC)
                h.ug[j, :, at] = (dot(h.gb[...], weight) * h.b_slope[:, at].astype(F32)).astype(BF)

                @pl.when(li == 0)
                def _():
                    h.stream[...] += dot(h.b_act[0, :, at], weight, NT)

            u = unit + 4 + s.NJ + j
            with_unit(h.w_down, l, j, u, body, lambda: pl.when(li == 0)(lambda: tick_weights(u + LAG_READY)))

            @pl.when(j + 1 < s.NJ)
            def _():
                for cp in act_loads(j + 1):
                    cp.start()


            @pl.when(j + 1 < s.NJ)
            def _():
                slope_load(j + 1).start()

            g_send(l, h.ug, h.ug_sib, j, j).start()

            def body_up(k, weight):
                h.acc[...] += dot(h.ug[j, :, lanes(k, s.PC)], weight, NT)

            with_unit(h.w_up, l, j, unit + 4 + j, body_up)
            return carry

        def produce_up(j):
            g_send(l, h.ug, h.ug_sib, j, j).wait_recv()
            produce(base + s.NJ + j, X_LATE, h.ug.at[j], h.ug_sib.at[j])

        lax.fori_loop(0, s.NJ, feed_back, 0)
        produce_up(0)
        middle = get(h.k_middle.at[l], h.resid, 5)
        middle.start()
        for cp in xt_sends(l, X_DOWN):
            cp.wait_send()
        middle.wait()
        norm_back(l, 1)
        turn(l, X_MIX)
        for cp in xt_sends(l, X_MIX):
            cp.wait_recv()
        stream = get(h.k_stream.at[l], h.resid, 5)
        stream.start()

        def body_mix(k, weight):
            h.rg[:, lanes(k, s.PC)] = dot(h.gb[...], weight).astype(BF)

        with_unit(h.w_mix, l, 0, unit + 3, body_mix)
        for cp in loads:
            cp.wait()
        round_one, round_two, round_three, arrive, settle = prefix_rounds(s, h, l, r, z, 1)

        def local_state(k, carry):
            totals = []
            for i in range(s.NP):
                at = lanes(k * s.NP + i, 128)
                query, wide = h.qkv[0, :, at], h.rg[:, at].astype(F32)
                den = h.den[:, at]
                num = (wide / den).astype(BF)
                product = wide * h.b_mixed[0, :, at].astype(F32)
                high = product.astype(BF)
                low = (product - high.astype(F32)).astype(BF)
                slope = -(dot(high, ones) + dot(low, ones)) / den
                h.ng[:, at] = num
                h.dg[:, at] = slope
                h.msg[k, i * HD:(i + 1) * HD] = pack_state(dot(query, num, TN), first).astype(BF)
                totals.append(jnp.sum(query.astype(F32) * slope, axis=0, keepdims=True))
            h.msg[k, s.NP * HD:] = spread_rows(s, totals).astype(BF)
            return carry

        lax.fori_loop(0, s.Z, local_state, 0)
        round_one()
        produce_up(1)
        round_two()
        produce_up(2)
        round_three()
        lax.fori_loop(3, s.NJ, lambda j, carry: (produce_up(j), carry)[1], 0)
        arrive()
        causal = (lax.broadcasted_iota(jnp.int32, (s.T, s.T), 1) <= lax.broadcasted_iota(jnp.int32, (s.T, s.T), 0))
        lane = lax.broadcasted_iota(jnp.int32, (1, 128), 1)

        def attend_back(p, carry):
            k, i = p // s.NP, p % s.NP
            at = lanes(p, 128)
            query, key, value, num = h.qkv[0, :, at], h.qkv[1, :, at], h.qkv[2, :, at], h.ng[:, at]
            slope = h.dg[:, at]
            high = slope.astype(BF)
            low = (slope - high.astype(F32)).astype(BF)
            zero = jnp.zeros_like(query)
            value_ones = jnp.concatenate([value, tall], axis=1)
            rows = pl.ds(pl.multiple_of(i * HD, HD), HD)
            state = unpack_state(h.state[k, rows, :], first)
            after = unpack_state(h.r3[k, rows, :], first)
            total = pick_row(h.state[k, s.NP * HD:, :], i)
            total_after = pick_row(h.r3[k, s.NP * HD:, :], i)
            value_grad = dot(key, after)
            query_grad = dot(num, state, NT) + slope * total
            key_grad = dot(value, after, NT) + total_after
            for head in range(2):
                mine = first if head == 0 else jnp.logical_not(first)
                query_mine = jnp.where(mine, query, zero)
                num_mine = jnp.where(mine, num, zero)
                key_mine = jnp.where(mine, key, zero)
                weights = jnp.where(causal, dot(query_mine, key, NT), 0.0).astype(BF)
                extra = jnp.where(lane == head * HD, high, jnp.where(lane == head * HD + 1, low, zero))
                score = dot(jnp.concatenate([num_mine, extra], axis=1), value_ones, NT)
                score = jnp.where(causal, score, 0.0).astype(BF)
                value_grad = value_grad + dot(weights, num_mine, TN)
                query_grad = query_grad + dot(score, key_mine)
                key_grad = key_grad + dot(score, query_mine, TN)
            h.pg[0, :, at] = (query_grad * jnp.minimum(query.astype(F32), 1.0)).astype(BF)
            h.pg[1, :, at] = (key_grad * jnp.minimum(key.astype(F32), 1.0)).astype(BF)
            h.pg[2, :, at] = value_grad.astype(BF)
            return carry

        half = s.Z * s.NP // 2
        lax.fori_loop(0, half, attend_back, 0)
        produce(base + 2 * s.NJ, X_MIX, h.b_mixed.at[0], h.b_mixed.at[1])
        lax.fori_loop(half, s.Z * s.NP, attend_back, 0)
        settle()
        for kind in range(3):
            g_send(l, h.pg, h.pg_sib, kind, s.NJ + kind).start()
        h.acc[...] = jnp.zeros_like(h.acc)

        def project_back(kind, carry):
            def body(k, weight):
                h.acc[...] += dot(h.pg[kind, :, lanes(k, s.PC)], weight, NT)

            with_unit(h.w_in, l, kind, unit + kind, body)
            g_send(l, h.pg, h.pg_sib, kind, s.NJ + kind).wait_recv()
            produce(base + 2 * s.NJ + 1 + kind, X_EARLY, h.pg.at[kind], h.pg_sib.at[kind])
            return carry

        lax.fori_loop(0, 3, project_back, 0)
        stream.wait()
        norm_back(l, 0)
        for cp in xt_sends(l, X_MIX):
            cp.wait_send()
        for j in range(s.NJ):
            g_send(l, h.ug, h.ug_sib, j, j).wait_send()
        for kind in range(3):
            g_send(l, h.pg, h.pg_sib, kind, s.NJ + kind).wait_send()

        @pl.when(li + 1 < s.L)
        def _():
            turn(l - 1, X_DOWN)

        return carry

    def run():
        lax.fori_loop(0, s.L, one_layer, 0)
        finish()

    def finish():
        h.vec[4 * s.L:4 * s.L + 2, :128] = h.logs[0:2]
        source = h.vec[...]
        top = lax.broadcasted_iota(jnp.int32, (16, s.D), 0) == 4 * s.L + 1
        stages = (
            (h.v_z, s.Z, z, lambda d: (r, (z + d) % s.Z)),
            (h.v_c, 2, c, lambda d: sibling),
            (h.v_x, s.NX, x, lambda d: (row_at(s, y, (x + d) % s.NX, c), z)),
            (h.v_y, s.NY, y, lambda d: (row_at(s, (y + d) % s.NY, x, c), z)),
        )
        pending = []
        for i, (slots, count, me, peer) in enumerate(stages):
            slots[me] = source
            for d in range(1, count):
                at = slots.at[me]
                cp = remote(at, at, h.v_send.at[i, d], h.v_recv.at[i, count - d], peer(d))
                cp.start()
                pending.append(cp)
            tick(s.U + i)
            for d in range(1, count):
                at = slots.at[(me + d) % count]
                remote(at, at, h.v_send.at[i, d], h.v_recv.at[i, d], (r, z)).wait_recv()
            total, largest = slots[0], slots[0]
            for k in range(1, count):
                total = total + slots[k]
                largest = jnp.maximum(largest, slots[k])
            source = jnp.where(top, largest, total)
        h.vector[...] = source
        for cp in pending:
            cp.wait_send()
        drain()
        settle_sums()

    return early, run


def unit_reader(s, h):
    def own(kind, l, j):
        if kind is h.w_in:
            src = h.w_in.at[l, j]
        elif kind is h.w_mix:
            src = h.w_mix.at[l]
        else:
            src = kind.at[l, :, :, :, :, lanes(j, s.PC)]
        return pltpu.make_async_copy(src, h.w.at[0], h.w_sem.at[0])

    def load(u, k):
        return pltpu.make_async_copy(h.whole.at[u, k - 1], h.w.at[k], h.w_sem.at[k])

    def with_unit(kind, l, j, u, body, advance=lambda: None):
        own(kind, l, j).start()
        advance()
        for k in range(1, s.Z):
            load(u, k).start()
        own(kind, l, j).wait()
        body(0, h.w[0].reshape(s.D, s.PC))

        @pl.loop(1, s.Z)
        def _(k):
            load(u, k).wait()
            body(k, h.w[k].reshape(s.D, s.PC))

    return with_unit


def kernel(s, *refs):
    scratch = forward_scratch(s) | backward_scratch(s)
    names = Inputs._fields + Outputs._fields + tuple(scratch)
    h = types.SimpleNamespace(**dict(zip(names, refs, strict=True)))
    spots = r, z, y, x, c = place(s)
    pieces = [
        pltpu.make_async_copy(h.w_in.at[:, :, y, x, c], h.piece.at[:, 0:3], h.piece_sem.at[0]),
        pltpu.make_async_copy(h.w_mix.at[:, y, x, c], h.piece.at[:, 3], h.piece_sem.at[1]),
    ]
    for j in range(s.NJ):
        cols = pl.ds(j * s.PC, s.PC)
        pieces.append(pltpu.make_async_copy(h.w_up.at[:, y, x, c, :, cols], h.piece.at[:, 4 + j], h.piece_sem.at[2 + j]))
        pieces.append(pltpu.make_async_copy(h.w_down.at[:, y, x, c, :, cols], h.piece.at[:, 4 + s.NJ + j],
                                            h.piece_sem.at[2 + s.NJ + j]))
    for cp in pieces:
        cp.start()
    greet(s, r, z)
    for cp in pieces:
        cp.wait()
    tick_weights, drain_weights = weight_gather(s, h, r, z, y, x, c)
    with_unit = unit_reader(s, h)
    sums = gradient_sums(s, h, r, z, y, x, c)
    early, backward = backward_part(s, h, spots, tick_weights, with_unit, sums)

    def before():
        h.vec[...] = jnp.zeros_like(h.vec)
        early()

    forward_part(s, h, spots, tick_weights, with_unit, before)
    backward()
    h.output[...] = h.stream[...].astype(BF)
    drain_weights()


def call(s, arrays):
    vmem = pl.BlockSpec(memory_space=pltpu.VMEM)
    smem = pl.BlockSpec(memory_space=pltpu.SMEM)
    hbm = pl.BlockSpec(memory_space=pl.ANY)
    shape = jax.ShapeDtypeStruct
    outs = Outputs(
        output=shape((s.T, s.D), BF),
        grad=shape((s.T, s.D), F32),
        vector=shape((16, s.D), F32),
        g_in=shape((s.L, 3, s.PR, s.PC), F32),
        g_mix=shape((s.L, s.PR, s.PC), F32),
        g_up=shape((s.L, s.PR, s.NJ * s.PC), F32),
        g_down=shape((s.L, s.PR, s.NJ * s.PC), F32),
        whole=shape((s.U, s.Z - 1, s.NY, s.NX, 2, s.PR, s.PC), BF),
        k_stream=shape((s.L, s.T, s.D), F32),
        k_middle=shape((s.L, s.T, s.D), F32),
        k_qkv=shape((s.L, 3, s.T, s.D), BF),
        k_mixed=shape((s.L, s.T, s.D), BF),
        k_den=shape((s.L, s.T, s.D), F32),
        k_state=shape((s.L, s.Z, s.MR, 128), BF),
        k_act=shape((s.L, s.NJ, s.T, s.D), BF),
        k_slope=shape((s.L, s.NJ, s.T, s.D), BF),
        k_normt=shape((s.L, 2, 2, s.NY, s.NX, s.PR, s.T), BF),
        s_mixed=shape((s.L, s.T, s.D), BF),
        s_act=shape((s.L, s.NJ, s.T, s.D), BF),
    )
    scratch = forward_scratch(s) | backward_scratch(s)
    out = pl.pallas_call(
        functools.partial(kernel, s),
        out_shape=list(outs),
        in_specs=[vmem] * 4 + [smem] * 3 + [hbm] * 4,
        out_specs=[vmem] * 3 + [hbm] * (len(outs) - 3),
        scratch_shapes=list(scratch.values()),
        compiler_params=pltpu.CompilerParams(
            collective_id=0, has_side_effects=True, vmem_limit_bytes=61 * 1024 * 1024),
    )(*arrays)
    return Outputs(*out)


def finish_kernel(s, count, *refs):
    sources, vector, results = refs[:count], refs[count], refs[count + 1:2 * count + 1]
    gain, bias, top, log_max, log_mean, sems = refs[2 * count + 1:2 * count + 7]
    held = refs[2 * count + 7:]
    loads = [pltpu.make_async_copy(src, mid, sems.at[0, i]) for i, (src, mid) in enumerate(zip(sources, held))]
    stores = [pltpu.make_async_copy(mid, dst, sems.at[1, i]) for i, (mid, dst) in enumerate(zip(held, results))]
    for cp in loads:
        cp.start()
    for load, store in zip(loads, stores):
        load.wait()
        store.start()
    for l in range(s.L):
        gain[l] = vector[2 * l:2 * l + 2]
        bias[l] = vector[2 * s.L + 2 * l:2 * s.L + 2 * l + 2]
    top[...] = vector[4 * s.L - 1:4 * s.L]
    logs = s.R * s.Z * s.T * s.D * s.L
    log_mean[...] = jnp.sum(vector[4 * s.L:4 * s.L + 1, :128], axis=1, keepdims=True) / logs
    log_max[...] = jnp.max(vector[4 * s.L + 1:4 * s.L + 2, :128], axis=1, keepdims=True)
    for cp in stores:
        cp.wait()


def finish(s, got):
    vmem = pl.BlockSpec(memory_space=pltpu.VMEM)
    hbm = pl.BlockSpec(memory_space=pl.ANY)
    shape = jax.ShapeDtypeStruct
    large = (got.output, got.grad, got.g_in, got.g_mix, got.g_up, got.g_down)
    return pl.pallas_call(
        functools.partial(finish_kernel, s, len(large)),
        out_shape=[shape(a.shape, a.dtype) for a in large] + [
            shape((s.L, 2, s.D), F32), shape((s.L, 2, s.D), F32), shape((1, s.D), F32), shape((1, 1), F32), shape((1, 1), F32)],
        in_specs=[hbm] * len(large) + [vmem],
        out_specs=[hbm] * len(large) + [vmem] * 5,
        scratch_shapes=[pltpu.SemaphoreType.DMA((2, len(large)))] + [pltpu.VMEM(a.shape, a.dtype) for a in large],
        compiler_params=pltpu.CompilerParams(vmem_limit_bytes=61 * 1024 * 1024),
    )(*large, got.vector)


def local(mesh, tokens, cotangent, image_length, image_start, norm_gain, norm_bias, weight_in, weight_mix, weight_up,
          weight_down):
    s = sizes_of(mesh, tokens, weight_in, weight_up)
    weights = split_rows(s, weight_in, weight_mix, weight_up, weight_down)
    *coefs, gain, bias = weigh_units(s, image_length, image_start, norm_gain, norm_bias)
    got = call(s, Inputs(tokens, cotangent, gain, bias, *coefs, *weights))
    output, grad, g_in, g_mix, g_up, g_down, grad_gain, grad_bias, top, log_max, log_mean = finish(s, got)
    return (output, grad, grad_gain, grad_bias, top.reshape(-1), jnp.transpose(g_in, (0, 2, 1, 3)), g_mix, g_up, g_down,
            log_max.reshape(()), log_mean.reshape(()))


def solution(mesh):
    pixels = P(("rows", "feat"), None)
    placed = (pixels, pixels, P(), P(), P(), P(), P(None, None, None, "feat"), P(None, None, "feat"), P(None, None, "feat"),
              P(None, None, "feat"))
    return jax.shard_map(
        functools.partial(local, mesh),
        mesh=mesh,
        in_specs=placed,
        out_specs=(pixels, pixels, P(), P(), P(), P(None, "rows", None, "feat"), P(None, "rows", "feat"),
                   P(None, "rows", "feat"), P(None, "rows", "feat"), P(), P()),
        check_vma=False,
    )
```

```python
import functools
import types
import typing

import jax
import jax.numpy as jnp
from jax import lax
from jax.experimental import pallas as pl
from jax.experimental.pallas import tpu as pltpu
from jax.sharding import PartitionSpec as P

HD = 64
EPS_NORM = 1e-05
EPS_DEN = 1e-06
MESH = pl.DeviceIdType.MESH
BF = jnp.bfloat16
F32 = jnp.float32
LAG_FIRST, LAG_SECOND, LAG_CORE, LAG_READY = 2, 3, 4, 5
RING = 4
ROOT_HALF = 0.7071067811865476
ROOT_TAU = 0.3989422804014327


def sizes_of(mesh, tokens, weight_in, weight_up):
    s = types.SimpleNamespace()
    s.R, s.Z = mesh.shape["rows"], mesh.shape["feat"]
    chips = s.R // 2
    s.NX = 1
    while s.NX * s.NX < chips:
        s.NX *= 2
    s.NY = chips // s.NX
    s.T, s.D = tokens.shape
    s.L = weight_in.shape[0]
    s.PC = weight_in.shape[3]
    s.PR = s.D // s.R
    s.NJ = weight_up.shape[2] // s.PC
    s.NU = 4 + 2 * s.NJ
    s.U = s.L * s.NU
    s.NP = s.PC // 128
    s.MR = s.NP * HD + 16
    s.NQ = s.NY * s.NX
    return s


def place(s):
    r, z = lax.axis_index("rows"), lax.axis_index("feat")
    return r, z, r // (2 * s.NX), (r // 2) % s.NX, r % 2


def row_at(s, y, x, c):
    return (y * s.NX + x) * 2 + c


def greet(s, r, z):
    barrier = pltpu.get_barrier_semaphore()
    peers = [((r + d) % s.R, z) for d in range(1, s.R)] + [(r, (z + d) % s.Z) for d in range(1, s.Z)]
    for peer in peers:
        pl.semaphore_signal(barrier, inc=1, device_id=peer, device_id_type=MESH)
    pl.semaphore_wait(barrier, len(peers))


def remote(src, dst, send, recv, device):
    return pltpu.make_async_remote_copy(
        src_ref=src, dst_ref=dst, send_sem=send, recv_sem=recv, device_id=device, device_id_type=MESH
    )


def dot(a, b, dims=((1,), (0,))):
    return lax.dot_general(a, b, (dims, ((), ())), preferred_element_type=F32)


NT = ((1,), (1,))
TN = ((0,), (0,))


def norm_parts(v):
    center = jnp.mean(v, axis=-1, keepdims=True)
    shifted = v - center
    spread = jnp.mean(shifted * shifted, axis=-1, keepdims=True)
    inv = lax.rsqrt(spread + EPS_NORM)
    return shifted * inv, inv


def weight_gather(s, h, r, z, y, x, c):
    half = s.PR // 2
    F, piece = h.whole, h.piece
    rows = (pl.ds(0, half), pl.ds(half, half))

    def z_copies(u):
        return [
            remote(
                piece.at[u // s.NU, u % s.NU],
                F.at[u, s.Z - d - 1, y, x, c],
                h.z_send.at[u % RING, d - 1],
                h.z_recv.at[u, s.Z - d - 1],
                (r, (z + d) % s.Z),
            )
            for d in range(1, s.Z)
        ]

    def first(u):
        out = []
        for d in range(1, s.NX):
            at = F.at[u, :, y, x, c, rows[0]]
            out.append(remote(at, at, h.x_send.at[u % RING, 0, d - 1], h.x_recv.at[u, 0, s.NX - d - 1],
                              (row_at(s, y, (x + d) % s.NX, c), z)))
        for d in range(1, s.NY):
            at = F.at[u, :, y, x, c, rows[1]]
            out.append(remote(at, at, h.y_send.at[u % RING, 0, d - 1], h.y_recv.at[u, 0, s.NY - d - 1],
                              (row_at(s, (y + d) % s.NY, x, c), z)))
        return out

    def first_landing(u):
        out = []
        for d in range(1, s.NX):
            at = F.at[u, :, y, (x + d) % s.NX, c, rows[0]]
            out.append(remote(at, at, h.x_send.at[u % RING, 0, d - 1], h.x_recv.at[u, 0, d - 1], (r, z)))
        for d in range(1, s.NY):
            at = F.at[u, :, (y + d) % s.NY, x, c, rows[1]]
            out.append(remote(at, at, h.y_send.at[u % RING, 0, d - 1], h.y_recv.at[u, 0, d - 1], (r, z)))
        return out

    def second(u):
        out = []
        for d in range(1, s.NY):
            at = F.at[u, :, y, :, c, rows[0]]
            out.append(remote(at, at, h.y_send.at[u % RING, 1, d - 1], h.y_recv.at[u, 1, s.NY - d - 1],
                              (row_at(s, (y + d) % s.NY, x, c), z)))
        for d in range(1, s.NX):
            at = F.at[u, :, :, x, c, rows[1]]
            out.append(remote(at, at, h.x_send.at[u % RING, 1, d - 1], h.x_recv.at[u, 1, s.NX - d - 1],
                              (row_at(s, y, (x + d) % s.NX, c), z)))
        return out

    def second_landing(u):
        out = []
        for d in range(1, s.NY):
            at = F.at[u, :, (y + d) % s.NY, :, c, rows[0]]
            out.append(remote(at, at, h.y_send.at[u % RING, 1, d - 1], h.y_recv.at[u, 1, d - 1], (r, z)))
        for d in range(1, s.NX):
            at = F.at[u, :, :, (x + d) % s.NX, c, rows[1]]
            out.append(remote(at, at, h.x_send.at[u % RING, 1, d - 1], h.x_recv.at[u, 1, d - 1], (r, z)))
        return out

    def share(u):
        at = F.at[u, :, :, :, c]
        return remote(at, at, h.c_send.at[u % RING], h.c_recv.at[u], (row_at(s, y, x, 1 - c), z))

    def share_landing(u):
        at = F.at[u, :, :, :, 1 - c]
        return remote(at, at, h.c_send.at[u % RING], h.c_recv.at[u], (r, z))

    reach = s.Z // 2

    def straight(d):
        return jnp.abs((z + d) % s.Z - z) <= reach

    def z_begin(u):
        for d, cp in zip(range(1, s.Z), z_copies(u)):
            pl.when(straight(d))(cp.start)

    def z_sent(u):
        for d, cp in zip(range(1, s.Z), z_copies(u)):
            pl.when(straight(d))(cp.wait_send)

    def relays(u):
        out = []
        for e in range(1, reach):
            to = jnp.where(z >= reach, z + e, z - e)
            slot = jnp.where(z >= reach, reach - e - 1, reach + e - 1)
            cp = remote(F.at[u, reach - 1, y, x, c], F.at[u, slot, y, x, c], h.relay_send.at[u % RING, e - 1],
                        h.z_recv.at[u, slot], (r, to))
            out.append(((to >= 0) & (to < s.Z), cp))
        return out

    def relay_begin(u):
        z_landing(u, reach - 1).wait_recv()
        for inner, cp in relays(u):
            pl.when(inner)(cp.start)

    def relay_sent(u):
        for inner, cp in relays(u):
            pl.when(inner)(cp.wait_send)

    def z_landing(u, k):
        return remote(piece.at[0, 0], F.at[u, k, y, x, c], h.z_send.at[u % RING, 0], h.z_recv.at[u, k], (r, z))

    def inside(u, what):
        pl.when((u >= 0) & (u < s.U))(functools.partial(what, u))

    def stage_z(u):
        z_begin(u)

    def stage_first(u):
        for k in range(s.Z - 1):
            if k != reach - 1:
                z_landing(u, k).wait_recv()
        for cp in first(u):
            cp.start()

    def stage_second(u):
        for cp in first_landing(u):
            cp.wait_recv()
        for cp in second(u):
            cp.start()

    def stage_core(u):
        for cp in second_landing(u):
            cp.wait_recv()
        share(u).start()

    def stage_ready(u):
        share_landing(u).wait_recv()

    def tick(t):
        inside(t - RING, z_sent)
        inside(t, stage_z)
        inside(t - 1 - RING, relay_sent)
        inside(t - 1, relay_begin)
        inside(t - LAG_FIRST - RING, lambda u: [cp.wait_send() for cp in first(u)] and None)
        inside(t - LAG_FIRST, stage_first)
        inside(t - LAG_SECOND - RING, lambda u: [cp.wait_send() for cp in second(u)] and None)
        inside(t - LAG_SECOND, stage_second)
        inside(t - LAG_CORE - RING, lambda u: share(u).wait_send())
        inside(t - LAG_CORE, stage_core)
        inside(t - LAG_READY, stage_ready)

    def drain_all():
        @pl.loop(s.U + LAG_READY, s.U + LAG_CORE + RING)
        def _(t):
            tick(t)

    return tick, drain_all


def head_masks(s):
    lane = lax.broadcasted_iota(jnp.int32, (1, 128), 1)
    first = lane < HD
    return first, jnp.where(first, 1.0, 0.0), jnp.where(first, 0.0, 1.0)


def pair_ones():
    row = lax.broadcasted_iota(jnp.int32, (128, 128), 0) // HD
    col = lax.broadcasted_iota(jnp.int32, (128, 128), 1) // HD
    return jnp.where(row == col, 1.0, 0.0).astype(BF)


def lanes(at, width):
    return pl.ds(pl.multiple_of(at * width, width), width)


def prefix_rounds(s, h, l, r, z, way):
    at = way * s.L + l
    msg, got, rows_got, back, out = h.msg, h.r1, h.r2, h.pre, h.r3

    def one(k):
        return remote(msg.at[k], got.at[s.Z - k], h.r1_send.at[at, k], h.r1_recv.at[at, s.Z - k], (r, (z + k) % s.Z))

    def two(d):
        return remote(rows_got.at[r], rows_got.at[r], h.r2_send.at[at, d], h.r2_recv.at[at, s.R - d],
                      ((r + d) % s.R, z))

    def two_landing(d):
        spot = rows_got.at[(r + d) % s.R]
        return remote(spot, spot, h.r2_send.at[at, d], h.r2_recv.at[at, d], (r, z))

    def three(k):
        return remote(back.at[k], out.at[s.Z - k], h.r3_send.at[at, k], h.r3_recv.at[at, s.Z - k], (r, (z + k) % s.Z))

    def round_one():
        for k in range(1, s.Z):
            one(k).start()

    def round_two():
        for k in range(1, s.Z):
            remote(msg.at[k], got.at[k], h.r1_send.at[at, k], h.r1_recv.at[at, k], (r, z)).wait_recv()
        total = h.coef_a[way * s.Z] * msg[0].astype(F32)
        for k in range(1, s.Z):
            total = total + h.coef_a[way * s.Z + k] * got[k].astype(F32)
        rows_got[r] = total.astype(BF)
        for d in range(1, s.R):
            two(d).start()

    def round_three():
        for d in range(1, s.R):
            two_landing(d).wait_recv()
        for k in range(s.Z):
            total = h.coef_b[(way * s.Z + k) * s.Z] * msg[0].astype(F32)
            for j in range(1, s.Z):
                total = total + h.coef_b[(way * s.Z + k) * s.Z + j] * got[j].astype(F32)
            for q in range(s.R):
                total = total + h.coef_c[(way * s.Z + k) * s.R + q] * rows_got[q].astype(F32)
            if k == 0:
                out[0] = total.astype(BF)
            else:
                back[k] = total.astype(BF)
                three(k).start()

    def arrive():
        for k in range(1, s.Z):
            remote(back.at[k], out.at[k], h.r3_send.at[at, k], h.r3_recv.at[at, k], (r, z)).wait_recv()

    def settle():
        for k in range(1, s.Z):
            one(k).wait_send()
            three(k).wait_send()
        for d in range(1, s.R):
            two(d).wait_send()

    return round_one, round_two, round_three, arrive, settle


def weigh_kernel(s, length, begin, gain, bias, coef_a, coef_b, coef_c, gain_out, bias_out):
    r, z = lax.axis_index("rows"), lax.axis_index("feat")
    for l in range(s.L):
        gain_out[2 * l:2 * l + 2] = gain[l]
        bias_out[2 * l:2 * l + 2] = bias[l]
    rows = range(s.R)
    turn = [(z + k) % s.Z for k in range(s.Z)]
    spots = [(r * s.Z + k) * s.T for k in turn] + [(r * s.Z + s.Z - 1) * s.T, r * s.Z * s.T]
    spots += [(q * s.Z + s.Z - 1) * s.T for q in rows] + [q * s.Z * s.T for q in rows]

    def count(n, begun):
        start, live = begin[n], jnp.where(length[n] > 0, 1, 0)
        return tuple(v + jnp.where(start <= at, live, 0) for v, at in zip(begun, spots))

    found = lax.fori_loop(0, begin.shape[0], count, tuple(jnp.int32(0) for _ in spots))
    mine, ends, row_ends = found[:s.Z], found[s.Z:s.Z + 2], (found[s.Z + 2:s.Z + 2 + s.R], found[s.Z + 2 + s.R:])
    for way in range(2):
        for k in range(s.Z):
            coef_a[way * s.Z + k] = jnp.where(mine[k] == ends[way], 1.0, 0.0)
            for j in range(s.Z):
                order = turn[j] < turn[k] if way == 0 else turn[j] > turn[k]
                coef_b[(way * s.Z + k) * s.Z + j] = jnp.where((mine[k] == mine[j]) & order, 1.0, 0.0)
            for q in rows:
                order = q < r if way == 0 else q > r
                coef_c[(way * s.Z + k) * s.R + q] = jnp.where((mine[k] == row_ends[way][q]) & order, 1.0, 0.0)


def weigh_units(s, image_length, image_start, gain, bias):
    vmem = pl.BlockSpec(memory_space=pltpu.VMEM)
    smem = pl.BlockSpec(memory_space=pltpu.SMEM)
    shape = jax.ShapeDtypeStruct
    return pl.pallas_call(
        functools.partial(weigh_kernel, s),
        out_shape=[shape((2 * s.Z,), F32), shape((2 * s.Z * s.Z,), F32), shape((2 * s.Z * s.R,), F32),
                   shape((2 * s.L, s.D), F32), shape((2 * s.L, s.D), F32)],
        in_specs=[smem] * 2 + [vmem] * 2,
        out_specs=[smem] * 3 + [vmem] * 2,
    )(image_length, image_start, gain, bias)


def pack_state(full, first):
    return jnp.where(first, full[:HD], full[HD:])


def unpack_state(packed, first):
    zero = jnp.zeros_like(packed)
    return jnp.concatenate([jnp.where(first, packed, zero), jnp.where(first, zero, packed)], axis=0)


def spread_rows(s, rows_list):
    at = lax.broadcasted_iota(jnp.int32, (16, 128), 0)
    block = jnp.zeros((16, 128), F32)
    for i, row in enumerate(rows_list):
        block = block + jnp.where(at == i, row, 0.0)
    return block


def pick_row(block, i):
    at = lax.broadcasted_iota(jnp.int32, (16, 128), 0)
    return jnp.sum(jnp.where(at == i, block.astype(F32), 0.0), axis=0, keepdims=True)


class Inputs(typing.NamedTuple):
    tokens: object
    cotangent: object
    gain: object
    bias: object
    coef_a: object
    coef_b: object
    coef_c: object
    w_in: object
    w_mix: object
    w_up: object
    w_down: object


class Outputs(typing.NamedTuple):
    output: object
    grad: object
    vector: object
    g_in: object
    g_mix: object
    g_up: object
    g_down: object
    whole: object
    k_stream: object
    k_middle: object
    k_qkv: object
    k_mixed: object
    k_den: object
    k_state: object
    k_act: object
    k_slope: object
    k_normt: object
    s_mixed: object
    s_act: object


def forward_scratch(s):
    dma = pltpu.SemaphoreType.DMA
    return dict(
        logs=pltpu.VMEM((8, 128), F32),
        piece=pltpu.VMEM((s.L, s.NU, s.PR, s.PC), BF),
        w=pltpu.VMEM((s.Z, s.NY, s.NX, 2, s.PR, s.PC), BF),
        stream=pltpu.VMEM((s.T, s.D), F32),
        acc=pltpu.VMEM((s.T, s.D), F32),
        middle=pltpu.VMEM((s.T, s.D), F32),
        den=pltpu.VMEM((s.T, s.D), F32),
        nrm=pltpu.VMEM((s.T, s.D), BF),
        nrmt=pltpu.VMEM((2, s.NY, s.NX, 2, s.PR, s.T), BF),
        qkv=pltpu.VMEM((3, s.T, s.D), BF),
        mixed=pltpu.VMEM((s.T, s.D), BF),
        act=pltpu.VMEM((s.NJ, s.T, s.D), BF),
        slope=pltpu.VMEM((s.NJ, s.T, s.D), BF),
        msg=pltpu.VMEM((s.Z, s.MR, 128), BF),
        r1=pltpu.VMEM((s.Z, s.MR, 128), BF),
        r2=pltpu.VMEM((s.R, s.MR, 128), BF),
        pre=pltpu.VMEM((s.Z, s.MR, 128), BF),
        r3=pltpu.VMEM((s.Z, s.MR, 128), BF),
        piece_sem=dma((2 + 2 * s.NJ,)),
        w_sem=dma((s.Z,)),
        z_send=dma((RING, s.Z - 1)),
        z_recv=dma((s.U, s.Z - 1)),
        relay_send=dma((RING, max(s.Z // 2 - 1, 1))),
        x_send=dma((RING, 2, s.NX - 1)),
        x_recv=dma((s.U, 2, s.NX - 1)),
        y_send=dma((RING, 2, s.NY - 1)),
        y_recv=dma((s.U, 2, s.NY - 1)),
        c_send=dma((RING,)),
        c_recv=dma((s.U,)),
        r1_send=dma((2 * s.L, s.Z)),
        r1_recv=dma((2 * s.L, s.Z)),
        r2_send=dma((2 * s.L, s.R)),
        r2_recv=dma((2 * s.L, s.R)),
        r3_send=dma((2 * s.L, s.Z)),
        r3_recv=dma((2 * s.L, s.Z)),
        keep=dma((8,)),
        keep_j=dma((2, s.NJ)),
        sib_send=dma((3 + s.NJ,)),
        sib_recv=dma((s.L, 3 + s.NJ)),
    )


def forward_part(s, h, spots, tick, with_unit, early):
    r, z, y, x, c = spots
    sibling = (row_at(s, y, x, 1 - c), z)
    first, _, _ = head_masks(s)

    def normalize(l, n, source):
        xhat, _ = norm_parts(source)
        v = xhat * h.gain[pl.ds(l * 2 + n, 1), :] + h.bias[pl.ds(l * 2 + n, 1), :]
        h.nrm[...] = v.astype(BF)
        h.nrmt[n] = v.T.astype(BF).reshape(s.NY, s.NX, 2, s.PR, s.T)
        keep_norm(l, n).start()
        send_norm(l, n).start()

    def keep_norm(l, n):
        return pltpu.make_async_copy(h.nrmt.at[n, :, :, c], h.k_normt.at[l, n, 0], h.keep.at[n])

    def send_norm(l, n):
        return remote(h.nrmt.at[n, :, :, 1 - c], h.k_normt.at[l, n, 1], h.sib_send.at[n], h.sib_recv.at[l, n],
                      sibling)

    def keep_one(l, index):
        src, dst = ((h.stream, h.k_stream), (h.qkv, h.k_qkv), (h.mixed, h.k_mixed), (h.den, h.k_den),
                    (h.middle, h.k_middle), (h.r3, h.k_state))[index - 2]
        return pltpu.make_async_copy(src, dst.at[l], h.keep.at[index])

    def send_mixed(l):
        return remote(h.mixed, h.s_mixed.at[l], h.sib_send.at[2], h.sib_recv.at[l, 2], sibling)

    def keep_act(l, j):
        return pltpu.make_async_copy(h.act.at[j], h.k_act.at[l, j], h.keep_j.at[0, j])

    def keep_slope(l, j):
        return pltpu.make_async_copy(h.slope.at[j], h.k_slope.at[l, j], h.keep_j.at[1, j])

    def send_act(l, j):
        return remote(h.act.at[j], h.s_act.at[l, j], h.sib_send.at[3 + j], h.sib_recv.at[l, 3 + j], sibling)

    ones = pair_ones()
    tall = jnp.ones((s.T, 128), BF)
    h.logs[...] = jnp.where(lax.broadcasted_iota(jnp.int32, (8, 128), 0) == 1, -jnp.inf, 0.0)
    tick(0)
    tick(1)
    early()
    tick(2)
    h.stream[...] = h.tokens[...].astype(F32)

    @pl.loop(3, LAG_READY)
    def _(t):
        tick(t)

    def one_layer(l, carry):
        base = l * s.NU
        keep_one(l, 2).start()
        normalize(l, 0, h.stream[...])

        def project(kind, carry):
            u = base + kind

            def body(k, weight):
                v = dot(h.nrm[...], weight)
                phi = jnp.where(v > 0, v + 1.0, jnp.exp(jnp.minimum(v, 0.0)))
                h.qkv[kind, :, lanes(k, s.PC)] = jnp.where(kind < 2, phi, v).astype(BF)

            with_unit(h.w_in, l, kind, u, body, lambda: tick(u + LAG_READY))
            return carry

        lax.fori_loop(0, 3, project, 0)
        keep_one(l, 3).start()
        round_one, round_two, round_three, arrive, settle = prefix_rounds(s, h, l, r, z, 0)

        def local_state(k, carry):
            totals = []
            for i in range(s.NP):
                at = lanes(k * s.NP + i, 128)
                keys, vals = h.qkv[1, :, at], h.qkv[2, :, at]
                h.msg[k, i * HD:(i + 1) * HD] = pack_state(dot(keys, vals, TN), first).astype(BF)
                totals.append(jnp.sum(keys.astype(F32), axis=0, keepdims=True))
            h.msg[k, s.NP * HD:] = spread_rows(s, totals).astype(BF)
            return carry

        lax.fori_loop(0, s.Z, local_state, 0)
        round_one()
        causal = (lax.broadcasted_iota(jnp.int32, (s.T, s.T), 1) <= lax.broadcasted_iota(jnp.int32, (s.T, s.T), 0))

        def attend(p, carry):
            at = lanes(p, 128)
            query, key, value = h.qkv[0, :, at], h.qkv[1, :, at], h.qkv[2, :, at]
            value_ones = jnp.concatenate([value, tall], axis=1)
            zero = jnp.zeros_like(query)
            results = []
            for head in range(2):
                mine = first if head == 0 else jnp.logical_not(first)
                scores = dot(jnp.where(mine, query, zero), key, NT)
                weights = jnp.where(causal, scores, 0.0).astype(BF)
                results.append(dot(weights, value_ones))
            h.acc[:, at] = jnp.where(first, results[0][:, :128], results[1][:, :128])
            h.den[:, at] = jnp.where(first, results[0][:, 128:], results[1][:, 128:])
            return carry

        def look_back(p, carry):
            k, i = p // s.NP, p % s.NP
            at = lanes(p, 128)
            query = h.qkv[0, :, at]
            state = unpack_state(h.r3[k, pl.ds(pl.multiple_of(i * HD, HD), HD), :], first)
            total = pick_row(h.r3[k, s.NP * HD:, :], i)
            square = jnp.zeros((128, 128), BF)
            right = jnp.concatenate(
                [jnp.concatenate([state, square], axis=1), jnp.concatenate([square, ones], axis=1)], axis=0)
            left = jnp.concatenate([query, (query.astype(F32) * total).astype(BF)], axis=1)
            earlier = dot(left, right)
            den = h.den[:, at] + earlier[:, 128:] + EPS_DEN
            h.mixed[:, at] = ((h.acc[:, at] + earlier[:, :128]) / den).astype(BF)
            h.den[:, at] = den
            logs = jnp.log(den)
            h.logs[0:1] += jnp.sum(logs, axis=0, keepdims=True)
            h.logs[1:2] = jnp.maximum(h.logs[1:2], jnp.max(logs, axis=0, keepdims=True))
            return carry

        pairs = s.Z * s.NP
        cut = [pairs * i // 4 for i in range(5)]
        lax.fori_loop(cut[0], cut[1], attend, 0)
        tick(base + 3 + LAG_READY)
        round_two()
        lax.fori_loop(cut[1], cut[2], attend, 0)
        tick(base + 4 + LAG_READY)
        round_three()
        lax.fori_loop(cut[2], cut[3], attend, 0)
        tick(base + 5 + LAG_READY)
        lax.fori_loop(cut[3], cut[4], attend, 0)
        arrive()
        keep_one(l, 7).start()
        lax.fori_loop(0, pairs, look_back, 0)
        settle()
        keep_one(l, 4).start()
        send_mixed(l).start()
        keep_one(l, 5).start()

        h.acc[...] = jnp.zeros_like(h.acc)

        def mix(k, weight):
            h.acc[...] += dot(h.mixed[:, lanes(k, s.PC)], weight, NT)

        with_unit(h.w_mix, l, 0, base + 3, mix, lambda: tick(base + 6 + LAG_READY))
        h.middle[...] = h.stream[...] + h.acc[...]
        keep_one(l, 6).start()
        normalize(l, 1, h.middle[...])

        def up(j, carry):
            u = base + 4 + j

            def body(k, weight):
                v = dot(h.nrm[...], weight)
                cdf = 0.5 * (1.0 + lax.erf(v * ROOT_HALF))
                h.act[j, :, lanes(k, s.PC)] = (v * cdf).astype(BF)
                h.slope[j, :, lanes(k, s.PC)] = (cdf + v * (ROOT_TAU * jnp.exp(-0.5 * v * v))).astype(BF)

            more = (l + 1 < s.L) | (j + 1 < s.NJ)
            with_unit(h.w_up, l, j, u, body, lambda: pl.when(more)(lambda: tick(u + s.NJ - 1 + LAG_READY)))
            keep_act(l, j).start()
            keep_slope(l, j).start()
            send_act(l, j).start()
            return carry

        lax.fori_loop(0, s.NJ, up, 0)
        keep_one(l, 2).wait()
        h.stream[...] = h.middle[...]

        def down(j, carry):
            u = base + 4 + s.NJ + j

            def body(k, weight):
                h.stream[...] += dot(h.act[j, :, lanes(k, s.PC)], weight, NT)

            with_unit(h.w_down, l, j, u, body, lambda: pl.when(j == 0)(lambda: tick(u + s.NJ - 1 + LAG_READY)))
            return carry

        @pl.when(l + 1 < s.L)
        def _():
            lax.fori_loop(0, s.NJ, down, 0)

        for n in range(2):
            keep_norm(l, n).wait()
            send_norm(l, n).wait_send()
            send_norm(l, n).wait_recv()
        for index in range(3, 8):
            keep_one(l, index).wait()
        send_mixed(l).wait()

        def finish(j, carry):
            keep_act(l, j).wait()
            keep_slope(l, j).wait()
            send_act(l, j).wait()
            return carry

        lax.fori_loop(0, s.NJ, finish, 0)
        return carry

    lax.fori_loop(0, s.L, one_layer, 0)


def split_rows(s, weight_in, *rest):
    cut = (s.NY, s.NX, 2, s.PR)
    turned = jnp.transpose(weight_in, (0, 2, 1, 3)).reshape((s.L, 3) + cut + (s.PC,))
    return (turned,) + tuple(w.reshape((s.L,) + cut + w.shape[2:]) for w in rest)


BACK_FIRST, BACK_SECOND, BACK_LAST = 2, 4, 6
SLOTS = 8
OUT_RING = 4
UPS_IN_LOOP = 2
X_EARLY, X_LATE, X_DOWN, X_MIX = 0, 1, 2, 3

def backward_scratch(s):
    dma = pltpu.SemaphoreType.DMA
    half = s.PR // 2
    return dict(
        part=pltpu.VMEM((SLOTS, s.NY, s.NX, s.Z, s.PR, s.PC), BF),
        land_x1=pltpu.VMEM((SLOTS, s.NX - 1, s.NY, s.Z, half, s.PC), BF),
        land_y1=pltpu.VMEM((SLOTS, s.NY - 1, s.NX, s.Z, half, s.PC), BF),
        land_x2=pltpu.VMEM((SLOTS, s.NX - 1, s.Z, half, s.PC), BF),
        land_y2=pltpu.VMEM((SLOTS, s.NY - 1, s.Z, half, s.PC), BF),
        land_z=pltpu.VMEM((SLOTS, s.Z - 1, s.PR, s.PC), BF),
        final=pltpu.VMEM((OUT_RING, s.PR, s.PC), F32),
        resid=pltpu.VMEM((s.T, s.D), F32),
        gb=pltpu.VMEM((s.T, s.D), BF),
        turned=pltpu.VMEM((s.NY, s.NX, 2, s.PR, s.T), BF),
        xt=pltpu.VMEM((4, 2, s.NY, s.NX, s.PR, s.T), BF),
        b_act=pltpu.VMEM((2, s.T, s.D), BF),
        b_slope=pltpu.VMEM((s.T, s.D), BF),
        ug=pltpu.VMEM((s.NJ, s.T, s.D), BF),
        ug_sib=pltpu.VMEM((s.NJ, s.T, s.D), BF),
        pg=pltpu.VMEM((3, s.T, s.D), BF),
        pg_sib=pltpu.VMEM((3, s.T, s.D), BF),
        b_mixed=pltpu.VMEM((2, s.T, s.D), BF),
        rg=pltpu.VMEM((s.T, s.D), BF),
        ng=pltpu.VMEM((s.T, s.D), BF),
        dg=pltpu.VMEM((s.T, s.D), F32),
        state=pltpu.VMEM((s.Z, s.MR, 128), BF),
        vec=pltpu.VMEM((16, s.D), F32),
        v_z=pltpu.VMEM((s.Z, 16, s.D), F32),
        v_c=pltpu.VMEM((2, 16, s.D), F32),
        v_x=pltpu.VMEM((s.NX, 16, s.D), F32),
        v_y=pltpu.VMEM((s.NY, 16, s.D), F32),
        x1_send=dma((SLOTS, s.NX - 1)),
        x1_recv=dma((SLOTS, s.NX - 1)),
        y1_send=dma((SLOTS, s.NY - 1)),
        y1_recv=dma((SLOTS, s.NY - 1)),
        x2_send=dma((SLOTS, s.NX - 1)),
        x2_recv=dma((SLOTS, s.NX - 1)),
        y2_send=dma((SLOTS, s.NY - 1)),
        y2_recv=dma((SLOTS, s.NY - 1)),
        bz_send=dma((SLOTS, s.Z - 1)),
        bz_recv=dma((SLOTS, s.Z - 1)),
        out_sem=dma((OUT_RING,)),
        xt_sem=dma((2, 2, s.NQ)),
        xt_send=dma((2, s.NQ)),
        xt_recv=dma((s.L, 2, s.NQ)),
        g_send=dma((s.NJ + 3,)),
        g_recv=dma((s.L, s.NJ + 3)),
        get=dma((8,)),
        v_send=dma((4, max(s.Z, s.NX, s.NY))),
        v_recv=dma((4, max(s.Z, s.NX, s.NY))),
    )


def down_at(s, j):
    return j + jnp.maximum(j - (s.NJ - UPS_IN_LOOP), 0) if not isinstance(j, int) else j + max(j - (s.NJ - UPS_IN_LOOP), 0)


def up_at(s, j):
    return s.NJ + j if j >= UPS_IN_LOOP else down_at(s, s.NJ - UPS_IN_LOOP + j) + 1


def gradient_sums(s, h, r, z, y, x, c):
    half = s.PR // 2
    rows = (pl.ds(0, half), pl.ds(half, half))
    part = h.part

    def to_x(d):
        return (row_at(s, y, (x + d) % s.NX, c), z)

    def to_y(d):
        return (row_at(s, (y + d) % s.NY, x, c), z)

    def first(v):
        b = v % SLOTS
        return [
            remote(part.at[b, :, d, :, rows[0]], h.land_x1.at[b, s.NX - d - 1], h.x1_send.at[b, d - 1],
                   h.x1_recv.at[b, s.NX - d - 1], to_x(d)) for d in range(1, s.NX)
        ] + [
            remote(part.at[b, d, :, :, rows[1]], h.land_y1.at[b, s.NY - d - 1], h.y1_send.at[b, d - 1],
                   h.y1_recv.at[b, s.NY - d - 1], to_y(d)) for d in range(1, s.NY)
        ]

    def second(v):
        b = v % SLOTS
        return [
            remote(part.at[b, d, 0, :, rows[0]], h.land_y2.at[b, s.NY - d - 1], h.y2_send.at[b, d - 1],
                   h.y2_recv.at[b, s.NY - d - 1], to_y(d)) for d in range(1, s.NY)
        ] + [
            remote(part.at[b, 0, d, :, rows[1]], h.land_x2.at[b, s.NX - d - 1], h.x2_send.at[b, d - 1],
                   h.x2_recv.at[b, s.NX - d - 1], to_x(d)) for d in range(1, s.NX)
        ]

    def last(v):
        b = v % SLOTS
        return [
            remote(part.at[b, 0, 0, d], h.land_z.at[b, s.Z - d - 1], h.bz_send.at[b, d - 1],
                   h.bz_recv.at[b, s.Z - d - 1], (r, (z + d) % s.Z)) for d in range(1, s.Z)
        ]

    def stage_second(v):
        b = v % SLOTS
        for cp in first(v):
            cp.wait_recv()

        def add(k, carry):
            for dy in range(s.NY):
                total = part[b, dy, 0, k, :half].astype(F32)
                for i in range(s.NX - 1):
                    total = total + h.land_x1[b, i, dy, k].astype(F32)
                part[b, dy, 0, k, :half] = total.astype(BF)
            for dx in range(s.NX):
                total = part[b, 0, dx, k, half:].astype(F32)
                for i in range(s.NY - 1):
                    total = total + h.land_y1[b, i, dx, k].astype(F32)
                part[b, 0, dx, k, half:] = total.astype(BF)
            return carry

        lax.fori_loop(0, s.Z, add, 0)
        for cp in second(v):
            cp.start()

    def stage_last(v):
        b = v % SLOTS
        for cp in second(v):
            cp.wait_recv()

        def add(k, carry):
            total = part[b, 0, 0, k, :half].astype(F32)
            for i in range(s.NY - 1):
                total = total + h.land_y2[b, i, k].astype(F32)
            part[b, 0, 0, k, :half] = total.astype(BF)
            total = part[b, 0, 0, k, half:].astype(F32)
            for i in range(s.NX - 1):
                total = total + h.land_x2[b, i, k].astype(F32)
            part[b, 0, 0, k, half:] = total.astype(BF)
            return carry

        lax.fori_loop(0, s.Z, add, 0)
        for cp in last(v):
            cp.start()

    def out_copy(at, o):
        return pltpu.make_async_copy(h.final.at[o], at, h.out_sem.at[o])

    def stage_out(v):
        b, o = v % SLOTS, v % OUT_RING
        for cp in last(v):
            cp.wait_recv()

        @pl.when(v >= OUT_RING)
        def _():
            out_copy(h.g_mix.at[0], o).wait()

        total = part[b, 0, 0, 0].astype(F32)
        for i in range(s.Z - 1):
            total = total + h.land_z[b, i].astype(F32)
        h.final[o] = total
        l, q = s.L - 1 - v // s.NU, v % s.NU
        wide = 2 * s.NJ
        for j in range(s.NJ):
            pl.when(q == down_at(s, j))(functools.partial(lambda to: out_copy(to, o).start(), h.g_down.at[l, :, lanes(j, s.PC)]))
            pl.when(q == up_at(s, j))(functools.partial(lambda to: out_copy(to, o).start(), h.g_up.at[l, :, lanes(j, s.PC)]))
        pl.when(q == wide)(lambda: out_copy(h.g_mix.at[l], o).start())
        pl.when(q > wide)(lambda: out_copy(h.g_in.at[l, q - wide - 1], o).start())

    def inside(v, what):
        pl.when((v >= 0) & (v < s.U))(functools.partial(what, v))

    def wait_sends(v):
        for cp in first(v) + second(v) + last(v):
            cp.wait_send()

    def tick(t):
        def start(v):
            for cp in first(v):
                cp.start()

        inside(t - BACK_LAST, stage_out)
        inside(t - BACK_SECOND, stage_last)
        inside(t - BACK_FIRST, stage_second)
        inside(t, start)

    def produce(v, which, own, sibling):
        b = v % SLOTS
        inside(v - SLOTS, wait_sends)
        left = [h.xt[which, i].reshape(s.NQ * s.PR, s.T) for i in range(2)]

        def block(k, carry):
            at = lanes(k, s.PC)
            total = dot(left[0], own[:, at]) + dot(left[1], sibling[:, at])
            part[b, :, :, k] = total.astype(BF).reshape(s.NY, s.NX, s.PR, s.PC)
            return carry

        lax.fori_loop(0, s.Z, block, 0)
        tick(v)

    def drain():
        @pl.loop(s.U + 4, s.U + max(BACK_LAST, 4))
        def _(t):
            tick(t)

    def settle():
        @pl.loop(s.U - SLOTS, s.U)
        def _(v):
            wait_sends(v)

        for o in range(OUT_RING):
            out_copy(h.g_mix.at[0], o).wait()

    return produce, tick, drain, settle


def backward_part(s, h, spots, tick_weights, with_unit, sums):
    r, z, y, x, c = spots
    produce, tick, drain, settle_sums = sums
    sibling = (row_at(s, y, x, 1 - c), z)
    first, _, _ = head_masks(s)
    ones = pair_ones()
    tall = jnp.ones((s.T, 128), BF)
    squares = [(dy, dx) for dy in range(s.NY) for dx in range(s.NX)]

    def get(src, dst, index):
        return pltpu.make_async_copy(src, dst, h.get.at[index])

    def xt_loads(l):
        return [
            pltpu.make_async_copy(h.k_normt.at[l, n, i, (y + dy) % s.NY, (x + dx) % s.NX], h.xt.at[n, i, dy, dx],
                                  h.xt_sem.at[n, i, q])
            for n in range(2) for i in range(2) for q, (dy, dx) in enumerate(squares)
        ]

    def xt_sends(l, which):
        return [
            remote(h.turned.at[(y + dy) % s.NY, (x + dx) % s.NX, 1 - c], h.xt.at[which, 1, dy, dx],
                   h.xt_send.at[which - 2, q], h.xt_recv.at[l, which - 2, q], sibling)
            for q, (dy, dx) in enumerate(squares)
        ]

    def turn(l, which):
        wide = h.grad[...]
        h.gb[...] = wide.astype(BF)
        h.turned[...] = wide.T.astype(BF).reshape(s.NY, s.NX, 2, s.PR, s.T)
        for cp in xt_sends(l, which):
            cp.start()
        for dy, dx in squares:
            h.xt[which, 0, dy, dx] = h.turned[(y + dy) % s.NY, (x + dx) % s.NX, c]
    def g_send(l, src, dst, j, index):
        return remote(src.at[j], dst.at[j], h.g_send.at[index], h.g_recv.at[l, index], sibling)

    def norm_back(l, n):
        back = h.acc[...]
        xhat, inv = norm_parts(h.resid[...])
        at = l * 2 + n
        h.vec[pl.ds(at, 1)] = jnp.sum(back * xhat, axis=0, keepdims=True)
        h.vec[pl.ds(2 * s.L + at, 1)] = jnp.sum(back, axis=0, keepdims=True)
        scaled = back * h.gain[pl.ds(l * 2 + n, 1), :]
        mean = jnp.mean(scaled, axis=-1, keepdims=True)
        along = jnp.mean(scaled * xhat, axis=-1, keepdims=True)
        h.grad[...] += inv * (scaled - mean - xhat * along)

    def early():
        h.grad[...] = h.cotangent[...].astype(F32)
        turn(s.L - 1, X_DOWN)

    def one_layer(li, carry):
        l = s.L - 1 - li
        base = li * s.NU
        unit = l * s.NU
        loads = [
            get(h.k_qkv.at[l], h.qkv, 0),
            get(h.k_mixed.at[l], h.b_mixed.at[0], 1),
            get(h.s_mixed.at[l], h.b_mixed.at[1], 2),
            get(h.k_den.at[l], h.den, 3),
            get(h.k_state.at[l], h.state, 4),
        ]
        act_loads = lambda j: [get(h.k_act.at[l, j], h.b_act.at[0], 5), get(h.s_act.at[l, j], h.b_act.at[1], 6)]
        slope_load = lambda j: get(h.k_slope.at[l, j], h.b_slope, 7)
        for cp in act_loads(0) + [slope_load(0)] + loads + xt_loads(l):
            cp.start()
        h.acc[...] = jnp.zeros_like(h.acc)
        for cp in xt_loads(l):
            cp.wait()
        for cp in xt_sends(l, X_DOWN):
            cp.wait_recv()

        def produce_up(j):
            g_send(l, h.ug, h.ug_sib, j, j).wait_recv()
            produce(base + up_at(s, j), X_LATE, h.ug.at[j], h.ug_sib.at[j])

        def feed_back(j, carry):
            for cp in act_loads(j):
                cp.wait()
            produce(base + down_at(s, j), X_DOWN, h.b_act.at[0], h.b_act.at[1])
            slope_load(j).wait()

            def body(k, weight):
                at = lanes(k, s.PC)
                h.ug[j, :, at] = (dot(h.gb[...], weight) * h.b_slope[:, at].astype(F32)).astype(BF)

                @pl.when(li == 0)
                def _():
                    h.stream[...] += dot(h.b_act[0, :, at], weight, NT)

            u = unit + 4 + s.NJ + j
            with_unit(h.w_down, l, j, u, body, lambda: pl.when((li == 0) & (j < 2))(lambda: tick_weights(u + s.NJ - 2 + LAG_READY)))

            @pl.when(j + 1 < s.NJ)
            def _():
                for cp in act_loads(j + 1):
                    cp.start()


            @pl.when(j + 1 < s.NJ)
            def _():
                slope_load(j + 1).start()

            g_send(l, h.ug, h.ug_sib, j, j).start()
            for i in range(UPS_IN_LOOP):
                pl.when(j == s.NJ - UPS_IN_LOOP + i)(functools.partial(produce_up, i))

            def body_up(k, weight):
                h.acc[...] += dot(h.ug[j, :, lanes(k, s.PC)], weight, NT)

            with_unit(h.w_up, l, j, unit + 4 + j, body_up)
            return carry

        lax.fori_loop(0, s.NJ, feed_back, 0)
        middle = get(h.k_middle.at[l], h.resid, 5)
        middle.start()
        for cp in xt_sends(l, X_DOWN):
            cp.wait_send()
        middle.wait()
        norm_back(l, 1)
        turn(l, X_MIX)
        for cp in xt_sends(l, X_MIX):
            cp.wait_recv()
        stream = get(h.k_stream.at[l], h.resid, 5)
        stream.start()

        def body_mix(k, weight):
            h.rg[:, lanes(k, s.PC)] = dot(h.gb[...], weight).astype(BF)

        with_unit(h.w_mix, l, 0, unit + 3, body_mix)
        for cp in loads:
            cp.wait()
        round_one, round_two, round_three, arrive, settle = prefix_rounds(s, h, l, r, z, 1)

        def local_state(k, carry):
            totals = []
            for i in range(s.NP):
                at = lanes(k * s.NP + i, 128)
                query, wide = h.qkv[0, :, at], h.rg[:, at].astype(F32)
                den = h.den[:, at]
                num = (wide / den).astype(BF)
                product = wide * h.b_mixed[0, :, at].astype(F32)
                high = product.astype(BF)
                low = (product - high.astype(F32)).astype(BF)
                slope = -(dot(high, ones) + dot(low, ones)) / den
                h.ng[:, at] = num
                h.dg[:, at] = slope
                h.msg[k, i * HD:(i + 1) * HD] = pack_state(dot(query, num, TN), first).astype(BF)
                totals.append(jnp.sum(query.astype(F32) * slope, axis=0, keepdims=True))
            h.msg[k, s.NP * HD:] = spread_rows(s, totals).astype(BF)
            return carry

        lax.fori_loop(0, s.Z, local_state, 0)
        round_one()
        causal = (lax.broadcasted_iota(jnp.int32, (s.T, s.T), 1) <= lax.broadcasted_iota(jnp.int32, (s.T, s.T), 0))
        lane = lax.broadcasted_iota(jnp.int32, (1, 128), 1)

        def attend_back(p, carry):
            k, i = p // s.NP, p % s.NP
            at = lanes(p, 128)
            query, key, value, num = h.qkv[0, :, at], h.qkv[1, :, at], h.qkv[2, :, at], h.ng[:, at]
            slope = h.dg[:, at]
            high = slope.astype(BF)
            low = (slope - high.astype(F32)).astype(BF)
            zero = jnp.zeros_like(query)
            value_ones = jnp.concatenate([value, tall], axis=1)
            rows = pl.ds(pl.multiple_of(i * HD, HD), HD)
            state = unpack_state(h.state[k, rows, :], first)
            total = pick_row(h.state[k, s.NP * HD:, :], i)
            query_grad = dot(num, state, NT) + slope * total
            value_grad = key_grad = jnp.zeros_like(query_grad)
            for head in range(2):
                mine = first if head == 0 else jnp.logical_not(first)
                query_mine = jnp.where(mine, query, zero)
                num_mine = jnp.where(mine, num, zero)
                key_mine = jnp.where(mine, key, zero)
                weights = jnp.where(causal, dot(query_mine, key, NT), 0.0).astype(BF)
                extra = jnp.where(lane == head * HD, high, jnp.where(lane == head * HD + 1, low, zero))
                score = dot(jnp.concatenate([num_mine, extra], axis=1), value_ones, NT)
                score = jnp.where(causal, score, 0.0).astype(BF)
                value_grad = value_grad + dot(weights, num_mine, TN)
                query_grad = query_grad + dot(score, key_mine)
                key_grad = key_grad + dot(score, query_mine, TN)
            h.pg[0, :, at] = (query_grad * jnp.minimum(query.astype(F32), 1.0)).astype(BF)
            h.dg[:, at] = key_grad
            h.acc[:, at] = value_grad
            return carry

        def look_ahead(p, carry):
            k, i = p // s.NP, p % s.NP
            at = lanes(p, 128)
            key, value = h.qkv[1, :, at], h.qkv[2, :, at]
            after = unpack_state(h.r3[k, pl.ds(pl.multiple_of(i * HD, HD), HD), :], first)
            total_after = pick_row(h.r3[k, s.NP * HD:, :], i)
            key_grad = h.dg[:, at] + dot(value, after, NT) + total_after
            h.pg[1, :, at] = (key_grad * jnp.minimum(key.astype(F32), 1.0)).astype(BF)
            h.pg[2, :, at] = (h.acc[:, at] + dot(key, after)).astype(BF)
            return carry

        pairs = s.Z * s.NP
        cut = [pairs * i // 4 for i in range(5)]
        lax.fori_loop(cut[0], cut[1], attend_back, 0)
        produce_up(2)
        round_two()
        lax.fori_loop(cut[1], cut[2], attend_back, 0)
        produce_up(3)
        round_three()
        lax.fori_loop(cut[2], cut[3], attend_back, 0)
        lax.fori_loop(cut[3], cut[4], attend_back, 0)
        produce(base + 2 * s.NJ, X_MIX, h.b_mixed.at[0], h.b_mixed.at[1])
        arrive()
        lax.fori_loop(0, pairs, look_ahead, 0)
        settle()
        for kind in range(3):
            g_send(l, h.pg, h.pg_sib, kind, s.NJ + kind).start()
        h.acc[...] = jnp.zeros_like(h.acc)

        def project_back(kind, carry):
            def body(k, weight):
                h.acc[...] += dot(h.pg[kind, :, lanes(k, s.PC)], weight, NT)

            with_unit(h.w_in, l, kind, unit + kind, body)
            g_send(l, h.pg, h.pg_sib, kind, s.NJ + kind).wait_recv()
            produce(base + 2 * s.NJ + 1 + kind, X_EARLY, h.pg.at[kind], h.pg_sib.at[kind])
            return carry

        lax.fori_loop(0, 3, project_back, 0)
        stream.wait()
        norm_back(l, 0)
        for cp in xt_sends(l, X_MIX):
            cp.wait_send()
        for j in range(s.NJ):
            g_send(l, h.ug, h.ug_sib, j, j).wait_send()
        for kind in range(3):
            g_send(l, h.pg, h.pg_sib, kind, s.NJ + kind).wait_send()

        @pl.when(li + 1 < s.L)
        def _():
            turn(l - 1, X_DOWN)

        return carry

    def run():
        lax.fori_loop(0, s.L, one_layer, 0)
        finish()

    def finish():
        h.vec[4 * s.L:4 * s.L + 2, :128] = h.logs[0:2]
        source = h.vec[...]
        top = lax.broadcasted_iota(jnp.int32, (16, s.D), 0) == 4 * s.L + 1
        stages = (
            (h.v_z, s.Z, z, lambda d: (r, (z + d) % s.Z)),
            (h.v_c, 2, c, lambda d: sibling),
            (h.v_x, s.NX, x, lambda d: (row_at(s, y, (x + d) % s.NX, c), z)),
            (h.v_y, s.NY, y, lambda d: (row_at(s, (y + d) % s.NY, x, c), z)),
        )
        pending = []
        for i, (slots, count, me, peer) in enumerate(stages):
            slots[me] = source
            for d in range(1, count):
                at = slots.at[me]
                cp = remote(at, at, h.v_send.at[i, d], h.v_recv.at[i, count - d], peer(d))
                cp.start()
                pending.append(cp)
            tick(s.U + i)
            for d in range(1, count):
                at = slots.at[(me + d) % count]
                remote(at, at, h.v_send.at[i, d], h.v_recv.at[i, d], (r, z)).wait_recv()
            total, largest = slots[0], slots[0]
            for k in range(1, count):
                total = total + slots[k]
                largest = jnp.maximum(largest, slots[k])
            source = jnp.where(top, largest, total)
        h.vector[...] = source
        for cp in pending:
            cp.wait_send()
        drain()
        settle_sums()

    return early, run


def unit_reader(s, h):
    def own(kind, l, j):
        if kind is h.w_in:
            src = h.w_in.at[l, j]
        elif kind is h.w_mix:
            src = h.w_mix.at[l]
        else:
            src = kind.at[l, :, :, :, :, lanes(j, s.PC)]
        return pltpu.make_async_copy(src, h.w.at[0], h.w_sem.at[0])

    def load(u, k):
        return pltpu.make_async_copy(h.whole.at[u, k - 1], h.w.at[k], h.w_sem.at[k])

    def with_unit(kind, l, j, u, body, advance=lambda: None):
        own(kind, l, j).start()
        advance()
        for k in range(1, s.Z):
            load(u, k).start()
        own(kind, l, j).wait()
        body(0, h.w[0].reshape(s.D, s.PC))

        @pl.loop(1, s.Z)
        def _(k):
            load(u, k).wait()
            body(k, h.w[k].reshape(s.D, s.PC))

    return with_unit


def kernel(s, *refs):
    scratch = forward_scratch(s) | backward_scratch(s)
    names = Inputs._fields + Outputs._fields + tuple(scratch)
    h = types.SimpleNamespace(**dict(zip(names, refs, strict=True)))
    spots = r, z, y, x, c = place(s)
    pieces = [
        pltpu.make_async_copy(h.w_in.at[:, :, y, x, c], h.piece.at[:, 0:3], h.piece_sem.at[0]),
        pltpu.make_async_copy(h.w_mix.at[:, y, x, c], h.piece.at[:, 3], h.piece_sem.at[1]),
    ]
    for j in range(s.NJ):
        cols = pl.ds(j * s.PC, s.PC)
        pieces.append(pltpu.make_async_copy(h.w_up.at[:, y, x, c, :, cols], h.piece.at[:, 4 + j], h.piece_sem.at[2 + j]))
        pieces.append(pltpu.make_async_copy(h.w_down.at[:, y, x, c, :, cols], h.piece.at[:, 4 + s.NJ + j],
                                            h.piece_sem.at[2 + s.NJ + j]))
    for cp in pieces:
        cp.start()
    greet(s, r, z)
    for cp in pieces:
        cp.wait()
    tick_weights, drain_weights = weight_gather(s, h, r, z, y, x, c)
    with_unit = unit_reader(s, h)
    sums = gradient_sums(s, h, r, z, y, x, c)
    early, backward = backward_part(s, h, spots, tick_weights, with_unit, sums)

    def before():
        h.vec[...] = jnp.zeros_like(h.vec)
        early()

    forward_part(s, h, spots, tick_weights, with_unit, before)
    backward()
    h.output[...] = h.stream[...].astype(BF)
    drain_weights()


def call(s, arrays):
    vmem = pl.BlockSpec(memory_space=pltpu.VMEM)
    smem = pl.BlockSpec(memory_space=pltpu.SMEM)
    hbm = pl.BlockSpec(memory_space=pl.ANY)
    shape = jax.ShapeDtypeStruct
    outs = Outputs(
        output=shape((s.T, s.D), BF),
        grad=shape((s.T, s.D), F32),
        vector=shape((16, s.D), F32),
        g_in=shape((s.L, 3, s.PR, s.PC), F32),
        g_mix=shape((s.L, s.PR, s.PC), F32),
        g_up=shape((s.L, s.PR, s.NJ * s.PC), F32),
        g_down=shape((s.L, s.PR, s.NJ * s.PC), F32),
        whole=shape((s.U, s.Z - 1, s.NY, s.NX, 2, s.PR, s.PC), BF),
        k_stream=shape((s.L, s.T, s.D), F32),
        k_middle=shape((s.L, s.T, s.D), F32),
        k_qkv=shape((s.L, 3, s.T, s.D), BF),
        k_mixed=shape((s.L, s.T, s.D), BF),
        k_den=shape((s.L, s.T, s.D), F32),
        k_state=shape((s.L, s.Z, s.MR, 128), BF),
        k_act=shape((s.L, s.NJ, s.T, s.D), BF),
        k_slope=shape((s.L, s.NJ, s.T, s.D), BF),
        k_normt=shape((s.L, 2, 2, s.NY, s.NX, s.PR, s.T), BF),
        s_mixed=shape((s.L, s.T, s.D), BF),
        s_act=shape((s.L, s.NJ, s.T, s.D), BF),
    )
    scratch = forward_scratch(s) | backward_scratch(s)
    out = pl.pallas_call(
        functools.partial(kernel, s),
        out_shape=list(outs),
        in_specs=[vmem] * 4 + [smem] * 3 + [hbm] * 4,
        out_specs=[vmem] * 3 + [hbm] * (len(outs) - 3),
        scratch_shapes=list(scratch.values()),
        compiler_params=pltpu.CompilerParams(
            collective_id=0, has_side_effects=True, vmem_limit_bytes=61 * 1024 * 1024),
    )(*arrays)
    return Outputs(*out)


def finish_kernel(s, count, *refs):
    sources, vector, results = refs[:count], refs[count], refs[count + 1:2 * count + 1]
    gain, bias, top, log_max, log_mean, sems = refs[2 * count + 1:2 * count + 7]
    held = refs[2 * count + 7:]
    loads = [pltpu.make_async_copy(src, mid, sems.at[0, i]) for i, (src, mid) in enumerate(zip(sources, held))]
    stores = [pltpu.make_async_copy(mid, dst, sems.at[1, i]) for i, (mid, dst) in enumerate(zip(held, results))]
    for cp in loads:
        cp.start()
    for load, store in zip(loads, stores):
        load.wait()
        store.start()
    for l in range(s.L):
        gain[l] = vector[2 * l:2 * l + 2]
        bias[l] = vector[2 * s.L + 2 * l:2 * s.L + 2 * l + 2]
    top[...] = vector[4 * s.L - 1:4 * s.L]
    logs = s.R * s.Z * s.T * s.D * s.L
    log_mean[...] = jnp.sum(vector[4 * s.L:4 * s.L + 1, :128], axis=1, keepdims=True) / logs
    log_max[...] = jnp.max(vector[4 * s.L + 1:4 * s.L + 2, :128], axis=1, keepdims=True)
    for cp in stores:
        cp.wait()


def finish(s, got):
    vmem = pl.BlockSpec(memory_space=pltpu.VMEM)
    hbm = pl.BlockSpec(memory_space=pl.ANY)
    shape = jax.ShapeDtypeStruct
    large = (got.output, got.grad, got.g_in, got.g_mix, got.g_up, got.g_down)
    return pl.pallas_call(
        functools.partial(finish_kernel, s, len(large)),
        out_shape=[shape(a.shape, a.dtype) for a in large] + [
            shape((s.L, 2, s.D), F32), shape((s.L, 2, s.D), F32), shape((1, s.D), F32), shape((1, 1), F32), shape((1, 1), F32)],
        in_specs=[hbm] * len(large) + [vmem],
        out_specs=[hbm] * len(large) + [vmem] * 5,
        scratch_shapes=[pltpu.SemaphoreType.DMA((2, len(large)))] + [pltpu.VMEM(a.shape, a.dtype) for a in large],
        compiler_params=pltpu.CompilerParams(vmem_limit_bytes=61 * 1024 * 1024),
    )(*large, got.vector)


def local(mesh, tokens, cotangent, image_length, image_start, norm_gain, norm_bias, weight_in, weight_mix, weight_up,
          weight_down):
    s = sizes_of(mesh, tokens, weight_in, weight_up)
    weights = split_rows(s, weight_in, weight_mix, weight_up, weight_down)
    *coefs, gain, bias = weigh_units(s, image_length, image_start, norm_gain, norm_bias)
    got = call(s, Inputs(tokens, cotangent, gain, bias, *coefs, *weights))
    output, grad, g_in, g_mix, g_up, g_down, grad_gain, grad_bias, top, log_max, log_mean = finish(s, got)
    return (output, grad, grad_gain, grad_bias, top.reshape(-1), jnp.transpose(g_in, (0, 2, 1, 3)), g_mix, g_up, g_down,
            log_max.reshape(()), log_mean.reshape(()))


def solution(mesh):
    pixels = P(("rows", "feat"), None)
    placed = (pixels, pixels, P(), P(), P(), P(), P(None, None, None, "feat"), P(None, None, "feat"), P(None, None, "feat"),
              P(None, None, "feat"))
    return jax.shard_map(
        functools.partial(local, mesh),
        mesh=mesh,
        in_specs=placed,
        out_specs=(pixels, pixels, P(), P(), P(), P(None, "rows", None, "feat"), P(None, "rows", "feat"),
                   P(None, "rows", "feat"), P(None, "rows", "feat"), P(), P()),
        check_vma=False,
    )
```

```python
import functools
import types
import typing

import jax
import jax.numpy as jnp
from jax import lax
from jax.experimental import pallas as pl
from jax.experimental.pallas import tpu as pltpu
from jax.sharding import PartitionSpec as P

HD = 64
EPS_NORM = 1e-05
EPS_DEN = 1e-06
MESH = pl.DeviceIdType.MESH
BF = jnp.bfloat16
F32 = jnp.float32
LAG_FIRST, LAG_SECOND, LAG_CORE, LAG_READY = 2, 3, 4, 5
RING = 4
ROOT_HALF = 0.7071067811865476
ROOT_TAU = 0.3989422804014327


def sizes_of(mesh, tokens, weight_in, weight_up):
    s = types.SimpleNamespace()
    s.R, s.Z = mesh.shape["rows"], mesh.shape["feat"]
    chips = s.R // 2
    s.NX = 1
    while s.NX * s.NX < chips:
        s.NX *= 2
    s.NY = chips // s.NX
    s.T, s.D = tokens.shape
    s.L = weight_in.shape[0]
    s.PC = weight_in.shape[3]
    s.PR = s.D // s.R
    s.NJ = weight_up.shape[2] // s.PC
    s.NU = 4 + 2 * s.NJ
    s.U = s.L * s.NU
    s.NP = s.PC // 128
    s.MR = s.NP * HD + 16
    s.NQ = s.NY * s.NX
    return s


def place(s):
    r, z = lax.axis_index("rows"), lax.axis_index("feat")
    return r, z, r // (2 * s.NX), (r // 2) % s.NX, r % 2


def row_at(s, y, x, c):
    return (y * s.NX + x) * 2 + c


def greet(s, r, z):
    barrier = pltpu.get_barrier_semaphore()
    peers = [((r + d) % s.R, z) for d in range(1, s.R)] + [(r, (z + d) % s.Z) for d in range(1, s.Z)]
    for peer in peers:
        pl.semaphore_signal(barrier, inc=1, device_id=peer, device_id_type=MESH)
    pl.semaphore_wait(barrier, len(peers))


def remote(src, dst, send, recv, device):
    return pltpu.make_async_remote_copy(
        src_ref=src, dst_ref=dst, send_sem=send, recv_sem=recv, device_id=device, device_id_type=MESH
    )


def dot(a, b, dims=((1,), (0,))):
    return lax.dot_general(a, b, (dims, ((), ())), preferred_element_type=F32)


NT = ((1,), (1,))
TN = ((0,), (0,))


def norm_parts(v):
    center = jnp.mean(v, axis=-1, keepdims=True)
    shifted = v - center
    spread = jnp.mean(shifted * shifted, axis=-1, keepdims=True)
    inv = lax.rsqrt(spread + EPS_NORM)
    return shifted * inv, inv


def weight_gather(s, h, r, z, y, x, c):
    half = s.PR // 2
    F, piece = h.whole, h.piece
    rows = (pl.ds(0, half), pl.ds(half, half))

    def z_copies(u):
        return [
            remote(
                piece.at[u // s.NU, u % s.NU],
                F.at[u, s.Z - d - 1, y, x, c],
                h.z_send.at[u % RING, d - 1],
                h.z_recv.at[u, s.Z - d - 1],
                (r, (z + d) % s.Z),
            )
            for d in range(1, s.Z)
        ]

    def first(u):
        out = []
        for d in range(1, s.NX):
            at = F.at[u, :, y, x, c, rows[0]]
            out.append(remote(at, at, h.x_send.at[u % RING, 0, d - 1], h.x_recv.at[u, 0, s.NX - d - 1],
                              (row_at(s, y, (x + d) % s.NX, c), z)))
        for d in range(1, s.NY):
            at = F.at[u, :, y, x, c, rows[1]]
            out.append(remote(at, at, h.y_send.at[u % RING, 0, d - 1], h.y_recv.at[u, 0, s.NY - d - 1],
                              (row_at(s, (y + d) % s.NY, x, c), z)))
        return out

    def first_landing(u):
        out = []
        for d in range(1, s.NX):
            at = F.at[u, :, y, (x + d) % s.NX, c, rows[0]]
            out.append(remote(at, at, h.x_send.at[u % RING, 0, d - 1], h.x_recv.at[u, 0, d - 1], (r, z)))
        for d in range(1, s.NY):
            at = F.at[u, :, (y + d) % s.NY, x, c, rows[1]]
            out.append(remote(at, at, h.y_send.at[u % RING, 0, d - 1], h.y_recv.at[u, 0, d - 1], (r, z)))
        return out

    def second(u):
        out = []
        for d in range(1, s.NY):
            at = F.at[u, :, y, :, c, rows[0]]
            out.append(remote(at, at, h.y_send.at[u % RING, 1, d - 1], h.y_recv.at[u, 1, s.NY - d - 1],
                              (row_at(s, (y + d) % s.NY, x, c), z)))
        for d in range(1, s.NX):
            at = F.at[u, :, :, x, c, rows[1]]
            out.append(remote(at, at, h.x_send.at[u % RING, 1, d - 1], h.x_recv.at[u, 1, s.NX - d - 1],
                              (row_at(s, y, (x + d) % s.NX, c), z)))
        return out

    def second_landing(u):
        out = []
        for d in range(1, s.NY):
            at = F.at[u, :, (y + d) % s.NY, :, c, rows[0]]
            out.append(remote(at, at, h.y_send.at[u % RING, 1, d - 1], h.y_recv.at[u, 1, d - 1], (r, z)))
        for d in range(1, s.NX):
            at = F.at[u, :, :, (x + d) % s.NX, c, rows[1]]
            out.append(remote(at, at, h.x_send.at[u % RING, 1, d - 1], h.x_recv.at[u, 1, d - 1], (r, z)))
        return out

    def share(u):
        at = F.at[u, :, :, :, c]
        return remote(at, at, h.c_send.at[u % RING], h.c_recv.at[u], (row_at(s, y, x, 1 - c), z))

    def share_landing(u):
        at = F.at[u, :, :, :, 1 - c]
        return remote(at, at, h.c_send.at[u % RING], h.c_recv.at[u], (r, z))

    reach = s.Z // 2

    def straight(d):
        return jnp.abs((z + d) % s.Z - z) <= reach

    def z_begin(u):
        for d, cp in zip(range(1, s.Z), z_copies(u)):
            pl.when(straight(d))(cp.start)

    def z_sent(u):
        for d, cp in zip(range(1, s.Z), z_copies(u)):
            pl.when(straight(d))(cp.wait_send)

    def relays(u):
        out = []
        for e in range(1, reach):
            to = jnp.where(z >= reach, z + e, z - e)
            slot = jnp.where(z >= reach, reach - e - 1, reach + e - 1)
            cp = remote(F.at[u, reach - 1, y, x, c], F.at[u, slot, y, x, c], h.relay_send.at[u % RING, e - 1],
                        h.z_recv.at[u, slot], (r, to))
            out.append(((to >= 0) & (to < s.Z), cp))
        return out

    def relay_begin(u):
        z_landing(u, reach - 1).wait_recv()
        for inner, cp in relays(u):
            pl.when(inner)(cp.start)

    def relay_sent(u):
        for inner, cp in relays(u):
            pl.when(inner)(cp.wait_send)

    def z_landing(u, k):
        return remote(piece.at[0, 0], F.at[u, k, y, x, c], h.z_send.at[u % RING, 0], h.z_recv.at[u, k], (r, z))

    def inside(u, what):
        pl.when((u >= 0) & (u < s.U))(functools.partial(what, u))

    def stage_z(u):
        z_begin(u)

    def stage_first(u):
        for k in range(s.Z - 1):
            if k != reach - 1:
                z_landing(u, k).wait_recv()
        for cp in first(u):
            cp.start()

    def stage_second(u):
        for cp in first_landing(u):
            cp.wait_recv()
        for cp in second(u):
            cp.start()

    def stage_core(u):
        for cp in second_landing(u):
            cp.wait_recv()
        share(u).start()

    def stage_ready(u):
        share_landing(u).wait_recv()

    def tick(t):
        inside(t - RING, z_sent)
        inside(t, stage_z)
        inside(t - 1 - RING, relay_sent)
        inside(t - 1, relay_begin)
        inside(t - LAG_FIRST - RING, lambda u: [cp.wait_send() for cp in first(u)] and None)
        inside(t - LAG_FIRST, stage_first)
        inside(t - LAG_SECOND - RING, lambda u: [cp.wait_send() for cp in second(u)] and None)
        inside(t - LAG_SECOND, stage_second)
        inside(t - LAG_CORE - RING, lambda u: share(u).wait_send())
        inside(t - LAG_CORE, stage_core)
        inside(t - LAG_READY, stage_ready)

    def drain_all():
        @pl.loop(s.U + LAG_READY, s.U + LAG_CORE + RING)
        def _(t):
            tick(t)

    return tick, drain_all


def head_masks(s):
    lane = lax.broadcasted_iota(jnp.int32, (1, 128), 1)
    first = lane < HD
    return first, jnp.where(first, 1.0, 0.0), jnp.where(first, 0.0, 1.0)


def pair_ones():
    row = lax.broadcasted_iota(jnp.int32, (128, 128), 0) // HD
    col = lax.broadcasted_iota(jnp.int32, (128, 128), 1) // HD
    return jnp.where(row == col, 1.0, 0.0).astype(BF)


def lanes(at, width):
    return pl.ds(pl.multiple_of(at * width, width), width)


def prefix_rounds(s, h, l, r, z, way):
    at = way * s.L + l
    msg, got, rows_got, back, out = h.msg, h.r1, h.r2, h.pre, h.r3

    def one(k):
        return remote(msg.at[k], got.at[s.Z - k], h.r1_send.at[at, k], h.r1_recv.at[at, s.Z - k], (r, (z + k) % s.Z))

    def two(d):
        return remote(rows_got.at[r], rows_got.at[r], h.r2_send.at[at, d], h.r2_recv.at[at, s.R - d],
                      ((r + d) % s.R, z))

    def two_landing(d):
        spot = rows_got.at[(r + d) % s.R]
        return remote(spot, spot, h.r2_send.at[at, d], h.r2_recv.at[at, d], (r, z))

    def three(k):
        return remote(back.at[k], out.at[s.Z - k], h.r3_send.at[at, k], h.r3_recv.at[at, s.Z - k], (r, (z + k) % s.Z))

    def round_one():
        for k in range(1, s.Z):
            one(k).start()

    def round_two():
        for k in range(1, s.Z):
            remote(msg.at[k], got.at[k], h.r1_send.at[at, k], h.r1_recv.at[at, k], (r, z)).wait_recv()
        total = h.coef_a[way * s.Z] * msg[0].astype(F32)
        for k in range(1, s.Z):
            total = total + h.coef_a[way * s.Z + k] * got[k].astype(F32)
        rows_got[r] = total.astype(BF)
        for d in range(1, s.R):
            two(d).start()

    def round_three():
        for d in range(1, s.R):
            two_landing(d).wait_recv()
        for k in range(s.Z):
            total = h.coef_b[(way * s.Z + k) * s.Z] * msg[0].astype(F32)
            for j in range(1, s.Z):
                total = total + h.coef_b[(way * s.Z + k) * s.Z + j] * got[j].astype(F32)
            for q in range(s.R):
                total = total + h.coef_c[(way * s.Z + k) * s.R + q] * rows_got[q].astype(F32)
            if k == 0:
                out[0] = total.astype(BF)
            else:
                back[k] = total.astype(BF)
                three(k).start()

    def arrive():
        for k in range(1, s.Z):
            remote(back.at[k], out.at[k], h.r3_send.at[at, k], h.r3_recv.at[at, k], (r, z)).wait_recv()

    def settle():
        for k in range(1, s.Z):
            one(k).wait_send()
            three(k).wait_send()
        for d in range(1, s.R):
            two(d).wait_send()

    return round_one, round_two, round_three, arrive, settle


def weigh_kernel(s, length, begin, gain, bias, coef_a, coef_b, coef_c, gain_out, bias_out):
    r, z = lax.axis_index("rows"), lax.axis_index("feat")
    for l in range(s.L):
        gain_out[2 * l:2 * l + 2] = gain[l]
        bias_out[2 * l:2 * l + 2] = bias[l]
    rows = range(s.R)
    turn = [(z + k) % s.Z for k in range(s.Z)]
    spots = [(r * s.Z + k) * s.T for k in turn] + [(r * s.Z + s.Z - 1) * s.T, r * s.Z * s.T]
    spots += [(q * s.Z + s.Z - 1) * s.T for q in rows] + [q * s.Z * s.T for q in rows]

    def count(n, begun):
        start, live = begin[n], jnp.where(length[n] > 0, 1, 0)
        return tuple(v + jnp.where(start <= at, live, 0) for v, at in zip(begun, spots))

    found = lax.fori_loop(0, begin.shape[0], count, tuple(jnp.int32(0) for _ in spots))
    mine, ends, row_ends = found[:s.Z], found[s.Z:s.Z + 2], (found[s.Z + 2:s.Z + 2 + s.R], found[s.Z + 2 + s.R:])
    for way in range(2):
        for k in range(s.Z):
            coef_a[way * s.Z + k] = jnp.where(mine[k] == ends[way], 1.0, 0.0)
            for j in range(s.Z):
                order = turn[j] < turn[k] if way == 0 else turn[j] > turn[k]
                coef_b[(way * s.Z + k) * s.Z + j] = jnp.where((mine[k] == mine[j]) & order, 1.0, 0.0)
            for q in rows:
                order = q < r if way == 0 else q > r
                coef_c[(way * s.Z + k) * s.R + q] = jnp.where((mine[k] == row_ends[way][q]) & order, 1.0, 0.0)


def weigh_units(s, image_length, image_start, gain, bias):
    vmem = pl.BlockSpec(memory_space=pltpu.VMEM)
    smem = pl.BlockSpec(memory_space=pltpu.SMEM)
    shape = jax.ShapeDtypeStruct
    return pl.pallas_call(
        functools.partial(weigh_kernel, s),
        out_shape=[shape((2 * s.Z,), F32), shape((2 * s.Z * s.Z,), F32), shape((2 * s.Z * s.R,), F32),
                   shape((2 * s.L, s.D), F32), shape((2 * s.L, s.D), F32)],
        in_specs=[smem] * 2 + [vmem] * 2,
        out_specs=[smem] * 3 + [vmem] * 2,
    )(image_length, image_start, gain, bias)


def pack_state(full, first):
    return jnp.where(first, full[:HD], full[HD:])


def unpack_state(packed, first):
    zero = jnp.zeros_like(packed)
    return jnp.concatenate([jnp.where(first, packed, zero), jnp.where(first, zero, packed)], axis=0)


def spread_rows(s, rows_list):
    at = lax.broadcasted_iota(jnp.int32, (16, 128), 0)
    block = jnp.zeros((16, 128), F32)
    for i, row in enumerate(rows_list):
        block = block + jnp.where(at == i, row, 0.0)
    return block


def pick_row(block, i):
    at = lax.broadcasted_iota(jnp.int32, (16, 128), 0)
    return jnp.sum(jnp.where(at == i, block.astype(F32), 0.0), axis=0, keepdims=True)


class Inputs(typing.NamedTuple):
    tokens: object
    cotangent: object
    gain: object
    bias: object
    coef_a: object
    coef_b: object
    coef_c: object
    w_in: object
    w_mix: object
    w_up: object
    w_down: object


class Outputs(typing.NamedTuple):
    output: object
    grad: object
    vector: object
    g_in: object
    g_mix: object
    g_up: object
    g_down: object
    whole: object
    k_stream: object
    k_middle: object
    k_qkv: object
    k_mixed: object
    k_den: object
    k_state: object
    k_act: object
    k_slope: object
    k_normt: object
    s_mixed: object
    s_act: object


def forward_scratch(s):
    dma = pltpu.SemaphoreType.DMA
    return dict(
        logs=pltpu.VMEM((8, 128), F32),
        piece=pltpu.VMEM((s.L, s.NU, s.PR, s.PC), BF),
        w=pltpu.VMEM((s.Z, s.NY, s.NX, 2, s.PR, s.PC), BF),
        stream=pltpu.VMEM((s.T, s.D), F32),
        acc=pltpu.VMEM((s.T, s.D), F32),
        middle=pltpu.VMEM((s.T, s.D), F32),
        den=pltpu.VMEM((s.T, s.D), F32),
        nrm=pltpu.VMEM((s.T, s.D), BF),
        nrmt=pltpu.VMEM((2, s.NY, s.NX, 2, s.PR, s.T), BF),
        qkv=pltpu.VMEM((3, s.T, s.D), BF),
        mixed=pltpu.VMEM((s.T, s.D), BF),
        act=pltpu.VMEM((s.NJ, s.T, s.D), BF),
        slope=pltpu.VMEM((s.NJ, s.T, s.D), BF),
        msg=pltpu.VMEM((s.Z, s.MR, 128), BF),
        r1=pltpu.VMEM((s.Z, s.MR, 128), BF),
        r2=pltpu.VMEM((s.R, s.MR, 128), BF),
        pre=pltpu.VMEM((s.Z, s.MR, 128), BF),
        r3=pltpu.VMEM((s.Z, s.MR, 128), BF),
        piece_sem=dma((2 + 2 * s.NJ,)),
        w_sem=dma((s.Z,)),
        z_send=dma((RING, s.Z - 1)),
        z_recv=dma((s.U, s.Z - 1)),
        relay_send=dma((RING, max(s.Z // 2 - 1, 1))),
        x_send=dma((RING, 2, s.NX - 1)),
        x_recv=dma((s.U, 2, s.NX - 1)),
        y_send=dma((RING, 2, s.NY - 1)),
        y_recv=dma((s.U, 2, s.NY - 1)),
        c_send=dma((RING,)),
        c_recv=dma((s.U,)),
        r1_send=dma((2 * s.L, s.Z)),
        r1_recv=dma((2 * s.L, s.Z)),
        r2_send=dma((2 * s.L, s.R)),
        r2_recv=dma((2 * s.L, s.R)),
        r3_send=dma((2 * s.L, s.Z)),
        r3_recv=dma((2 * s.L, s.Z)),
        keep=dma((8,)),
        keep_j=dma((2, s.NJ)),
        sib_send=dma((3 + s.NJ,)),
        sib_recv=dma((s.L, 3 + s.NJ)),
    )


def forward_part(s, h, spots, tick, with_unit, early):
    r, z, y, x, c = spots
    sibling = (row_at(s, y, x, 1 - c), z)
    first, _, _ = head_masks(s)

    def normalize(l, n, source):
        xhat, _ = norm_parts(source)
        v = xhat * h.gain[pl.ds(l * 2 + n, 1), :] + h.bias[pl.ds(l * 2 + n, 1), :]
        h.nrm[...] = v.astype(BF)
        h.nrmt[n] = v.T.astype(BF).reshape(s.NY, s.NX, 2, s.PR, s.T)
        keep_norm(l, n).start()
        send_norm(l, n).start()

    def keep_norm(l, n):
        return pltpu.make_async_copy(h.nrmt.at[n, :, :, c], h.k_normt.at[l, n, 0], h.keep.at[n])

    def send_norm(l, n):
        return remote(h.nrmt.at[n, :, :, 1 - c], h.k_normt.at[l, n, 1], h.sib_send.at[n], h.sib_recv.at[l, n],
                      sibling)

    def keep_one(l, index):
        src, dst = ((h.stream, h.k_stream), (h.qkv, h.k_qkv), (h.mixed, h.k_mixed), (h.den, h.k_den),
                    (h.middle, h.k_middle), (h.r3, h.k_state))[index - 2]
        return pltpu.make_async_copy(src, dst.at[l], h.keep.at[index])

    def send_mixed(l):
        return remote(h.mixed, h.s_mixed.at[l], h.sib_send.at[2], h.sib_recv.at[l, 2], sibling)

    def keep_act(l, j):
        return pltpu.make_async_copy(h.act.at[j], h.k_act.at[l, j], h.keep_j.at[0, j])

    def keep_slope(l, j):
        return pltpu.make_async_copy(h.slope.at[j], h.k_slope.at[l, j], h.keep_j.at[1, j])

    def send_act(l, j):
        return remote(h.act.at[j], h.s_act.at[l, j], h.sib_send.at[3 + j], h.sib_recv.at[l, 3 + j], sibling)

    ones = pair_ones()
    tall = jnp.ones((s.T, 128), BF)
    h.logs[...] = jnp.where(lax.broadcasted_iota(jnp.int32, (8, 128), 0) == 1, -jnp.inf, 0.0)
    tick(0)
    tick(1)
    early()
    tick(2)
    h.stream[...] = h.tokens[...].astype(F32)

    @pl.loop(3, LAG_READY)
    def _(t):
        tick(t)

    def one_layer(l, carry):
        base = l * s.NU
        keep_one(l, 2).start()
        normalize(l, 0, h.stream[...])

        def project(kind, carry):
            u = base + kind

            def body(k, weight):
                v = dot(h.nrm[...], weight)
                phi = jnp.where(v > 0, v + 1.0, jnp.exp(jnp.minimum(v, 0.0)))
                h.qkv[kind, :, lanes(k, s.PC)] = jnp.where(kind < 2, phi, v).astype(BF)

            with_unit(h.w_in, l, kind, u, body, lambda: tick(u + LAG_READY))
            return carry

        lax.fori_loop(0, 3, project, 0)
        keep_one(l, 3).start()
        round_one, round_two, round_three, arrive, settle = prefix_rounds(s, h, l, r, z, 0)

        def local_state(k, carry):
            totals = []
            for i in range(s.NP):
                at = lanes(k * s.NP + i, 128)
                keys, vals = h.qkv[1, :, at], h.qkv[2, :, at]
                h.msg[k, i * HD:(i + 1) * HD] = pack_state(dot(keys, vals, TN), first).astype(BF)
                totals.append(jnp.sum(keys.astype(F32), axis=0, keepdims=True))
            h.msg[k, s.NP * HD:] = spread_rows(s, totals).astype(BF)
            return carry

        lax.fori_loop(0, s.Z, local_state, 0)
        round_one()
        causal = (lax.broadcasted_iota(jnp.int32, (s.T, s.T), 1) <= lax.broadcasted_iota(jnp.int32, (s.T, s.T), 0))

        def attend(p, carry):
            at = lanes(p, 128)
            query, key, value = h.qkv[0, :, at], h.qkv[1, :, at], h.qkv[2, :, at]
            value_ones = jnp.concatenate([value, tall], axis=1)
            zero = jnp.zeros_like(query)
            results = []
            for head in range(2):
                mine = first if head == 0 else jnp.logical_not(first)
                scores = dot(jnp.where(mine, query, zero), key, NT)
                weights = jnp.where(causal, scores, 0.0).astype(BF)
                results.append(dot(weights, value_ones))
            h.acc[:, at] = jnp.where(first, results[0][:, :128], results[1][:, :128])
            h.den[:, at] = jnp.where(first, results[0][:, 128:], results[1][:, 128:])
            return carry

        def look_back(p, carry):
            k, i = p // s.NP, p % s.NP
            at = lanes(p, 128)
            query = h.qkv[0, :, at]
            state = unpack_state(h.r3[k, pl.ds(pl.multiple_of(i * HD, HD), HD), :], first)
            total = pick_row(h.r3[k, s.NP * HD:, :], i)
            square = jnp.zeros((128, 128), BF)
            right = jnp.concatenate(
                [jnp.concatenate([state, square], axis=1), jnp.concatenate([square, ones], axis=1)], axis=0)
            left = jnp.concatenate([query, (query.astype(F32) * total).astype(BF)], axis=1)
            earlier = dot(left, right)
            den = h.den[:, at] + earlier[:, 128:] + EPS_DEN
            h.mixed[:, at] = ((h.acc[:, at] + earlier[:, :128]) / den).astype(BF)
            h.den[:, at] = den
            logs = jnp.log(den)
            h.logs[0:1] += jnp.sum(logs, axis=0, keepdims=True)
            h.logs[1:2] = jnp.maximum(h.logs[1:2], jnp.max(logs, axis=0, keepdims=True))
            return carry

        pairs = s.Z * s.NP
        cut = [pairs * i // 4 for i in range(5)]
        lax.fori_loop(cut[0], cut[1], attend, 0)
        tick(base + 3 + LAG_READY)
        round_two()
        lax.fori_loop(cut[1], cut[2], attend, 0)
        tick(base + 4 + LAG_READY)
        round_three()
        lax.fori_loop(cut[2], cut[3], attend, 0)
        tick(base + 5 + LAG_READY)
        lax.fori_loop(cut[3], cut[4], attend, 0)
        arrive()
        keep_one(l, 7).start()
        lax.fori_loop(0, pairs, look_back, 0)
        settle()
        keep_one(l, 4).start()
        send_mixed(l).start()
        keep_one(l, 5).start()

        h.acc[...] = jnp.zeros_like(h.acc)

        def mix(k, weight):
            h.acc[...] += dot(h.mixed[:, lanes(k, s.PC)], weight, NT)

        with_unit(h.w_mix, l, 0, base + 3, mix, lambda: tick(base + 6 + LAG_READY))
        h.middle[...] = h.stream[...] + h.acc[...]
        keep_one(l, 6).start()
        normalize(l, 1, h.middle[...])

        def up(j, carry):
            u = base + 4 + j

            def body(k, weight):
                v = dot(h.nrm[...], weight)
                cdf = 0.5 * (1.0 + lax.erf(v * ROOT_HALF))
                h.act[j, :, lanes(k, s.PC)] = (v * cdf).astype(BF)
                h.slope[j, :, lanes(k, s.PC)] = (cdf + v * (ROOT_TAU * jnp.exp(-0.5 * v * v))).astype(BF)

            more = (l + 1 < s.L) | (j + 1 < s.NJ)
            with_unit(h.w_up, l, j, u, body, lambda: pl.when(more)(lambda: tick(u + s.NJ - 1 + LAG_READY)))
            keep_act(l, j).start()
            keep_slope(l, j).start()
            send_act(l, j).start()
            return carry

        lax.fori_loop(0, s.NJ, up, 0)
        keep_one(l, 2).wait()
        h.stream[...] = h.middle[...]

        def down(j, carry):
            u = base + 4 + s.NJ + j

            def body(k, weight):
                h.stream[...] += dot(h.act[j, :, lanes(k, s.PC)], weight, NT)

            with_unit(h.w_down, l, j, u, body, lambda: pl.when(j == 0)(lambda: tick(u + s.NJ - 1 + LAG_READY)))
            return carry

        @pl.when(l + 1 < s.L)
        def _():
            lax.fori_loop(0, s.NJ, down, 0)

        for n in range(2):
            keep_norm(l, n).wait()
            send_norm(l, n).wait_send()
            send_norm(l, n).wait_recv()
        for index in range(3, 8):
            keep_one(l, index).wait()
        send_mixed(l).wait()

        def finish(j, carry):
            keep_act(l, j).wait()
            keep_slope(l, j).wait()
            send_act(l, j).wait()
            return carry

        lax.fori_loop(0, s.NJ, finish, 0)
        return carry

    lax.fori_loop(0, s.L, one_layer, 0)


def split_rows(s, weight_in, *rest):
    cut = (s.NY, s.NX, 2, s.PR)
    turned = jnp.transpose(weight_in, (0, 2, 1, 3)).reshape((s.L, 3) + cut + (s.PC,))
    return (turned,) + tuple(w.reshape((s.L,) + cut + w.shape[2:]) for w in rest)


BACK_FIRST, BACK_SECOND, BACK_LAST = 2, 4, 6
SLOTS = 8
OUT_RING = 4
UPS_IN_LOOP = 2
X_EARLY, X_LATE, X_DOWN, X_MIX = 0, 1, 2, 3

def backward_scratch(s):
    dma = pltpu.SemaphoreType.DMA
    half = s.PR // 2
    return dict(
        part=pltpu.VMEM((SLOTS, s.NY, s.NX, s.Z, s.PR, s.PC), BF),
        land_x1=pltpu.VMEM((SLOTS, s.NX - 1, s.NY, s.Z, half, s.PC), BF),
        land_y1=pltpu.VMEM((SLOTS, s.NY - 1, s.NX, s.Z, half, s.PC), BF),
        land_x2=pltpu.VMEM((SLOTS, s.NX - 1, s.Z, half, s.PC), BF),
        land_y2=pltpu.VMEM((SLOTS, s.NY - 1, s.Z, half, s.PC), BF),
        land_z=pltpu.VMEM((SLOTS, s.Z - 1, s.PR, s.PC), BF),
        final=pltpu.VMEM((OUT_RING, s.PR, s.PC), F32),
        resid=pltpu.VMEM((s.T, s.D), F32),
        gb=pltpu.VMEM((s.T, s.D), BF),
        turned=pltpu.VMEM((s.NY, s.NX, 2, s.PR, s.T), BF),
        xt=pltpu.VMEM((4, 2, s.NY, s.NX, s.PR, s.T), BF),
        b_act=pltpu.VMEM((2, s.T, s.D), BF),
        b_slope=pltpu.VMEM((s.T, s.D), BF),
        ug=pltpu.VMEM((s.NJ, s.T, s.D), BF),
        ug_sib=pltpu.VMEM((s.NJ, s.T, s.D), BF),
        pg=pltpu.VMEM((3, s.T, s.D), BF),
        pg_sib=pltpu.VMEM((3, s.T, s.D), BF),
        b_mixed=pltpu.VMEM((2, s.T, s.D), BF),
        rg=pltpu.VMEM((s.T, s.D), BF),
        ng=pltpu.VMEM((s.T, s.D), BF),
        dg=pltpu.VMEM((s.T, s.D), F32),
        state=pltpu.VMEM((s.Z, s.MR, 128), BF),
        vec=pltpu.VMEM((16, s.D), F32),
        v_z=pltpu.VMEM((s.Z, 16, s.D), F32),
        v_c=pltpu.VMEM((2, 16, s.D), F32),
        v_x=pltpu.VMEM((s.NX, 16, s.D), F32),
        v_y=pltpu.VMEM((s.NY, 16, s.D), F32),
        x1_send=dma((SLOTS, s.NX - 1)),
        x1_recv=dma((SLOTS, s.NX - 1)),
        y1_send=dma((SLOTS, s.NY - 1)),
        y1_recv=dma((SLOTS, s.NY - 1)),
        x2_send=dma((SLOTS, s.NX - 1)),
        x2_recv=dma((SLOTS, s.NX - 1)),
        y2_send=dma((SLOTS, s.NY - 1)),
        y2_recv=dma((SLOTS, s.NY - 1)),
        bz_send=dma((SLOTS, s.Z - 1)),
        bz_recv=dma((SLOTS, s.Z - 1)),
        out_sem=dma((OUT_RING,)),
        xt_sem=dma((2, 2, s.NQ)),
        xt_send=dma((2, s.NQ)),
        xt_recv=dma((s.L, 2, s.NQ)),
        g_send=dma((s.NJ + 3,)),
        g_recv=dma((s.L, s.NJ + 3)),
        get=dma((8,)),
        v_send=dma((4, max(s.Z, s.NX, s.NY))),
        v_recv=dma((4, max(s.Z, s.NX, s.NY))),
    )


def down_at(s, j):
    return j + jnp.maximum(j - (s.NJ - UPS_IN_LOOP), 0) if not isinstance(j, int) else j + max(j - (s.NJ - UPS_IN_LOOP), 0)


def up_at(s, j):
    return s.NJ + j if j >= UPS_IN_LOOP else down_at(s, s.NJ - UPS_IN_LOOP + j) + 1


def gradient_sums(s, h, r, z, y, x, c):
    half = s.PR // 2
    rows = (pl.ds(0, half), pl.ds(half, half))
    part = h.part

    def to_x(d):
        return (row_at(s, y, (x + d) % s.NX, c), z)

    def to_y(d):
        return (row_at(s, (y + d) % s.NY, x, c), z)

    def first(v):
        b = v % SLOTS
        return [
            remote(part.at[b, :, d, :, rows[0]], h.land_x1.at[b, s.NX - d - 1], h.x1_send.at[b, d - 1],
                   h.x1_recv.at[b, s.NX - d - 1], to_x(d)) for d in range(1, s.NX)
        ] + [
            remote(part.at[b, d, :, :, rows[1]], h.land_y1.at[b, s.NY - d - 1], h.y1_send.at[b, d - 1],
                   h.y1_recv.at[b, s.NY - d - 1], to_y(d)) for d in range(1, s.NY)
        ]

    def second(v):
        b = v % SLOTS
        return [
            remote(part.at[b, d, 0, :, rows[0]], h.land_y2.at[b, s.NY - d - 1], h.y2_send.at[b, d - 1],
                   h.y2_recv.at[b, s.NY - d - 1], to_y(d)) for d in range(1, s.NY)
        ] + [
            remote(part.at[b, 0, d, :, rows[1]], h.land_x2.at[b, s.NX - d - 1], h.x2_send.at[b, d - 1],
                   h.x2_recv.at[b, s.NX - d - 1], to_x(d)) for d in range(1, s.NX)
        ]

    def last(v):
        b = v % SLOTS
        return [
            remote(part.at[b, 0, 0, d], h.land_z.at[b, s.Z - d - 1], h.bz_send.at[b, d - 1],
                   h.bz_recv.at[b, s.Z - d - 1], (r, (z + d) % s.Z)) for d in range(1, s.Z)
        ]

    def stage_second(v):
        b = v % SLOTS
        for cp in first(v):
            cp.wait_recv()

        def add(k, carry):
            for dy in range(s.NY):
                total = part[b, dy, 0, k, :half].astype(F32)
                for i in range(s.NX - 1):
                    total = total + h.land_x1[b, i, dy, k].astype(F32)
                part[b, dy, 0, k, :half] = total.astype(BF)
            for dx in range(s.NX):
                total = part[b, 0, dx, k, half:].astype(F32)
                for i in range(s.NY - 1):
                    total = total + h.land_y1[b, i, dx, k].astype(F32)
                part[b, 0, dx, k, half:] = total.astype(BF)
            return carry

        lax.fori_loop(0, s.Z, add, 0)
        for cp in second(v):
            cp.start()

    def stage_last(v):
        b = v % SLOTS
        for cp in second(v):
            cp.wait_recv()

        def add(k, carry):
            total = part[b, 0, 0, k, :half].astype(F32)
            for i in range(s.NY - 1):
                total = total + h.land_y2[b, i, k].astype(F32)
            part[b, 0, 0, k, :half] = total.astype(BF)
            total = part[b, 0, 0, k, half:].astype(F32)
            for i in range(s.NX - 1):
                total = total + h.land_x2[b, i, k].astype(F32)
            part[b, 0, 0, k, half:] = total.astype(BF)
            return carry

        lax.fori_loop(0, s.Z, add, 0)
        for cp in last(v):
            cp.start()

    def out_copy(at, o):
        return pltpu.make_async_copy(h.final.at[o], at, h.out_sem.at[o])

    def stage_out(v):
        b, o = v % SLOTS, v % OUT_RING
        for cp in last(v):
            cp.wait_recv()

        @pl.when(v >= OUT_RING)
        def _():
            out_copy(h.g_mix.at[0], o).wait()

        total = part[b, 0, 0, 0].astype(F32)
        for i in range(s.Z - 1):
            total = total + h.land_z[b, i].astype(F32)
        h.final[o] = total
        l, q = s.L - 1 - v // s.NU, v % s.NU
        wide = 2 * s.NJ
        for j in range(s.NJ):
            pl.when(q == down_at(s, j))(functools.partial(lambda to: out_copy(to, o).start(), h.g_down.at[l, :, lanes(j, s.PC)]))
            pl.when(q == up_at(s, j))(functools.partial(lambda to: out_copy(to, o).start(), h.g_up.at[l, :, lanes(j, s.PC)]))
        pl.when(q == wide)(lambda: out_copy(h.g_mix.at[l], o).start())
        pl.when(q > wide)(lambda: out_copy(h.g_in.at[l, q - wide - 1], o).start())

    def inside(v, what):
        pl.when((v >= 0) & (v < s.U))(functools.partial(what, v))

    def wait_sends(v):
        for cp in first(v) + second(v) + last(v):
            cp.wait_send()

    def tick(t):
        def start(v):
            for cp in first(v):
                cp.start()

        inside(t - BACK_LAST, stage_out)
        inside(t - BACK_SECOND, stage_last)
        inside(t - BACK_FIRST, stage_second)
        inside(t, start)

    def produce(v, which, own, sibling):
        b = v % SLOTS
        inside(v - SLOTS, wait_sends)
        left = [h.xt[which, i].reshape(s.NQ * s.PR, s.T) for i in range(2)]

        def block(k, carry):
            at = lanes(k, s.PC)
            total = dot(left[0], own[:, at]) + dot(left[1], sibling[:, at])
            part[b, :, :, k] = total.astype(BF).reshape(s.NY, s.NX, s.PR, s.PC)
            return carry

        lax.fori_loop(0, s.Z, block, 0)
        tick(v)

    def drain():
        @pl.loop(s.U + 4, s.U + max(BACK_LAST, 4))
        def _(t):
            tick(t)

    def settle():
        @pl.loop(s.U - SLOTS, s.U)
        def _(v):
            wait_sends(v)

        for o in range(OUT_RING):
            out_copy(h.g_mix.at[0], o).wait()

    return produce, tick, drain, settle


def backward_part(s, h, spots, tick_weights, with_unit, sums):
    r, z, y, x, c = spots
    produce, tick, drain, settle_sums = sums
    sibling = (row_at(s, y, x, 1 - c), z)
    first, _, _ = head_masks(s)
    ones = pair_ones()
    tall = jnp.ones((s.T, 128), BF)
    squares = [(dy, dx) for dy in range(s.NY) for dx in range(s.NX)]

    def get(src, dst, index):
        return pltpu.make_async_copy(src, dst, h.get.at[index])

    def xt_loads(l):
        return [
            pltpu.make_async_copy(h.k_normt.at[l, n, i, (y + dy) % s.NY, (x + dx) % s.NX], h.xt.at[n, i, dy, dx],
                                  h.xt_sem.at[n, i, q])
            for n in range(2) for i in range(2) for q, (dy, dx) in enumerate(squares)
        ]

    def xt_sends(l, which):
        return [
            remote(h.turned.at[(y + dy) % s.NY, (x + dx) % s.NX, 1 - c], h.xt.at[which, 1, dy, dx],
                   h.xt_send.at[which - 2, q], h.xt_recv.at[l, which - 2, q], sibling)
            for q, (dy, dx) in enumerate(squares)
        ]

    def turn(l, which):
        wide = h.grad[...]
        h.gb[...] = wide.astype(BF)
        h.turned[...] = wide.T.astype(BF).reshape(s.NY, s.NX, 2, s.PR, s.T)
        for cp in xt_sends(l, which):
            cp.start()
        for dy, dx in squares:
            h.xt[which, 0, dy, dx] = h.turned[(y + dy) % s.NY, (x + dx) % s.NX, c]
    def g_send(l, src, dst, j, index):
        return remote(src.at[j], dst.at[j], h.g_send.at[index], h.g_recv.at[l, index], sibling)

    def norm_back(l, n):
        back = h.acc[...]
        xhat, inv = norm_parts(h.resid[...])
        at = l * 2 + n
        h.vec[pl.ds(at, 1)] = jnp.sum(back * xhat, axis=0, keepdims=True)
        h.vec[pl.ds(2 * s.L + at, 1)] = jnp.sum(back, axis=0, keepdims=True)
        scaled = back * h.gain[pl.ds(l * 2 + n, 1), :]
        mean = jnp.mean(scaled, axis=-1, keepdims=True)
        along = jnp.mean(scaled * xhat, axis=-1, keepdims=True)
        h.grad[...] += inv * (scaled - mean - xhat * along)

    def early():
        h.grad[...] = h.cotangent[...].astype(F32)
        turn(s.L - 1, X_DOWN)

    def one_layer(li, carry):
        l = s.L - 1 - li
        base = li * s.NU
        unit = l * s.NU
        loads = [
            get(h.k_qkv.at[l], h.qkv, 0),
            get(h.k_mixed.at[l], h.b_mixed.at[0], 1),
            get(h.s_mixed.at[l], h.b_mixed.at[1], 2),
            get(h.k_den.at[l], h.den, 3),
            get(h.k_state.at[l], h.state, 4),
        ]
        act_loads = lambda j: [get(h.k_act.at[l, j], h.b_act.at[0], 5), get(h.s_act.at[l, j], h.b_act.at[1], 6)]
        slope_load = lambda j: get(h.k_slope.at[l, j], h.b_slope, 7)
        for cp in act_loads(0) + [slope_load(0)] + loads + xt_loads(l):
            cp.start()
        h.acc[...] = jnp.zeros_like(h.acc)
        for cp in xt_loads(l):
            cp.wait()
        for cp in xt_sends(l, X_DOWN):
            cp.wait_recv()

        def produce_up(j):
            g_send(l, h.ug, h.ug_sib, j, j).wait_recv()
            produce(base + up_at(s, j), X_LATE, h.ug.at[j], h.ug_sib.at[j])

        def feed_back(j, carry):
            for cp in act_loads(j):
                cp.wait()
            produce(base + down_at(s, j), X_DOWN, h.b_act.at[0], h.b_act.at[1])
            slope_load(j).wait()

            def body(k, weight):
                at = lanes(k, s.PC)
                h.ug[j, :, at] = (dot(h.gb[...], weight) * h.b_slope[:, at].astype(F32)).astype(BF)

                @pl.when(li == 0)
                def _():
                    h.stream[...] += dot(h.b_act[0, :, at], weight, NT)

            u = unit + 4 + s.NJ + j
            with_unit(h.w_down, l, j, u, body, lambda: pl.when((li == 0) & (j < 2))(lambda: tick_weights(u + s.NJ - 2 + LAG_READY)))

            @pl.when(j + 1 < s.NJ)
            def _():
                for cp in act_loads(j + 1):
                    cp.start()


            @pl.when(j + 1 < s.NJ)
            def _():
                slope_load(j + 1).start()

            g_send(l, h.ug, h.ug_sib, j, j).start()
            for i in range(UPS_IN_LOOP):
                pl.when(j == s.NJ - UPS_IN_LOOP + i)(functools.partial(produce_up, i))

            def body_up(k, weight):
                h.acc[...] += dot(h.ug[j, :, lanes(k, s.PC)], weight, NT)

            with_unit(h.w_up, l, j, unit + 4 + j, body_up)
            return carry

        lax.fori_loop(0, s.NJ, feed_back, 0)
        middle = get(h.k_middle.at[l], h.resid, 5)
        middle.start()
        for cp in xt_sends(l, X_DOWN):
            cp.wait_send()
        middle.wait()
        norm_back(l, 1)
        turn(l, X_MIX)
        for cp in xt_sends(l, X_MIX):
            cp.wait_recv()
        stream = get(h.k_stream.at[l], h.resid, 5)
        stream.start()

        def body_mix(k, weight):
            h.rg[:, lanes(k, s.PC)] = dot(h.gb[...], weight).astype(BF)

        with_unit(h.w_mix, l, 0, unit + 3, body_mix)
        for cp in loads:
            cp.wait()
        round_one, round_two, round_three, arrive, settle = prefix_rounds(s, h, l, r, z, 1)

        def local_state(k, carry):
            totals = []
            for i in range(s.NP):
                at = lanes(k * s.NP + i, 128)
                query, wide = h.qkv[0, :, at], h.rg[:, at].astype(F32)
                den = h.den[:, at]
                num = (wide / den).astype(BF)
                product = wide * h.b_mixed[0, :, at].astype(F32)
                high = product.astype(BF)
                low = (product - high.astype(F32)).astype(BF)
                slope = -(dot(high, ones) + dot(low, ones)) / den
                h.ng[:, at] = num
                h.dg[:, at] = slope
                h.msg[k, i * HD:(i + 1) * HD] = pack_state(dot(query, num, TN), first).astype(BF)
                totals.append(jnp.sum(query.astype(F32) * slope, axis=0, keepdims=True))
            h.msg[k, s.NP * HD:] = spread_rows(s, totals).astype(BF)
            return carry

        lax.fori_loop(0, s.Z, local_state, 0)
        round_one()
        causal = (lax.broadcasted_iota(jnp.int32, (s.T, s.T), 1) <= lax.broadcasted_iota(jnp.int32, (s.T, s.T), 0))
        lane = lax.broadcasted_iota(jnp.int32, (1, 128), 1)

        def attend_back(p, carry):
            k, i = p // s.NP, p % s.NP
            at = lanes(p, 128)
            query, key, value, num = h.qkv[0, :, at], h.qkv[1, :, at], h.qkv[2, :, at], h.ng[:, at]
            slope = h.dg[:, at]
            high = slope.astype(BF)
            low = (slope - high.astype(F32)).astype(BF)
            zero = jnp.zeros_like(query)
            value_ones = jnp.concatenate([value, tall], axis=1)
            rows = pl.ds(pl.multiple_of(i * HD, HD), HD)
            state = unpack_state(h.state[k, rows, :], first)
            total = pick_row(h.state[k, s.NP * HD:, :], i)
            query_grad = dot(num, state, NT) + slope * total
            value_grad = key_grad = jnp.zeros_like(query_grad)
            for head in range(2):
                mine = first if head == 0 else jnp.logical_not(first)
                query_mine = jnp.where(mine, query, zero)
                num_mine = jnp.where(mine, num, zero)
                key_mine = jnp.where(mine, key, zero)
                weights = jnp.where(causal, dot(query_mine, key, NT), 0.0).astype(BF)
                extra = jnp.where(lane == head * HD, high, jnp.where(lane == head * HD + 1, low, zero))
                score = dot(jnp.concatenate([num_mine, extra], axis=1), value_ones, NT)
                score = jnp.where(causal, score, 0.0).astype(BF)
                value_grad = value_grad + dot(weights, num_mine, TN)
                query_grad = query_grad + dot(score, key_mine)
                key_grad = key_grad + dot(score, query_mine, TN)
            h.pg[0, :, at] = (query_grad * jnp.minimum(query.astype(F32), 1.0)).astype(BF)
            h.dg[:, at] = key_grad
            h.acc[:, at] = value_grad
            return carry

        def look_ahead(p, carry):
            k, i = p // s.NP, p % s.NP
            at = lanes(p, 128)
            key, value = h.qkv[1, :, at], h.qkv[2, :, at]
            after = unpack_state(h.r3[k, pl.ds(pl.multiple_of(i * HD, HD), HD), :], first)
            total_after = pick_row(h.r3[k, s.NP * HD:, :], i)
            key_grad = h.dg[:, at] + dot(value, after, NT) + total_after
            h.pg[1, :, at] = (key_grad * jnp.minimum(key.astype(F32), 1.0)).astype(BF)
            h.pg[2, :, at] = (h.acc[:, at] + dot(key, after)).astype(BF)
            return carry

        pairs = s.Z * s.NP
        cut = [pairs * i // 4 for i in range(5)]
        lax.fori_loop(cut[0], cut[1], attend_back, 0)
        produce_up(2)
        round_two()
        lax.fori_loop(cut[1], cut[2], attend_back, 0)
        produce_up(3)
        round_three()
        lax.fori_loop(cut[2], cut[3], attend_back, 0)
        lax.fori_loop(cut[3], cut[4], attend_back, 0)
        produce(base + 2 * s.NJ, X_MIX, h.b_mixed.at[0], h.b_mixed.at[1])
        arrive()
        lax.fori_loop(0, pairs, look_ahead, 0)
        settle()
        for kind in range(3):
            g_send(l, h.pg, h.pg_sib, kind, s.NJ + kind).start()
        h.acc[...] = jnp.zeros_like(h.acc)

        def project_back(kind, carry):
            def body(k, weight):
                h.acc[...] += dot(h.pg[kind, :, lanes(k, s.PC)], weight, NT)

            with_unit(h.w_in, l, kind, unit + kind, body)
            g_send(l, h.pg, h.pg_sib, kind, s.NJ + kind).wait_recv()
            produce(base + 2 * s.NJ + 1 + kind, X_EARLY, h.pg.at[kind], h.pg_sib.at[kind])
            return carry

        lax.fori_loop(0, 3, project_back, 0)
        stream.wait()
        norm_back(l, 0)
        for cp in xt_sends(l, X_MIX):
            cp.wait_send()
        for j in range(s.NJ):
            g_send(l, h.ug, h.ug_sib, j, j).wait_send()
        for kind in range(3):
            g_send(l, h.pg, h.pg_sib, kind, s.NJ + kind).wait_send()

        @pl.when(li + 1 < s.L)
        def _():
            turn(l - 1, X_DOWN)

        return carry

    def run():
        lax.fori_loop(0, s.L, one_layer, 0)
        finish()

    def finish():
        h.vec[4 * s.L:4 * s.L + 2, :128] = h.logs[0:2]
        source = h.vec[...]
        top = lax.broadcasted_iota(jnp.int32, (16, s.D), 0) == 4 * s.L + 1
        stages = (
            (h.v_z, s.Z, z, lambda d: (r, (z + d) % s.Z)),
            (h.v_c, 2, c, lambda d: sibling),
            (h.v_x, s.NX, x, lambda d: (row_at(s, y, (x + d) % s.NX, c), z)),
            (h.v_y, s.NY, y, lambda d: (row_at(s, (y + d) % s.NY, x, c), z)),
        )
        pending = []
        for i, (slots, count, me, peer) in enumerate(stages):
            slots[me] = source
            for d in range(1, count):
                at = slots.at[me]
                cp = remote(at, at, h.v_send.at[i, d], h.v_recv.at[i, count - d], peer(d))
                cp.start()
                pending.append(cp)
            tick(s.U + i)
            for d in range(1, count):
                at = slots.at[(me + d) % count]
                remote(at, at, h.v_send.at[i, d], h.v_recv.at[i, d], (r, z)).wait_recv()
            total, largest = slots[0], slots[0]
            for k in range(1, count):
                total = total + slots[k]
                largest = jnp.maximum(largest, slots[k])
            source = jnp.where(top, largest, total)
        h.vector[...] = source
        for cp in pending:
            cp.wait_send()
        drain()
        settle_sums()

    return early, run


def unit_reader(s, h):
    def own(kind, l, j):
        if kind is h.w_in:
            src = h.w_in.at[l, j]
        elif kind is h.w_mix:
            src = h.w_mix.at[l]
        else:
            src = kind.at[l, :, :, :, :, lanes(j, s.PC)]
        return pltpu.make_async_copy(src, h.w.at[0], h.w_sem.at[0])

    def load(u, k):
        return pltpu.make_async_copy(h.whole.at[u, k - 1], h.w.at[k], h.w_sem.at[k])

    def with_unit(kind, l, j, u, body, advance=lambda: None):
        own(kind, l, j).start()
        advance()
        for k in range(1, s.Z):
            load(u, k).start()
        own(kind, l, j).wait()
        body(0, h.w[0].reshape(s.D, s.PC))

        @pl.loop(1, s.Z)
        def _(k):
            load(u, k).wait()
            body(k, h.w[k].reshape(s.D, s.PC))

    return with_unit


def kernel(s, *refs):
    scratch = forward_scratch(s) | backward_scratch(s)
    names = Inputs._fields + Outputs._fields + tuple(scratch)
    h = types.SimpleNamespace(**dict(zip(names, refs, strict=True)))
    spots = r, z, y, x, c = place(s)
    pieces = [
        pltpu.make_async_copy(h.w_in.at[:, :, y, x, c], h.piece.at[:, 0:3], h.piece_sem.at[0]),
        pltpu.make_async_copy(h.w_mix.at[:, y, x, c], h.piece.at[:, 3], h.piece_sem.at[1]),
    ]
    for j in range(s.NJ):
        cols = pl.ds(j * s.PC, s.PC)
        pieces.append(pltpu.make_async_copy(h.w_up.at[:, y, x, c, :, cols], h.piece.at[:, 4 + j], h.piece_sem.at[2 + j]))
        pieces.append(pltpu.make_async_copy(h.w_down.at[:, y, x, c, :, cols], h.piece.at[:, 4 + s.NJ + j],
                                            h.piece_sem.at[2 + s.NJ + j]))
    for cp in pieces:
        cp.start()
    greet(s, r, z)
    pieces[0].wait()
    tick_weights, drain_weights = weight_gather(s, h, r, z, y, x, c)
    with_unit = unit_reader(s, h)
    sums = gradient_sums(s, h, r, z, y, x, c)
    early, backward = backward_part(s, h, spots, tick_weights, with_unit, sums)

    def before():
        for cp in pieces[1:]:
            cp.wait()
        h.vec[...] = jnp.zeros_like(h.vec)
        early()

    forward_part(s, h, spots, tick_weights, with_unit, before)
    backward()
    h.output[...] = h.stream[...].astype(BF)
    drain_weights()


def call(s, arrays):
    vmem = pl.BlockSpec(memory_space=pltpu.VMEM)
    smem = pl.BlockSpec(memory_space=pltpu.SMEM)
    hbm = pl.BlockSpec(memory_space=pl.ANY)
    shape = jax.ShapeDtypeStruct
    outs = Outputs(
        output=shape((s.T, s.D), BF),
        grad=shape((s.T, s.D), F32),
        vector=shape((16, s.D), F32),
        g_in=shape((s.L, 3, s.PR, s.PC), F32),
        g_mix=shape((s.L, s.PR, s.PC), F32),
        g_up=shape((s.L, s.PR, s.NJ * s.PC), F32),
        g_down=shape((s.L, s.PR, s.NJ * s.PC), F32),
        whole=shape((s.U, s.Z - 1, s.NY, s.NX, 2, s.PR, s.PC), BF),
        k_stream=shape((s.L, s.T, s.D), F32),
        k_middle=shape((s.L, s.T, s.D), F32),
        k_qkv=shape((s.L, 3, s.T, s.D), BF),
        k_mixed=shape((s.L, s.T, s.D), BF),
        k_den=shape((s.L, s.T, s.D), F32),
        k_state=shape((s.L, s.Z, s.MR, 128), BF),
        k_act=shape((s.L, s.NJ, s.T, s.D), BF),
        k_slope=shape((s.L, s.NJ, s.T, s.D), BF),
        k_normt=shape((s.L, 2, 2, s.NY, s.NX, s.PR, s.T), BF),
        s_mixed=shape((s.L, s.T, s.D), BF),
        s_act=shape((s.L, s.NJ, s.T, s.D), BF),
    )
    scratch = forward_scratch(s) | backward_scratch(s)
    out = pl.pallas_call(
        functools.partial(kernel, s),
        out_shape=list(outs),
        in_specs=[vmem] * 4 + [smem] * 3 + [hbm] * 4,
        out_specs=[vmem] * 3 + [hbm] * (len(outs) - 3),
        scratch_shapes=list(scratch.values()),
        compiler_params=pltpu.CompilerParams(
            collective_id=0, has_side_effects=True, vmem_limit_bytes=61 * 1024 * 1024),
    )(*arrays)
    return Outputs(*out)


def finish_kernel(s, count, *refs):
    sources, vector, results = refs[:count], refs[count], refs[count + 1:2 * count + 1]
    gain, bias, top, log_max, log_mean, sems = refs[2 * count + 1:2 * count + 7]
    held = refs[2 * count + 7:]
    loads = [pltpu.make_async_copy(src, mid, sems.at[0, i]) for i, (src, mid) in enumerate(zip(sources, held))]
    stores = [pltpu.make_async_copy(mid, dst, sems.at[1, i]) for i, (mid, dst) in enumerate(zip(held, results))]
    for cp in loads:
        cp.start()
    for load, store in zip(loads, stores):
        load.wait()
        store.start()
    for l in range(s.L):
        gain[l] = vector[2 * l:2 * l + 2]
        bias[l] = vector[2 * s.L + 2 * l:2 * s.L + 2 * l + 2]
    top[...] = vector[4 * s.L - 1:4 * s.L]
    logs = s.R * s.Z * s.T * s.D * s.L
    log_mean[...] = jnp.sum(vector[4 * s.L:4 * s.L + 1, :128], axis=1, keepdims=True) / logs
    log_max[...] = jnp.max(vector[4 * s.L + 1:4 * s.L + 2, :128], axis=1, keepdims=True)
    for cp in stores:
        cp.wait()


def finish(s, got):
    vmem = pl.BlockSpec(memory_space=pltpu.VMEM)
    hbm = pl.BlockSpec(memory_space=pl.ANY)
    shape = jax.ShapeDtypeStruct
    large = (got.output, got.grad, got.g_in, got.g_mix, got.g_up, got.g_down)
    return pl.pallas_call(
        functools.partial(finish_kernel, s, len(large)),
        out_shape=[shape(a.shape, a.dtype) for a in large] + [
            shape((s.L, 2, s.D), F32), shape((s.L, 2, s.D), F32), shape((1, s.D), F32), shape((1, 1), F32), shape((1, 1), F32)],
        in_specs=[hbm] * len(large) + [vmem],
        out_specs=[hbm] * len(large) + [vmem] * 5,
        scratch_shapes=[pltpu.SemaphoreType.DMA((2, len(large)))] + [pltpu.VMEM(a.shape, a.dtype) for a in large],
        compiler_params=pltpu.CompilerParams(vmem_limit_bytes=61 * 1024 * 1024),
    )(*large, got.vector)


def local(mesh, tokens, cotangent, image_length, image_start, norm_gain, norm_bias, weight_in, weight_mix, weight_up,
          weight_down):
    s = sizes_of(mesh, tokens, weight_in, weight_up)
    weights = split_rows(s, weight_in, weight_mix, weight_up, weight_down)
    *coefs, gain, bias = weigh_units(s, image_length, image_start, norm_gain, norm_bias)
    got = call(s, Inputs(tokens, cotangent, gain, bias, *coefs, *weights))
    output, grad, g_in, g_mix, g_up, g_down, grad_gain, grad_bias, top, log_max, log_mean = finish(s, got)
    return (output, grad, grad_gain, grad_bias, top.reshape(-1), jnp.transpose(g_in, (0, 2, 1, 3)), g_mix, g_up, g_down,
            log_max.reshape(()), log_mean.reshape(()))


def solution(mesh):
    pixels = P(("rows", "feat"), None)
    placed = (pixels, pixels, P(), P(), P(), P(), P(None, None, None, "feat"), P(None, None, "feat"), P(None, None, "feat"),
              P(None, None, "feat"))
    return jax.shard_map(
        functools.partial(local, mesh),
        mesh=mesh,
        in_specs=placed,
        out_specs=(pixels, pixels, P(), P(), P(), P(None, "rows", None, "feat"), P(None, "rows", "feat"),
                   P(None, "rows", "feat"), P(None, "rows", "feat"), P(), P()),
        check_vma=False,
    )
```
